32 devices in a mesh: dp: 8 (over y, x, core), expert: 4 (over z).
Axes of the slice: x: 2, y: 2, z: 4, core: 2. Of those that a mesh axis runs over, the one named last changes fastest.
Arguments:
- tokens: bfloat16 [2, 4, 1024, 2048], P(None, 'expert', 'dp'), may hold values from -6 to 6
- segment_ids: int32 [2, 4, 1024], P(None, 'expert'), may hold values from 0 to 2, as said below
- attn_routes: int32 [2, 4, 1024, 2], P(None, 'expert', 'dp'), may hold values from 0 to 3, all different within a row; in each aligned block of 128 rows (0 to 127, 128 to 255, ..., all dimensions but the last counted through in order) at most 64 rows name the same one
- mlp_routes: int32 [2, 4, 1024, 2], P(None, 'expert', 'dp'), may hold values from 0 to 3, all different within a row; in each aligned block of 128 rows (0 to 127, 128 to 255, ..., all dimensions but the last counted through in order) at most 64 rows name the same one
- cotangent: bfloat16 [2, 4, 1024, 2048], P(None, 'expert', 'dp'), may hold values from -6 to 6
- attn_gain: bfloat16 [2048], P(('dp', 'expert')), may hold values from 0.099609375 to 1.8984375
- kv_weights: bfloat16 [2048, 2, 2048], P(('dp', 'expert')), may hold values from -0.125 to 0.125
- attn_router: bfloat16 [2048, 4], P(('dp', 'expert')), may hold values from -0.09375 to 0.09375
- query_maps: bfloat16 [4, 2048, 2048], P('expert', 'dp'), may hold values from -0.125 to 0.125
- output_maps: bfloat16 [4, 2048, 2048], P('expert', 'dp'), may hold values from -0.5 to 0.5
- mlp_gain: bfloat16 [2048], P(('dp', 'expert')), may hold values from 0.099609375 to 1.8984375
- mlp_router: bfloat16 [2048, 4], P(('dp', 'expert')), may hold values from -0.09375 to 0.09375
- gate_up: bfloat16 [4, 5632, 2, 2048], P('expert', 'dp'), may hold values from -0.125 to 0.125
- down_maps: bfloat16 [4, 5632, 2048], P('expert', 'dp'), may hold values from -0.078125 to 0.078125
Outputs:
- mixed: bfloat16 [2, 4, 1024, 2048], P(None, 'expert', 'dp')
- input_grad: float32 [2, 4, 1024, 2048], P(None, 'expert', 'dp')
- attn_gain_grad: float32 [2048], P(('dp', 'expert'))
- kv_grad: float32 [2048, 2, 2048], P(('dp', 'expert'))
- attn_router_grad: float32 [2048, 4], P(('dp', 'expert'))
- query_grad: float32 [4, 2048, 2048], P('expert', 'dp')
- output_grad: float32 [4, 2048, 2048], P('expert', 'dp')
- mlp_gain_grad: float32 [2048], P(('dp', 'expert'))
- mlp_router_grad: float32 [2048, 4], P(('dp', 'expert'))
- gate_up_grad: float32 [4, 5632, 2, 2048], P('expert', 'dp')
- down_grad: float32 [4, 5632, 2048], P('expert', 'dp')
The draws below stay inside these ranges and needn't reach their ends.
Inputs may be any that keep to these rules, and one draw needn't show every extreme that they name: `attn_routes`: A token's two experts differ. Within the 1024 // 8 consecutive positions of one sequence that one device holds, every expert is named exactly 64 times. `mlp_routes`: A token's two experts differ. Within the 1024 // 8 consecutive positions of one sequence that one device holds, every expert is named exactly 64 times. `segment_ids`: each sequence holds three documents numbered 0, 1, 2 in order: 0 ends at a position from 32 to 64, 2 begins at a position from 960 to 992.
All inputs are finite; a program needn't handle non-finite values.
Results may differ from the reference program's by a relative error of at most 0.02.
Values may be sent and summed in bfloat16 or wider, within the bound.
No kernel may reach another device: no remote copies, remote signals or barrier semaphores. Data moves between devices by JAX's collectives and lax.ppermute only.
A program may use at most 640 MiB of HBM per device.

```python
import math
import jax
import jax.numpy as jnp
import numpy as np
from jax import lax

D = 2048
HEADS = 16
HEAD_WIDTH = 128
FF = 5632
EXPERTS = 4
LENGTH = 1024
SEQS = 4
MICRO = 2
CAP = 64
N_DP = 8


def draw_segment_ids(key, part):
    key = jax.random.fold_in(key, 11)
    first_key, last_key = jax.random.split(key)
    first_end = jax.random.randint(first_key, (MICRO, SEQS, 1), LENGTH // 32, LENGTH // 16 + 1)
    last_start = jax.random.randint(last_key, (MICRO, SEQS, 1), LENGTH - LENGTH // 16, LENGTH - LENGTH // 32 + 1)
    positions = jnp.arange(LENGTH, dtype=jnp.int32)[None, None, :]
    return (positions >= first_end).astype(jnp.int32) + (positions >= last_start).astype(jnp.int32)


def level_of(key, shape, pieces, smallest, high):
    factor_of = 1.0
    for axis_at, parts in pieces:
        heights = jax.random.uniform(jax.random.fold_in(jax.random.fold_in(key, 6), axis_at), (parts,), jnp.float32, smallest / len(pieces), high / len(pieces))
        factor_of = factor_of * jnp.repeat(jnp.exp(heights), shape[axis_at] // parts).reshape((-1,) + (1,) * (len(shape) - 1 - axis_at))
    return factor_of


def shared_out(own_key, own, number, rows, number_of, top, limit, skew):
    ranking = jax.random.permutation(own_key, number_of)
    packed, common = portions_of(number_of, rows * top, limit, skew, True), portions_of(number_of, rows * top, limit, skew, False)
    places = jnp.arange(number_of)

    def named(tallies, rotation):
        used = int((tallies > 0).sum())
        fixed = max(1, used // 4)
        shifted = fixed + (places - fixed + rotation * (used - fixed)) % max(1, number_of - fixed)
        return jnp.zeros((number_of,), jnp.int32).at[ranking[jnp.where(places < fixed, places, shifted)]].set(jnp.asarray(tallies, jnp.int32))

    tallies = jnp.where(number % 4 == 0, named(packed, number // 4), named(common, number - number // 4 - 1))
    mixed = jax.random.permutation(jax.random.fold_in(own, 3), number_of)
    giver, taker = mixed[0:number_of // 2 * 2:2], mixed[1:number_of // 2 * 2:2]
    margin = jnp.minimum(tallies[giver] - 1, limit - tallies[taker]) // 2
    margin = jnp.where((giver == ranking[0]) | (taker == ranking[0]) | (tallies[taker] == 0), 0, jnp.maximum(margin, 0))
    shifted = jax.random.randint(jax.random.fold_in(own, 4), (number_of // 2,), 0, 1 << 20) % (margin + 1)
    tallies = tallies.at[giver].add(-shifted).at[taker].add(shifted)
    items = jnp.searchsorted(jnp.cumsum(tallies), jnp.arange(rows * top), side="right").astype(jnp.int32)
    listing = items.reshape(top, rows).T
    listing = listing[jax.random.permutation(jax.random.fold_in(own, 1), rows)]
    rotation = jax.random.randint(jax.random.fold_in(own, 2), (rows, 1), 0, top)
    return jnp.take_along_axis(listing, (jnp.arange(top)[None, :] + rotation) % top, axis=1)


def portions_of(amount, total, limit, skew, full):
    portions = [(1 << 20) // math.isqrt(standing ** skew) + 1 for standing in range(1, amount + 1)]
    largest = limit if full else min(limit, max(-(-total // amount), total * portions[0] // sum(portions)))
    least = 1 if total - largest >= amount - 1 else 0
    holding, spare = [largest] + [least] * (amount - 1), total - largest - least * (amount - 1)
    while spare > 0:
        movable = [i for i in range(1, amount) if holding[i] < largest] or [i for i in range(1, amount) if holding[i] < limit]
        mass, budget = sum([portions[i] for i in movable]), spare
        for i in movable:
            extra = min(limit - holding[i], max(1, budget * portions[i] // mass), spare)
            holding[i] = holding[i] + extra
            spare = spare - extra
    return np.array(holding)


def bell_draw(key, shape, scale, most, pieces=(), kind=jnp.bfloat16):
    drawn = scale * jax.random.normal(key, shape, jnp.float32)
    if pieces:
        drawn = drawn * level_of(key, shape, pieces, -0.22, 0.18)
    return jnp.clip(drawn, -most, most).astype(kind)


def setup_inputs(seed: int = 0) -> dict:
    splits = jax.random.split(jax.random.key(seed), 15)
    tokens = bell_draw(splits[0], (MICRO, SEQS, LENGTH, D), 1.0, 6.0, ((1, 4), (2, 8)))
    segment_ids = draw_segment_ids(jax.random.fold_in(splits[14], 71), 0)
    attn_routes_keys = jax.random.split(jax.random.fold_in(splits[2], 1), MICRO * SEQS * LENGTH // (LENGTH // N_DP))
    attn_routes_turns = jax.random.permutation(jax.random.fold_in(splits[2], 3), MICRO * SEQS * LENGTH // (LENGTH // N_DP))
    attn_routes = jax.vmap(lambda own, number: shared_out(jax.random.fold_in(splits[2], 2), own, number, LENGTH // N_DP, EXPERTS, 2, CAP, 0))(attn_routes_keys, attn_routes_turns).reshape((MICRO, SEQS, LENGTH, 2))
    mlp_routes_keys = jax.random.split(jax.random.fold_in(splits[3], 1), MICRO * SEQS * LENGTH // (LENGTH // N_DP))
    mlp_routes_turns = jax.random.permutation(jax.random.fold_in(splits[3], 3), MICRO * SEQS * LENGTH // (LENGTH // N_DP))
    mlp_routes = jax.vmap(lambda own, number: shared_out(jax.random.fold_in(splits[3], 2), own, number, LENGTH // N_DP, EXPERTS, 2, CAP, 0))(mlp_routes_keys, mlp_routes_turns).reshape((MICRO, SEQS, LENGTH, 2))
    cotangent = bell_draw(splits[4], (MICRO, SEQS, LENGTH, D), 1.0, 6.0, ((1, 4), (2, 8)))
    attn_gain = jnp.clip(1.0 + 0.18 * jax.random.normal(splits[5], (D,), jnp.float32), 0.099609375, 1.8984375).astype(jnp.bfloat16)
    kv_weights = bell_draw(splits[6], (D, 2, D), D ** -0.5, 0.125, ((0, 32),))
    attn_router = bell_draw(splits[7], (D, EXPERTS), (2 * D) ** -0.5, 0.09375, ((0, 32),))
    query_maps = bell_draw(splits[8], (EXPERTS, D, D), D ** -0.5, 0.125, ((0, 4), (1, 8)))
    output_maps = bell_draw(splits[9], (EXPERTS, D, D), (D // 16) ** -0.5, 0.5, ((0, 4), (1, 8)))
    mlp_gain = jnp.clip(1.0 + 0.18 * jax.random.normal(splits[10], (D,), jnp.float32), 0.099609375, 1.8984375).astype(jnp.bfloat16)
    mlp_router = bell_draw(splits[11], (D, EXPERTS), (2 * D) ** -0.5, 0.09375, ((0, 32),))
    gate_up = bell_draw(splits[12], (EXPERTS, FF, 2, D), D ** -0.5, 0.125, ((0, 4), (1, 8)))
    down_maps = bell_draw(splits[13], (EXPERTS, FF, D), FF ** -0.5, 0.078125, ((0, 4), (1, 8)))
    return {"tokens": tokens, "segment_ids": segment_ids, "attn_routes": attn_routes, "mlp_routes": mlp_routes, "cotangent": cotangent, "attn_gain": attn_gain, "kv_weights": kv_weights, "attn_router": attn_router, "query_maps": query_maps, "output_maps": output_maps, "mlp_gain": mlp_gain, "mlp_router": mlp_router, "gate_up": gate_up, "down_maps": down_maps}


EPSILON = 1e-05
THETA_BASE = 10000.0
NEGATIVE = -1000000000.0
PRECISION_TOP = lax.Precision.HIGHEST

@jax.custom_vjp
def low(v):
    return lax.optimization_barrier(v.astype(jnp.bfloat16)).astype(jnp.float32)

@jax.custom_vjp
def low_back(v):
    return v

def low_keep(v):
    return (low(v), None)

def low_pass(kept, grad):
    return (grad,)

def back_keep(v):
    return (v, None)

def back_low(kept, grad):
    return (low(grad),)
low.defvjp(low_keep, low_pass)
low_back.defvjp(back_keep, back_low)

def rope_tables(positions, half_dim):
    frequency = THETA_BASE ** (-jnp.arange(half_dim, dtype=jnp.float32) / half_dim)
    angles = positions.astype(jnp.float32)[:, None] * frequency[None, :]
    return (jnp.cos(angles), jnp.sin(angles))

def rotate(values, cosine, sine_table):
    half_dim = values.shape[-1] // 2
    first_half = values[..., :half_dim]
    second_half = values[..., half_dim:]
    return jnp.concatenate([first_half * cosine - second_half * sine_table, second_half * cosine + first_half * sine_table], axis=-1)

def normalize(values, gain_row):
    inverse = lax.rsqrt(lax.optimization_barrier(jnp.mean(values * values, axis=-1, keepdims=True)) + EPSILON)
    return values * inverse * gain_row

def route_gates(logits, routes):
    chosen = jnp.take_along_axis(logits, routes, axis=1)
    return jax.nn.softmax(chosen, axis=-1)

def expert_apply(pair_rows, routes, compute):
    flat_routes = routes.reshape(-1)
    sort_order = jnp.argsort(flat_routes, stable=True).astype(jnp.int32)
    inverse = jnp.argsort(sort_order, stable=True).astype(jnp.int32)
    groups = pair_rows[sort_order].reshape(EXPERTS, -1, pair_rows.shape[-1])
    result = compute(groups)
    return result.reshape(sort_order.shape[0], -1)[inverse].reshape(routes.shape[0], 2, -1)

def attend(sequence):
    query_vectors, key_matrix_rows, value_matrix_rows, seg_row = sequence
    positions = jnp.arange(LENGTH, dtype=jnp.int32)
    key_mask = (positions[None, :] <= positions[:, None]) & (seg_row[None, :] == seg_row[:, None])
    score_matrix = jnp.einsum('exrt,jrt->xrej', query_vectors, key_matrix_rows, precision=PRECISION_TOP) * HEAD_WIDTH ** (-0.5)
    score_matrix = low_back(jnp.where(key_mask[None, None], score_matrix, NEGATIVE))
    attention_weights = low(jax.nn.softmax(score_matrix, axis=-1))
    return jnp.einsum('wfxs,sfa->xwfa', attention_weights, value_matrix_rows, precision=PRECISION_TOP)

def reference(tokens, segment_ids, attn_routes, mlp_routes, cotangent, attn_gain, kv_weights, attn_router, query_maps, output_maps, mlp_gain, mlp_router, gate_up, down_maps):
    inputs = tokens.reshape(-1, D).astype(jnp.float32)
    row_total = inputs.shape[0]
    seq_total = row_total // LENGTH
    seg_rows = segment_ids.reshape(seq_total, LENGTH)
    routes_attn = attn_routes.reshape(-1, 2)
    routes_mlp = mlp_routes.reshape(-1, 2)
    positions = jnp.tile(jnp.arange(LENGTH, dtype=jnp.int32), seq_total)
    cosine, sine_table = rope_tables(positions, HEAD_WIDTH // 2)

    def forward(inputs, gain_one, kv_full, router_one, query_full, output_full, gain_two, router_two, gate_full, down_full):
        normed_one = low(normalize(inputs, gain_one))
        gates_attn = route_gates(jnp.dot(normed_one, router_one, precision=PRECISION_TOP), routes_attn)
        kv_proj = low_back(jnp.dot(normed_one, kv_full.reshape(D, 2 * D), precision=PRECISION_TOP))
        key_matrix_rows = low(rotate(kv_proj[:, :D].reshape(row_total, HEADS, HEAD_WIDTH), cosine[:, None], sine_table[:, None]))
        value_matrix_rows = low(kv_proj[:, D:].reshape(row_total, HEADS, HEAD_WIDTH))
        query_raw = expert_apply(jnp.repeat(normed_one, 2, axis=0), routes_attn, lambda groups: low(low_back(jnp.einsum('emd,edf->emf', groups, query_full, precision=PRECISION_TOP))))
        query_vectors = low(rotate(query_raw.reshape(row_total, 2, HEADS, HEAD_WIDTH), cosine[:, None, None], sine_table[:, None, None]))
        context = lax.map(jax.checkpoint(attend), (query_vectors.reshape(seq_total, LENGTH, 2, HEADS, HEAD_WIDTH), key_matrix_rows.reshape(seq_total, LENGTH, HEADS, HEAD_WIDTH), value_matrix_rows.reshape(seq_total, LENGTH, HEADS, HEAD_WIDTH), seg_rows))
        context_low = low(low_back(context.reshape(row_total * 2, D)))
        attn_back = expert_apply(context_low, routes_attn, lambda groups: low(low_back(jnp.einsum('emd,edf->emf', groups, output_full, precision=PRECISION_TOP))))
        hidden_state = inputs + lax.optimization_barrier(jnp.sum(gates_attn[..., None] * attn_back, axis=1))
        normed_two = low(normalize(hidden_state, gain_two))
        gates_mlp = route_gates(jnp.dot(normed_two, router_two, precision=PRECISION_TOP), routes_mlp)

        def feed_forward(groups):
            projected = jnp.einsum('emd,efcd->emcf', groups, gate_full, precision=PRECISION_TOP)
            gate_val = low_back(projected[:, :, 0])
            up_val = low_back(projected[:, :, 1])
            hidden_rows = low(jax.nn.silu(gate_val) * up_val)
            return low(low_back(jnp.einsum('emf,efd->emd', hidden_rows, down_full, precision=PRECISION_TOP)))
        mlp_back = expert_apply(jnp.repeat(normed_two, 2, axis=0), routes_mlp, feed_forward)
        return hidden_state + lax.optimization_barrier(jnp.sum(gates_mlp[..., None] * mlp_back, axis=1))
    result, pullback = jax.vjp(forward, inputs, attn_gain.astype(jnp.float32), kv_weights.astype(jnp.float32), attn_router.astype(jnp.float32), query_maps.astype(jnp.float32), output_maps.astype(jnp.float32), mlp_gain.astype(jnp.float32), mlp_router.astype(jnp.float32), gate_up.astype(jnp.float32), down_maps.astype(jnp.float32))
    gradients = pullback(cotangent.reshape(-1, D).astype(jnp.float32))
    return (result.astype(jnp.bfloat16).reshape(tokens.shape), gradients[0].reshape(tokens.shape), gradients[1], gradients[2], gradients[3], gradients[4], gradients[5], gradients[6], gradients[7], gradients[8], gradients[9])
```

```python
import jax
import jax.numpy as jnp
from jax import lax
from jax.sharding import PartitionSpec as P

HEAD_WIDTH = 128


EPSILON = 1e-05
THETA_BASE = 10000.0
NEGATIVE = -1000000000.0
PRECISION_TOP = lax.Precision.HIGHEST
BF16 = jnp.bfloat16
F32 = jnp.float32


def rope_tables(positions, half_dim):
    frequency = THETA_BASE ** (-jnp.arange(half_dim, dtype=F32) / half_dim)
    angles = positions.astype(F32)[:, None] * frequency[None, :]
    return (jnp.cos(angles), jnp.sin(angles))


def rotate(values, cosine, sine_table):
    half_dim = values.shape[-1] // 2
    first_half = values[..., :half_dim]
    second_half = values[..., half_dim:]
    return jnp.concatenate(
        [
            first_half * cosine - second_half * sine_table,
            second_half * cosine + first_half * sine_table,
        ],
        axis=-1,
    )


def rotate_back(gradients, cosine, sine_table):
    return rotate(gradients, cosine, -sine_table)


def norm_forward(values, gain_row):
    inverse = lax.rsqrt(jnp.mean(values * values, axis=-1, keepdims=True) + EPSILON)
    return (values * inverse * gain_row, inverse)


def norm_backward(values, inverse, gain_row, grad_normed):
    scaled = gain_row * grad_normed
    gain_term = jnp.sum(grad_normed * values * inverse, axis=0)
    grad_values = inverse * scaled - values * inverse**3 * jnp.mean(
        scaled * values, axis=-1, keepdims=True
    )
    return (grad_values, gain_term)


def route_onehot(routes, experts):
    return (routes[..., None] == jnp.arange(experts, dtype=jnp.int32)).astype(F32)


def gate_forward(logits, onehot):
    chosen = jnp.sum(logits[:, None, :] * onehot, axis=-1)
    return jax.nn.softmax(chosen, axis=-1)


def gate_backward(gate_probs, grad_gates, onehot):
    centered = gate_probs * (grad_gates - jnp.sum(gate_probs * grad_gates, axis=-1, keepdims=True))
    return jnp.sum(centered[..., None] * onehot, axis=1)


def slot_columns(routes, experts, capacity):
    flat_routes = routes.reshape(-1)
    onehot = (flat_routes[:, None] == jnp.arange(experts, dtype=jnp.int32)[None, :]).astype(
        jnp.int32
    )
    slot_rank = jnp.sum((jnp.cumsum(onehot, axis=0) - 1) * onehot, axis=1)
    return (flat_routes * capacity + slot_rank).reshape(routes.shape)


def dot_f32(left, right):
    return jnp.dot(left, right, preferred_element_type=F32)


def to_planes(slots, experts):
    return lax.all_to_all(
        slots.reshape(experts, -1, slots.shape[-1]), "expert", split_axis=0, concat_axis=0, tiled=True
    ).reshape(slots.shape)


def per_device(
    tokens,
    segment_ids,
    attn_routes,
    mlp_routes,
    cotangent,
    attn_gain,
    kv_weights,
    attn_router,
    query_maps,
    output_maps,
    mlp_gain,
    mlp_router,
    gate_up,
    down_maps,
):
    micro_count, seq_count, local_len, width = tokens.shape
    units = micro_count * seq_count
    length = segment_ids.shape[2]
    experts = attn_router.shape[1]
    dp = lax.axis_size("dp")
    planes = lax.axis_size("expert")
    capacity = 2 * local_len // experts
    slots = experts * capacity
    both = ("dp", "expert")
    head_cols = width // dp
    heads = head_cols // HEAD_WIDTH
    scale = HEAD_WIDTH ** (-0.5)
    my_expert = lax.axis_index("expert")
    my_dp = lax.axis_index("dp")

    tokens = tokens.reshape(units, local_len, width)
    cotangent = cotangent.reshape(units, local_len, width)
    segments = segment_ids.reshape(units, length)
    attn_routes = attn_routes.reshape(units, local_len, 2)
    mlp_routes = mlp_routes.reshape(units, local_len, 2)

    columns = [slot_columns(mlp_routes[u], experts, capacity) for u in range(units)]
    slot_ids = jnp.arange(slots, dtype=jnp.int32)
    tables = []
    others = []
    for u in range(units):
        hits = (columns[u][None] == slot_ids[:, None, None]).astype(F32)
        tables.append(hits)
        others.append(jnp.sum(hits * mlp_routes[u][None, :, ::-1].astype(F32), axis=(1, 2)))
    small = jnp.concatenate(
        [
            attn_gain.astype(F32),
            mlp_gain.astype(F32),
            attn_router.astype(F32).reshape(-1),
            mlp_router.astype(F32).reshape(-1),
            attn_routes.astype(F32).reshape(-1),
        ]
        + others
    )
    small_all = lax.all_gather(small, both, axis=0)
    rows_each = attn_gain.shape[0]
    at = 0
    gain_one = small_all[:, at : at + rows_each].reshape(width)
    at += rows_each
    gain_two = small_all[:, at : at + rows_each].reshape(width)
    at += rows_each
    router_one = small_all[:, at : at + rows_each * experts].reshape(width, experts)
    at += rows_each * experts
    router_two = small_all[:, at : at + rows_each * experts].reshape(width, experts)
    at += rows_each * experts
    routes_count = units * local_len * 2
    grid = small_all[:, at:].reshape(dp, planes, -1)
    mine = lax.dynamic_index_in_dim(grid, my_expert, axis=1, keepdims=False)
    routes_all = (
        mine[:, :routes_count]
        .reshape(dp, units, local_len, 2)
        .transpose(1, 0, 2, 3)
        .reshape(units, length, 2)
        .astype(jnp.int32)
    )
    other_grid = grid[:, :, routes_count:].reshape(dp, planes, units, experts, capacity)
    other_rows = lax.dynamic_index_in_dim(other_grid, my_expert, axis=3, keepdims=False)
    other_rows = other_rows.transpose(2, 0, 1, 3).reshape(units, dp * slots).astype(jnp.int32)
    router_one_low = router_one.astype(BF16)
    router_two_low = router_two.astype(BF16)

    kv_rows = kv_weights.shape[0]
    packed = jnp.concatenate([query_maps[0], kv_weights.reshape(kv_rows * 2, width)], axis=0)
    packed = lax.all_to_all(
        packed.reshape(-1, dp, head_cols).transpose(1, 0, 2), "dp", split_axis=0, concat_axis=0, tiled=True
    )
    packed = lax.all_gather(packed, "expert", axis=0)
    query_rows = query_maps.shape[1]
    query_cols = packed[:, :, :query_rows].reshape(experts, width, head_cols)
    kv_cols = (
        packed[:, :, query_rows:]
        .reshape(planes, dp, kv_rows, 2, head_cols)
        .transpose(1, 0, 2, 3, 4)
        .reshape(width, 2 * head_cols)
    )
    qkv_cols = jnp.concatenate(
        [query_cols.transpose(1, 0, 2).reshape(width, experts * head_cols), kv_cols], axis=1
    )
    output_rows = lax.all_gather(output_maps[0], "expert", axis=0, tiled=True)

    positions = jnp.arange(length, dtype=jnp.int32)
    cosine, sine_table = rope_tables(positions, HEAD_WIDTH // 2)

    gate_up_local = gate_up[0]
    down_local = down_maps[0]

    mixed_parts = []
    input_parts = []
    a_list, g_list, ctx_list, dh_list = [], [], [], []
    b_rows_list, dgate_list, dup_list, hid_list, cot_rows_list = [], [], [], [], []
    a_home_list, dla_list, b_home_list, dlm_list = [], [], [], []
    gain_one_sum = jnp.zeros((width,), F32)
    gain_two_sum = jnp.zeros((width,), F32)
    for u in range(units):
        table = jnp.sum(tables[u], axis=2).astype(BF16)
        hits = tables[u]
        inputs = tokens[u].astype(F32)
        normed_one, inverse_one = norm_forward(inputs, gain_one)
        a_home = normed_one.astype(BF16)
        a_all = lax.all_gather(a_home, "dp", axis=0, tiled=True)

        cot = cotangent[u]
        cot_rows = lax.all_gather(
            to_planes(dot_f32(table, cot).astype(BF16), experts), "dp", axis=0, tiled=True
        )
        cot_hidden = jnp.einsum("rd,fd->rf", cot_rows, down_local, preferred_element_type=F32)

        onehot_all = route_onehot(routes_all[u], experts)
        gates_all = gate_forward(dot_f32(a_all, router_one_low), onehot_all)
        qkv = dot_f32(a_all, qkv_cols)
        query_dense = qkv[:, : experts * head_cols].astype(BF16).astype(F32)
        query_dense = query_dense.reshape(length, 1, experts, head_cols)
        query_raw = jnp.sum(query_dense * onehot_all[..., None], axis=2)
        query_vectors = rotate(
            query_raw.reshape(length, 2, heads, HEAD_WIDTH),
            cosine[:, None, None],
            sine_table[:, None, None],
        ).astype(BF16)
        keys = rotate(
            qkv[:, experts * head_cols : (experts + 1) * head_cols].reshape(
                length, heads, HEAD_WIDTH
            ),
            cosine[:, None],
            sine_table[:, None],
        ).astype(BF16)
        values = qkv[:, (experts + 1) * head_cols :].astype(BF16).reshape(length, heads, HEAD_WIDTH)
        mask = (positions[None, :] <= positions[:, None]) & (
            segments[u][:, None] == segments[u][None, :]
        )

        def score_of(query_vectors, keys, mask):
            score = jnp.einsum("lkhd,mhd->khlm", query_vectors, keys, preferred_element_type=F32)
            return jnp.where(mask[None, None], score * scale, NEGATIVE)

        score = score_of(query_vectors, keys, mask)
        row_top = jnp.max(score, axis=-1, keepdims=True)
        exponent = jnp.exp(score - row_top)
        row_total = jnp.sum(exponent, axis=-1, keepdims=True)
        log_total = row_top + jnp.log(row_total)
        probs = (exponent / row_total).astype(BF16)
        context = (
            jnp.einsum("khlm,mhd->lkhd", probs, values, preferred_element_type=F32)
            .astype(BF16)
            .reshape(length, 2, head_cols)
        )
        gated_onehot = gates_all[..., None] * onehot_all
        context_gated = (
            jnp.sum(context.astype(F32)[:, :, None, :] * gated_onehot[..., None], axis=1)
            .astype(BF16)
            .reshape(length, experts * head_cols)
        )
        attn_sum = lax.psum_scatter(
            dot_f32(context_gated, output_rows).astype(BF16), "dp", scatter_dimension=0, tiled=True
        )
        hidden_state = inputs + attn_sum.astype(F32)

        normed_two, inverse_two = norm_forward(hidden_state, gain_two)
        b_home = normed_two.astype(BF16)
        onehot_mlp = route_onehot(mlp_routes[u], experts)
        gates_mlp = gate_forward(dot_f32(b_home, router_two_low), onehot_mlp)
        b_rows = lax.all_gather(
            to_planes(dot_f32(table, b_home).astype(BF16), experts), "dp", axis=0, tiled=True
        )
        logits_rows = dot_f32(b_rows, router_two_low)
        own_logit = jnp.sum(
            jnp.where(jnp.arange(experts)[None] == my_expert, logits_rows, 0.0), axis=1
        )
        other_logit = jnp.sum(
            jnp.where(jnp.arange(experts)[None] == other_rows[u][:, None], logits_rows, 0.0), axis=1
        )
        gate_rows = jax.nn.sigmoid(own_logit - other_logit)[:, None]
        gate_up_rows = jnp.einsum("rd,fcd->rcf", b_rows, gate_up_local, preferred_element_type=F32)
        gate_val = gate_up_rows[:, 0]
        up_val = gate_up_rows[:, 1]
        sigmoid = jax.nn.sigmoid(gate_val)
        silu = gate_val * sigmoid
        hidden = silu * up_val
        hidden_low = hidden.astype(BF16)
        hidden_gated = (hidden * gate_rows).astype(BF16)
        grad_hidden = cot_hidden * gate_rows
        grad_gate = (grad_hidden * up_val * sigmoid * (1.0 + gate_val * (1.0 - sigmoid))).astype(BF16)
        grad_up = (grad_hidden * silu).astype(BF16)
        out_rows = lax.psum_scatter(
            dot_f32(hidden_low, down_local).astype(BF16), "dp", scatter_dimension=0, tiled=True
        )
        grad_b_rows = lax.psum_scatter(
            jnp.einsum(
                "rcf,fcd->rd",
                jnp.stack([grad_gate, grad_up], axis=1),
                gate_up_local,
                preferred_element_type=F32,
            ).astype(BF16),
            "dp",
            scatter_dimension=0,
            tiled=True,
        )
        out_slots = to_planes(out_rows, experts)
        grad_b_slots = to_planes(grad_b_rows, experts)

        gated_table = jnp.sum(hits * gates_mlp[None], axis=2).T
        gated_high = gated_table.astype(BF16)
        gated_low = (gated_table - gated_high.astype(F32)).astype(BF16)
        mlp_sum = dot_f32(gated_high, out_slots) + dot_f32(gated_low, out_slots)
        mixed_parts.append((hidden_state + mlp_sum).astype(BF16))

        cot_out = jnp.einsum("td,sd->st", cot, out_slots, preferred_element_type=F32)
        grad_gates_mlp = jnp.sum(hits * cot_out[..., None], axis=0)
        dlm = gate_backward(gates_mlp, grad_gates_mlp, onehot_mlp)
        grad_b = jnp.einsum("st,sd->td", table, grad_b_slots, preferred_element_type=F32) + jnp.einsum(
            "re,de->rd", dlm, router_two, precision=PRECISION_TOP
        )
        grad_state, gain_two_term = norm_backward(hidden_state, inverse_two, gain_two, grad_b)
        grad_state = cot.astype(F32) + grad_state
        dh_all = lax.all_gather(grad_state.astype(BF16), "dp", axis=0, tiled=True)

        grad_context_dense = jnp.einsum(
            "td,cd->tc", dh_all, output_rows, preferred_element_type=F32
        ).reshape(length, 1, experts, head_cols)
        grad_context = jnp.sum(grad_context_dense * onehot_all[..., None], axis=2)
        dga = lax.psum_scatter(
            jnp.sum(grad_context * context.astype(F32), axis=-1),
            "dp",
            scatter_dimension=0,
            tiled=True,
        )
        grad_context = (
            (grad_context * gates_all[..., None]).astype(BF16).reshape(length, 2, heads, HEAD_WIDTH)
        )
        score = score_of(query_vectors, keys, mask)
        probs_full = jnp.exp(score - log_total)
        probs_low = probs_full.astype(BF16)
        grad_probs = jnp.einsum("lkhd,mhd->khlm", grad_context, values, preferred_element_type=F32)
        grad_scores = (
            probs_full * (grad_probs - jnp.sum(probs_full * grad_probs, axis=-1, keepdims=True))
        ).astype(BF16)
        grad_queries = (
            jnp.einsum("khlm,mhd->lkhd", grad_scores, keys, preferred_element_type=F32) * scale
        )
        grad_keys = (
            jnp.einsum("khlm,lkhd->mhd", grad_scores, query_vectors, preferred_element_type=F32)
            * scale
        )
        grad_values = jnp.einsum("khlm,lkhd->mhd", probs_low, grad_context, preferred_element_type=F32)
        grad_keys = rotate_back(grad_keys, cosine[:, None], sine_table[:, None])
        grad_query_raw = (
            rotate_back(grad_queries, cosine[:, None, None], sine_table[:, None, None])
            .astype(BF16)
            .astype(F32)
            .reshape(length, 2, 1, head_cols)
        )
        grad_query_dense = jnp.sum(grad_query_raw * onehot_all[..., None], axis=1)
        grad_qkv = jnp.concatenate(
            [
                grad_query_dense.reshape(length, experts * head_cols).astype(BF16),
                grad_keys.reshape(length, head_cols).astype(BF16),
                grad_values.reshape(length, head_cols).astype(BF16),
            ],
            axis=1,
        )
        grad_a = lax.psum_scatter(
            jnp.einsum("tc,dc->td", grad_qkv, qkv_cols, preferred_element_type=F32).astype(BF16),
            "dp",
            scatter_dimension=0,
            tiled=True,
        ).astype(F32)
        onehot_home = route_onehot(attn_routes[u], experts)
        gates_home = lax.dynamic_slice_in_dim(gates_all, my_dp * local_len, local_len, axis=0)
        dla = gate_backward(gates_home, dga, onehot_home)
        grad_a = grad_a + jnp.einsum("re,de->rd", dla, router_one, precision=PRECISION_TOP)
        grad_inputs, gain_one_term = norm_backward(inputs, inverse_one, gain_one, grad_a)
        input_parts.append(grad_state + grad_inputs)

        gain_one_sum = gain_one_sum + gain_one_term
        gain_two_sum = gain_two_sum + gain_two_term
        a_list.append(a_all)
        g_list.append(grad_qkv)
        ctx_list.append(context_gated)
        dh_list.append(dh_all)
        b_rows_list.append(b_rows)
        dgate_list.append(grad_gate)
        dup_list.append(grad_up)
        hid_list.append(hidden_gated)
        cot_rows_list.append(cot_rows)
        a_home_list.append(a_home)
        dla_list.append(dla)
        b_home_list.append(b_home)
        dlm_list.append(dlm)

    def summed(pattern, lefts, rights):
        total = None
        for left, right in zip(lefts, rights):
            term = jnp.einsum(pattern, left, right, preferred_element_type=F32)
            total = term if total is None else total + term
        return total

    down_grad = summed("rf,rd->fd", hid_list, cot_rows_list)
    gate_grad = summed("rf,rd->fd", dgate_list, b_rows_list)
    up_grad = summed("rf,rd->fd", dup_list, b_rows_list)
    gate_up_grad = jnp.stack([gate_grad, up_grad], axis=1)

    output_grad = lax.psum_scatter(
        summed("tc,td->cd", ctx_list, dh_list).astype(BF16), "expert", scatter_dimension=0, tiled=True
    ).astype(F32)

    qkv_grad = summed("td,tc->dc", a_list, g_list).astype(BF16)
    query_part = (
        qkv_grad[:, : experts * head_cols]
        .reshape(dp, query_rows, experts, head_cols)
        .transpose(2, 0, 1, 3)
    )
    kv_part = (
        qkv_grad[:, experts * head_cols :]
        .reshape(dp, planes, kv_rows * 2, head_cols)
        .transpose(1, 0, 2, 3)
    )
    packed_grad = lax.psum_scatter(
        jnp.concatenate([query_part, kv_part], axis=2), "expert", scatter_dimension=0, tiled=False
    )
    packed_grad = lax.all_to_all(packed_grad, "dp", split_axis=0, concat_axis=0, tiled=True)
    packed_grad = packed_grad.transpose(1, 0, 2).reshape(-1, width).astype(F32)
    query_grad = packed_grad[:query_rows]
    kv_grad = packed_grad[query_rows:].reshape(kv_rows, 2, width)

    router_one_grad = jnp.einsum(
        "rd,re->de",
        jnp.concatenate(a_home_list, axis=0).astype(F32),
        jnp.concatenate(dla_list, axis=0),
        precision=PRECISION_TOP,
    )
    router_two_grad = jnp.einsum(
        "rd,re->de",
        jnp.concatenate(b_home_list, axis=0).astype(F32),
        jnp.concatenate(dlm_list, axis=0),
        precision=PRECISION_TOP,
    )
    small_grad = jnp.concatenate(
        [gain_one_sum[:, None], gain_two_sum[:, None], router_one_grad, router_two_grad], axis=1
    )
    small_grad = lax.psum_scatter(small_grad, both, scatter_dimension=0, tiled=True)

    shape = (micro_count, seq_count, local_len, width)
    return (
        jnp.stack(mixed_parts, axis=0).reshape(shape),
        jnp.stack(input_parts, axis=0).reshape(shape),
        small_grad[:, 0],
        kv_grad,
        small_grad[:, 2 : 2 + experts],
        query_grad[None],
        output_grad[None],
        small_grad[:, 1],
        small_grad[:, 2 + experts :],
        gate_up_grad[None],
        down_grad[None],
    )


def solution(mesh):
    in_specs = (
        P(None, "expert", "dp", None),
        P(None, "expert", None),
        P(None, "expert", "dp", None),
        P(None, "expert", "dp", None),
        P(None, "expert", "dp", None),
        P(("dp", "expert")),
        P(("dp", "expert"), None, None),
        P(("dp", "expert"), None),
        P("expert", "dp", None),
        P("expert", "dp", None),
        P(("dp", "expert")),
        P(("dp", "expert"), None),
        P("expert", "dp", None, None),
        P("expert", "dp", None),
    )
    out_specs = (
        P(None, "expert", "dp", None),
        P(None, "expert", "dp", None),
        P(("dp", "expert")),
        P(("dp", "expert"), None, None),
        P(("dp", "expert"), None),
        P("expert", "dp", None),
        P("expert", "dp", None),
        P(("dp", "expert")),
        P(("dp", "expert"), None),
        P("expert", "dp", None, None),
        P("expert", "dp", None),
    )
    return jax.shard_map(
        per_device, mesh=mesh, in_specs=in_specs, out_specs=out_specs, check_vma=False
    )
```

```python
import functools

import jax
import jax.numpy as jnp
from jax import lax
from jax.experimental import pallas as pl
from jax.experimental.pallas import tpu as pltpu
from jax.sharding import PartitionSpec as P

HEAD_WIDTH = 128


EPSILON = 1e-05
THETA_BASE = 10000.0
NEGATIVE = -1000000000.0
PRECISION_TOP = lax.Precision.HIGHEST
BF16 = jnp.bfloat16
F32 = jnp.float32


def rope_in(values, cosine, sine_signed):
    return values * cosine + pltpu.roll(values, HEAD_WIDTH // 2, 1) * sine_signed


def contract(left, right, left_dim, right_dim):
    return lax.dot_general(
        left, right, (((left_dim,), (right_dim,)), ((), ())), preferred_element_type=F32
    )


def attn_forward_kernel(
    routes_ref, gates_ref, seg_col_ref, seg_row_ref, cos_ref, sin_ref, qkv_ref,
    q_ref, k_ref, v_ref, o_ref, gated_ref, *, experts, block, scale,
):
    length = cos_ref.shape[0]
    width = HEAD_WIDTH
    cosine = cos_ref[...]
    sine = sin_ref[...]
    k_ref[0] = rope_in(qkv_ref[:, experts * width : (experts + 1) * width], cosine, sine).astype(BF16)
    v_ref[0] = qkv_ref[:, (experts + 1) * width :].astype(BF16)
    for choice in range(2):
        route = routes_ref[:, choice : choice + 1]
        raw = qkv_ref[:, :width]
        for e in range(1, experts):
            raw = jnp.where(route == e, qkv_ref[:, e * width : (e + 1) * width], raw)
        q_ref[0, choice] = rope_in(raw.astype(BF16).astype(F32), cosine, sine).astype(BF16)
    for i in range(length // block):
        rows = slice(i * block, (i + 1) * block)
        n = (i + 1) * block
        keys = k_ref[0, :n]
        values = v_ref[0, :n]
        mask = (
            lax.broadcasted_iota(jnp.int32, (block, n), 1)
            <= lax.broadcasted_iota(jnp.int32, (block, n), 0) + i * block
        ) & (seg_col_ref[rows, :] == seg_row_ref[:, :n])
        for choice in range(2):
            score = jnp.where(mask, contract(q_ref[0, choice, rows], keys, 1, 1) * scale, NEGATIVE)
            exponent = jnp.exp(score - jnp.max(score, axis=1, keepdims=True))
            inverse = 1.0 / jnp.sum(exponent, axis=1, keepdims=True)
            probs = (exponent * inverse).astype(BF16)
            o_ref[0, choice, rows] = contract(probs, values, 1, 0).astype(BF16)
    first = o_ref[0, 0].astype(F32) * gates_ref[:, 0:1]
    second = o_ref[0, 1].astype(F32) * gates_ref[:, 1:2]
    for e in range(experts):
        part = jnp.where(routes_ref[:, 0:1] == e, first, 0.0)
        part = jnp.where(routes_ref[:, 1:2] == e, second, part)
        gated_ref[:, e * width : (e + 1) * width] = part.astype(BF16)


def attn_backward_kernel(
    routes_ref, gates_ref, seg_col_ref, seg_row_ref, cos_ref, sin_ref, q_ref, k_ref, v_ref, o_ref, up_ref,
    grad_ref, dgate_ref, dctx_ref, dq_ref, dk_ref, dv_ref, *, experts, block, scale,
):
    length = cos_ref.shape[0]
    width = HEAD_WIDTH
    lanes = lax.broadcasted_iota(jnp.int32, (length, width), 1)
    dgate = jnp.zeros((length, width), F32)
    for choice in range(2):
        route = routes_ref[:, choice : choice + 1]
        up = up_ref[:, :width]
        for e in range(1, experts):
            up = jnp.where(route == e, up_ref[:, e * width : (e + 1) * width], up)
        part = jnp.sum(up * o_ref[0, choice].astype(F32), axis=1, keepdims=True)
        dgate = dgate + jnp.where(lanes == choice, part, 0.0)
        dctx_ref[choice] = (up * gates_ref[:, choice : choice + 1]).astype(BF16)
    dgate_ref[0] = dgate
    dk_ref[...] = jnp.zeros_like(dk_ref)
    dv_ref[...] = jnp.zeros_like(dv_ref)
    for i in range(length // block):
        rows = slice(i * block, (i + 1) * block)
        n = (i + 1) * block
        keys = k_ref[0, :n]
        values = v_ref[0, :n]
        mask = (
            lax.broadcasted_iota(jnp.int32, (n, block), 0)
            <= lax.broadcasted_iota(jnp.int32, (n, block), 1) + i * block
        ) & (seg_col_ref[:n, :] == seg_row_ref[:, rows])
        for choice in range(2):
            query = q_ref[0, choice, rows]
            dctx = dctx_ref[choice, rows]
            score = jnp.where(mask, contract(keys, query, 1, 1) * scale, NEGATIVE)
            exponent = jnp.exp(score - jnp.max(score, axis=0, keepdims=True))
            probs = exponent * (1.0 / jnp.sum(exponent, axis=0, keepdims=True))
            dprobs = contract(values, dctx, 1, 1)
            dscore = (probs * (dprobs - jnp.sum(probs * dprobs, axis=0, keepdims=True))).astype(BF16)
            dv_ref[:n] += contract(probs.astype(BF16), dctx, 1, 0)
            dk_ref[:n] += contract(dscore, query, 1, 0)
            dq_ref[choice, rows] = contract(dscore, keys, 0, 0)
    cosine = cos_ref[...]
    sine = -sin_ref[...]
    first = rope_in(dq_ref[0] * scale, cosine, sine)
    second = rope_in(dq_ref[1] * scale, cosine, sine)
    for e in range(experts):
        part = jnp.where(routes_ref[:, 0:1] == e, first, 0.0)
        part = jnp.where(routes_ref[:, 1:2] == e, second, part)
        grad_ref[:, e * width : (e + 1) * width] = part.astype(BF16)
    grad_ref[:, experts * width : (experts + 1) * width] = rope_in(
        dk_ref[...] * scale, cosine, sine
    ).astype(BF16)
    grad_ref[:, (experts + 1) * width :] = dv_ref[...].astype(BF16)


def attn_forward(routes, gates, segments, cosine, sine, qkv, experts):
    length = qkv.shape[0]
    width = HEAD_WIDTH
    heads = qkv.shape[1] // ((experts + 2) * width)
    whole = lambda *shape: pl.BlockSpec(shape, lambda h: (0,) * len(shape))
    head3 = pl.BlockSpec((1, length, width), lambda h: (h, 0, 0))
    head4 = pl.BlockSpec((1, 2, length, width), lambda h: (h, 0, 0, 0))
    cols = lambda parts: pl.BlockSpec((length, parts * width), lambda h: (0, h))
    scores = heads * length * length * 2
    return pl.pallas_call(
        functools.partial(attn_forward_kernel, experts=experts, block=min(256, length), scale=width**-0.5),
        grid=(heads,),
        in_specs=[whole(length, 2), whole(length, 2), whole(length, 1), whole(1, length),
                  whole(length, width), whole(length, width), cols(experts + 2)],
        out_specs=[head4, head3, head3, head4, cols(experts)],
        out_shape=[
            jax.ShapeDtypeStruct((heads, 2, length, width), BF16),
            jax.ShapeDtypeStruct((heads, length, width), BF16),
            jax.ShapeDtypeStruct((heads, length, width), BF16),
            jax.ShapeDtypeStruct((heads, 2, length, width), BF16),
            jax.ShapeDtypeStruct((length, heads * experts * width), BF16),
        ],
        compiler_params=pltpu.CompilerParams(vmem_limit_bytes=48 * 2**20),
        cost_estimate=pl.CostEstimate(flops=scores * width * 8, bytes_accessed=12 * 2**20, transcendentals=scores),
    )(routes, gates, segments[:, None], segments[None, :], cosine, sine, qkv)


def attn_backward(routes, gates, segments, cosine, sine, q, k, v, o, up, experts):
    heads, _, length, width = q.shape
    whole = lambda *shape: pl.BlockSpec(shape, lambda h: (0,) * len(shape))
    head3 = pl.BlockSpec((1, length, width), lambda h: (h, 0, 0))
    head4 = pl.BlockSpec((1, 2, length, width), lambda h: (h, 0, 0, 0))
    cols = lambda parts: pl.BlockSpec((length, parts * width), lambda h: (0, h))
    scores = heads * length * length * 2
    return pl.pallas_call(
        functools.partial(attn_backward_kernel, experts=experts, block=min(256, length), scale=width**-0.5),
        grid=(heads,),
        in_specs=[whole(length, 2), whole(length, 2), whole(length, 1), whole(1, length),
                  whole(length, width), whole(length, width), head4, head3, head3, head4, cols(experts)],
        out_specs=[cols(experts + 2), head3],
        out_shape=[
            jax.ShapeDtypeStruct((length, heads * (experts + 2) * width), BF16),
            jax.ShapeDtypeStruct((heads, length, width), F32),
        ],
        scratch_shapes=[
            pltpu.VMEM((2, length, width), BF16),
            pltpu.VMEM((2, length, width), F32),
            pltpu.VMEM((length, width), F32),
            pltpu.VMEM((length, width), F32),
        ],
        compiler_params=pltpu.CompilerParams(vmem_limit_bytes=48 * 2**20),
        cost_estimate=pl.CostEstimate(flops=scores * width * 20, bytes_accessed=12 * 2**20, transcendentals=scores),
    )(routes, gates, segments[:, None], segments[None, :], cosine, sine, q, k, v, o, up)


def rope_tables(positions, half_dim):
    frequency = THETA_BASE ** (-jnp.arange(half_dim, dtype=F32) / half_dim)
    angles = positions.astype(F32)[:, None] * frequency[None, :]
    return (jnp.cos(angles), jnp.sin(angles))


def norm_forward(values, gain_row):
    inverse = lax.rsqrt(jnp.mean(values * values, axis=-1, keepdims=True) + EPSILON)
    return (values * inverse * gain_row, inverse)


def norm_backward(values, inverse, gain_row, grad_normed):
    scaled = gain_row * grad_normed
    gain_term = jnp.sum(grad_normed * values * inverse, axis=0)
    grad_values = inverse * scaled - values * inverse**3 * jnp.mean(
        scaled * values, axis=-1, keepdims=True
    )
    return (grad_values, gain_term)


def route_onehot(routes, experts):
    return (routes[..., None] == jnp.arange(experts, dtype=jnp.int32)).astype(F32)


def gate_forward(logits, onehot):
    chosen = jnp.sum(logits[:, None, :] * onehot, axis=-1)
    return jax.nn.softmax(chosen, axis=-1)


def gate_backward(gate_probs, grad_gates, onehot):
    centered = gate_probs * (grad_gates - jnp.sum(gate_probs * grad_gates, axis=-1, keepdims=True))
    return jnp.sum(centered[..., None] * onehot, axis=1)


def slot_columns(routes, experts, capacity):
    flat_routes = routes.reshape(-1)
    onehot = (flat_routes[:, None] == jnp.arange(experts, dtype=jnp.int32)[None, :]).astype(
        jnp.int32
    )
    slot_rank = jnp.sum((jnp.cumsum(onehot, axis=0) - 1) * onehot, axis=1)
    return (flat_routes * capacity + slot_rank).reshape(routes.shape)


def dot_f32(left, right):
    return jnp.dot(left, right, preferred_element_type=F32)


def after(value, *others):
    return lax.optimization_barrier((value,) + others)[0]


def shift_planes(value, amount):
    planes = lax.axis_size("expert")
    return lax.ppermute(value, "expert", [(i, (i + amount) % planes) for i in range(planes)])


def exchange_planes(blocks, direction):
    arrived = [blocks[0]]
    for c in range(1, blocks.shape[0]):
        arrived.append(shift_planes(blocks[c], direction * c))
    return jnp.stack(arrived, axis=0)


def gather_planes(value, me):
    planes = lax.axis_size("expert")
    right, left = value, value
    rights, lefts = [], []
    for d in range(1, planes):
        right = lax.ppermute(right, "expert", [(i, i + 1) for i in range(d - 1, planes - 1)])
        left = lax.ppermute(left, "expert", [(i + 1, i) for i in range(0, planes - d)])
        rights.append(right)
        lefts.append(left)
    gathered = [value]
    for c in range(1, planes):
        gathered.append(jnp.where(me + c < planes, lefts[c - 1], rights[planes - c - 1]))
    return gathered


def reduce_planes(parts):
    planes = len(parts)
    right, left = None, None
    for t in range(1, planes):
        send_right, send_left = parts[planes - t], parts[t]
        if right is not None:
            send_right = (send_right.astype(F32) + right.astype(F32)).astype(BF16)
            send_left = (send_left.astype(F32) + left.astype(F32)).astype(BF16)
        right = lax.ppermute(send_right, "expert", [(i, i + 1) for i in range(0, t)])
        left = lax.ppermute(
            send_left, "expert", [(i, i - 1) for i in range(planes - t, planes)]
        )
    return parts[0].astype(F32) + right.astype(F32) + left.astype(F32)


def swap_dp(value, mask):
    size = lax.axis_size("dp")
    return lax.ppermute(value, "dp", [(i, i ^ mask) for i in range(size)])


def all_sum(value, axis):
    size = lax.axis_size(axis)
    mask = 1
    while mask < size:
        value = value + lax.ppermute(value, axis, [(i, i ^ mask) for i in range(size)])
        mask *= 2
    return value


def reduce_rows(left, matmul, me):
    size = lax.axis_size("dp")
    blocks = left.reshape(size // 2, 2, left.shape[0] // size, left.shape[1])
    core, chip = me % 2, me // 2

    def half(index):
        rows = lax.dynamic_index_in_dim(blocks, index, axis=1, keepdims=False)
        return matmul(rows.reshape(-1, left.shape[1])).reshape(size // 2, blocks.shape[2], -1)

    arrived = swap_dp(half(1 - core).astype(BF16), 1)
    mine = half(core) + arrived.astype(F32)
    low = mine.astype(BF16)
    total = lax.dynamic_index_in_dim(low, chip, axis=0, keepdims=False).astype(F32)
    for other in range(1, size // 2):
        send = lax.dynamic_index_in_dim(low, chip ^ other, axis=0, keepdims=False)
        total = total + swap_dp(send, 2 * other).astype(F32)
    return total


def per_device(
    tokens,
    segment_ids,
    attn_routes,
    mlp_routes,
    cotangent,
    attn_gain,
    kv_weights,
    attn_router,
    query_maps,
    output_maps,
    mlp_gain,
    mlp_router,
    gate_up,
    down_maps,
):
    micro_count, seq_count, local_len, width = tokens.shape
    units = micro_count * seq_count
    length = segment_ids.shape[2]
    experts = attn_router.shape[1]
    dp = lax.axis_size("dp")
    planes = lax.axis_size("expert")
    capacity = 2 * local_len // experts
    slots = experts * capacity
    head_cols = width // dp
    heads = head_cols // HEAD_WIDTH
    plane = lax.axis_index("expert")
    my_dp = lax.axis_index("dp")

    tokens = tokens.reshape(units, local_len, width)
    cotangent = cotangent.reshape(units, local_len, width)
    segments = segment_ids.reshape(units, length)
    attn_routes = attn_routes.reshape(units, local_len, 2)
    mlp_routes = mlp_routes.reshape(units, local_len, 2)

    slot_ids = jnp.arange(slots, dtype=jnp.int32)
    hits_list, tables, x_alls, infos = [], [], [], []
    for u in range(units):
        columns = slot_columns((mlp_routes[u] - plane) % experts, experts, capacity)
        hits = (columns[None] == slot_ids[:, None, None]).astype(F32)
        hits_list.append(hits)
        tables.append(jnp.sum(hits, axis=2).astype(BF16))
        other = jnp.sum(hits * mlp_routes[u][None, :, ::-1].astype(F32), axis=(1, 2))
        info = jnp.concatenate([attn_routes[u].astype(F32).reshape(-1), other])
        info = jnp.pad(info, (0, 16 * width - info.shape[0])).reshape(16, width).astype(BF16)
        gathered = lax.all_gather(jnp.concatenate([tokens[u], info], axis=0), "dp", axis=0)
        x_alls.append(gathered[:, :local_len].reshape(length, width))
        infos.append(gathered[:, local_len])
    routes_count = 2 * local_len
    others = jnp.stack([i[:, routes_count : routes_count + slots] for i in infos], axis=0)
    others = others.reshape(units * dp, experts, capacity).transpose(1, 0, 2)
    others = exchange_planes(others, 1)
    other_rows = (
        others.reshape(planes, units, dp, capacity)
        .transpose(1, 2, 0, 3)
        .reshape(units, dp * slots)
        .astype(jnp.int32)
    )

    kv_rows = kv_weights.shape[0]
    query_rows = query_maps.shape[1]
    params = jnp.concatenate(
        [attn_gain[:, None], mlp_gain[:, None], attn_router, mlp_router], axis=1
    ).reshape(-1)
    param_count = params.shape[0]
    params = jnp.pad(params, (0, 16 * head_cols - param_count)).reshape(1, 16, head_cols)
    packed = jnp.concatenate([query_maps[0], kv_weights.reshape(kv_rows * 2, width)], axis=0)
    packed = packed.reshape(-1, dp, head_cols).transpose(1, 0, 2)
    packed = jnp.concatenate([packed, jnp.broadcast_to(params, (dp, 16, head_cols))], axis=1)
    packed = lax.all_to_all(packed, "dp", split_axis=0, concat_axis=0, tiled=True)
    packed = gather_planes(packed, plane)
    output_rows = after(output_maps[0], packed[-1])
    output_rows = gather_planes(output_rows, plane)

    shared = jnp.stack([p[:, query_rows:] for p in packed], axis=0)
    shared = lax.dynamic_slice_in_dim(
        jnp.concatenate([shared, shared], axis=0), (planes - plane) % planes, planes, axis=0
    ).transpose(1, 0, 2, 3)
    kv_cols = shared[:, :, : 2 * kv_rows].reshape(width, 2, heads, HEAD_WIDTH).transpose(0, 2, 1, 3)
    params = shared[:, :, 2 * kv_rows :].reshape(dp * planes, -1)[:, :param_count]
    params = params.reshape(width, 2 + 2 * experts)
    gain_one = params[:, 0].astype(F32)
    gain_two = params[:, 1].astype(F32)
    router_one_low = params[:, 2 : 2 + experts]
    router_two_low = params[:, 2 + experts :]
    router_one = router_one_low.astype(F32)
    router_two = router_two_low.astype(F32)
    query_cols = jnp.stack(
        [p[:, :query_rows].reshape(width, heads, HEAD_WIDTH) for p in packed], axis=2
    )
    qkv_cols = jnp.concatenate([query_cols, kv_cols], axis=2).reshape(width, -1)
    output_rows = jnp.stack(
        [o.reshape(heads, HEAD_WIDTH, width) for o in output_rows], axis=1
    ).reshape(experts * head_cols, width)

    cosine, sine_table = rope_tables(jnp.arange(length, dtype=jnp.int32), HEAD_WIDTH // 2)
    cosine = jnp.concatenate([cosine, cosine], axis=1)
    sine_table = jnp.concatenate([-sine_table, sine_table], axis=1)

    gate_up_local = gate_up[0]
    down_local = down_maps[0]

    def to_experts(slot_rows):
        moved = exchange_planes(slot_rows.reshape(planes, capacity, width), 1)
        return lax.all_gather(moved.reshape(slots, width), "dp", axis=0, tiled=True)

    def to_home(rows):
        return exchange_planes(rows.reshape(planes, capacity, width), -1).reshape(slots, width)

    mixed_parts = []
    input_parts = []
    a_list, g_list, ctx_list, dh_list = [], [], [], []
    b_rows_list, dgate_list, dup_list, hid_list, cot_rows_list = [], [], [], [], []
    a_home_list, dla_list, b_home_list, dlm_list = [], [], [], []
    gain_one_sum = jnp.zeros((width,), F32)
    gain_two_sum = jnp.zeros((width,), F32)
    for u in range(units):
        table = tables[u]
        hits = hits_list[u]
        inputs = tokens[u].astype(F32)
        normed_one, inverse_one = norm_forward(inputs, gain_one)
        a_home = normed_one.astype(BF16)
        a_all = norm_forward(x_alls[u].astype(F32), gain_one)[0].astype(BF16)

        cot = cotangent[u]
        cot_slots = after(dot_f32(table, cot).astype(BF16), output_rows[:16])
        cot_rows = to_experts(cot_slots)
        cot_hidden = jnp.einsum("rd,fd->rf", cot_rows, down_local, preferred_element_type=F32)

        routes_all = infos[u][:, :routes_count].reshape(length, 2).astype(jnp.int32)
        routes_here = (routes_all - plane) % experts
        gates_all = gate_forward(dot_f32(a_all, router_one_low), route_onehot(routes_all, experts))
        qkv = dot_f32(a_all, qkv_cols)
        queries, keys, values, context, context_gated = attn_forward(
            routes_here, gates_all, segments[u], cosine, sine_table, qkv, experts
        )
        hidden_state = inputs + reduce_rows(
            context_gated, lambda rows: dot_f32(rows, output_rows), my_dp
        )

        normed_two, inverse_two = norm_forward(hidden_state, gain_two)
        b_home = normed_two.astype(BF16)
        onehot_mlp = route_onehot(mlp_routes[u], experts)
        gates_mlp = gate_forward(dot_f32(b_home, router_two_low), onehot_mlp)
        b_rows = to_experts(dot_f32(table, b_home).astype(BF16))
        logits_rows = dot_f32(b_rows, router_two_low)
        own_logit = jnp.sum(jnp.where(jnp.arange(experts)[None] == plane, logits_rows, 0.0), axis=1)
        other_logit = jnp.sum(
            jnp.where(jnp.arange(experts)[None] == other_rows[u][:, None], logits_rows, 0.0), axis=1
        )
        gate_rows = jax.nn.sigmoid(own_logit - other_logit)[:, None]
        gate_up_rows = jnp.einsum("rd,fcd->rcf", b_rows, gate_up_local, preferred_element_type=F32)
        gate_val = gate_up_rows[:, 0]
        up_val = gate_up_rows[:, 1]
        sigmoid = jax.nn.sigmoid(gate_val)
        silu = gate_val * sigmoid
        hidden = silu * up_val
        hidden_low = hidden.astype(BF16)
        hidden_gated = (hidden * gate_rows).astype(BF16)
        grad_hidden = cot_hidden * gate_rows
        grad_gate = (grad_hidden * up_val * sigmoid * (1.0 + gate_val * (1.0 - sigmoid))).astype(BF16)
        grad_up = (grad_hidden * silu).astype(BF16)
        hidden_units = gate_val.shape[1]
        out_rows = lax.psum_scatter(
            dot_f32(hidden_low, down_local).astype(BF16), "dp", scatter_dimension=0, tiled=True
        )
        grad_b_rows = reduce_rows(
            jnp.concatenate([grad_gate, grad_up], axis=1),
            lambda rows: jnp.einsum(
                "rcf,fcd->rd",
                rows.reshape(-1, 2, hidden_units),
                gate_up_local,
                preferred_element_type=F32,
            ),
            my_dp,
        ).astype(BF16)
        out_slots = to_home(out_rows)
        grad_b_slots = to_home(grad_b_rows)

        gated_table = jnp.sum(hits * gates_mlp[None], axis=2).T
        gated_high = gated_table.astype(BF16)
        gated_low = (gated_table - gated_high.astype(F32)).astype(BF16)
        mlp_sum = dot_f32(gated_high, out_slots) + dot_f32(gated_low, out_slots)
        mixed_parts.append((hidden_state + mlp_sum).astype(BF16))

        cot_out = jnp.einsum("td,sd->st", cot, out_slots, preferred_element_type=F32)
        grad_gates_mlp = jnp.sum(hits * cot_out[..., None], axis=0)
        dlm = gate_backward(gates_mlp, grad_gates_mlp, onehot_mlp)
        grad_b = jnp.einsum("st,sd->td", table, grad_b_slots, preferred_element_type=F32) + jnp.einsum(
            "re,de->rd", dlm, router_two, precision=PRECISION_TOP
        )
        grad_state, gain_two_term = norm_backward(hidden_state, inverse_two, gain_two, grad_b)
        grad_state = cot.astype(F32) + grad_state
        dh_all = lax.all_gather(grad_state.astype(BF16), "dp", axis=0, tiled=True)

        grad_context = jnp.einsum("td,cd->tc", dh_all, output_rows, preferred_element_type=F32)
        grad_qkv, grad_gates = attn_backward(
            routes_here,
            gates_all,
            segments[u],
            cosine,
            sine_table,
            queries,
            keys,
            values,
            context,
            grad_context,
            experts,
        )
        dga = all_sum(jnp.sum(grad_gates[:, :, :2], axis=0), "dp")
        dga = lax.dynamic_slice_in_dim(dga, my_dp * local_len, local_len, axis=0)
        grad_a = reduce_rows(
            grad_qkv,
            lambda rows: jnp.einsum("tc,dc->td", rows, qkv_cols, preferred_element_type=F32),
            my_dp,
        )
        onehot_home = route_onehot(attn_routes[u], experts)
        gates_home = lax.dynamic_slice_in_dim(gates_all, my_dp * local_len, local_len, axis=0)
        dla = gate_backward(gates_home, dga, onehot_home)
        grad_a = grad_a + jnp.einsum("re,de->rd", dla, router_one, precision=PRECISION_TOP)
        grad_inputs, gain_one_term = norm_backward(inputs, inverse_one, gain_one, grad_a)
        input_parts.append(grad_state + grad_inputs)

        gain_one_sum = gain_one_sum + gain_one_term
        gain_two_sum = gain_two_sum + gain_two_term
        a_list.append(a_all)
        g_list.append(grad_qkv)
        ctx_list.append(context_gated)
        dh_list.append(dh_all)
        b_rows_list.append(b_rows)
        dgate_list.append(grad_gate)
        dup_list.append(grad_up)
        hid_list.append(hidden_gated)
        cot_rows_list.append(cot_rows)
        a_home_list.append(a_home)
        dla_list.append(dla)
        b_home_list.append(b_home)
        dlm_list.append(dlm)

    def summed(pattern, lefts, rights):
        total = None
        for left, right in zip(lefts, rights):
            term = jnp.einsum(pattern, left, right, preferred_element_type=F32)
            total = term if total is None else total + term
        return total

    down_grad = summed("rf,rd->fd", hid_list, cot_rows_list)
    gate_grad = summed("rf,rd->fd", dgate_list, b_rows_list)
    up_grad = summed("rf,rd->fd", dup_list, b_rows_list)
    gate_up_grad = jnp.stack([gate_grad, up_grad], axis=1)

    output_part = summed("tc,td->cd", ctx_list, dh_list).astype(BF16)
    output_part = output_part.reshape(heads, experts, HEAD_WIDTH, width)
    output_grad = reduce_planes([output_part[:, c] for c in range(planes)])
    output_grad = output_grad.reshape(head_cols, width)

    qkv_grad = summed("td,tc->dc", a_list, g_list).astype(BF16)
    qkv_grad = qkv_grad.reshape(width, heads, experts + 2, HEAD_WIDTH)
    kv_part = qkv_grad[:, :, experts:].transpose(0, 2, 1, 3).reshape(dp, planes, 2 * kv_rows, head_cols)
    kv_part = kv_part.transpose(1, 0, 2, 3)
    kv_part = lax.dynamic_slice_in_dim(
        jnp.concatenate([kv_part, kv_part], axis=0), plane, planes, axis=0
    )
    parts = [
        jnp.concatenate([qkv_grad[:, :, c].reshape(dp, query_rows, head_cols), kv_part[c]], axis=1)
        for c in range(planes)
    ]
    packed_grad = reduce_planes(parts).astype(BF16)
    packed_grad = lax.all_to_all(packed_grad, "dp", split_axis=0, concat_axis=0, tiled=True)
    packed_grad = packed_grad.transpose(1, 0, 2).reshape(-1, width).astype(F32)
    query_grad = packed_grad[:query_rows]
    kv_grad = packed_grad[query_rows:].reshape(kv_rows, 2, width)

    router_one_grad = jnp.einsum(
        "re,rd->ed",
        jnp.concatenate(dla_list, axis=0),
        jnp.concatenate(a_home_list, axis=0).astype(F32),
        precision=PRECISION_TOP,
    )
    router_two_grad = jnp.einsum(
        "re,rd->ed",
        jnp.concatenate(dlm_list, axis=0),
        jnp.concatenate(b_home_list, axis=0).astype(F32),
        precision=PRECISION_TOP,
    )
    small_grad = jnp.concatenate(
        [gain_one_sum[None], gain_two_sum[None], router_one_grad, router_two_grad], axis=0
    )
    small_grad = all_sum(all_sum(small_grad, "dp"), "expert")
    small_grad = lax.dynamic_index_in_dim(
        small_grad.reshape(-1, dp * planes, kv_rows), my_dp * planes + plane, axis=1, keepdims=False
    )

    shape = (micro_count, seq_count, local_len, width)
    return (
        jnp.stack(mixed_parts, axis=0).reshape(shape),
        jnp.stack(input_parts, axis=0).reshape(shape),
        small_grad[0],
        kv_grad,
        small_grad[2 : 2 + experts].T,
        query_grad[None],
        output_grad[None],
        small_grad[1],
        small_grad[2 + experts :].T,
        gate_up_grad[None],
        down_grad[None],
    )


def solution(mesh):
    in_specs = (
        P(None, "expert", "dp", None),
        P(None, "expert", None),
        P(None, "expert", "dp", None),
        P(None, "expert", "dp", None),
        P(None, "expert", "dp", None),
        P(("dp", "expert")),
        P(("dp", "expert"), None, None),
        P(("dp", "expert"), None),
        P("expert", "dp", None),
        P("expert", "dp", None),
        P(("dp", "expert")),
        P(("dp", "expert"), None),
        P("expert", "dp", None, None),
        P("expert", "dp", None),
    )
    out_specs = (
        P(None, "expert", "dp", None),
        P(None, "expert", "dp", None),
        P(("dp", "expert")),
        P(("dp", "expert"), None, None),
        P(("dp", "expert"), None),
        P("expert", "dp", None),
        P("expert", "dp", None),
        P(("dp", "expert")),
        P(("dp", "expert"), None),
        P("expert", "dp", None, None),
        P("expert", "dp", None),
    )
    return jax.shard_map(
        per_device, mesh=mesh, in_specs=in_specs, out_specs=out_specs, check_vma=False
    )
```

```python
import functools

import jax
import jax.numpy as jnp
from jax import lax
from jax.experimental import pallas as pl
from jax.experimental.pallas import tpu as pltpu
from jax.sharding import PartitionSpec as P

HEAD_WIDTH = 128


EPSILON = 1e-05
THETA_BASE = 10000.0
NEGATIVE = -1000000000.0
PRECISION_TOP = lax.Precision.HIGHEST
BF16 = jnp.bfloat16
F32 = jnp.float32


def rope_in(values, cosine, sine_signed):
    return values * cosine + pltpu.roll(values, HEAD_WIDTH // 2, 1) * sine_signed


def contract(left, right, left_dim, right_dim):
    return lax.dot_general(
        left, right, (((left_dim,), (right_dim,)), ((), ())), preferred_element_type=F32
    )


def block_mask(seg_col_ref, seg_row_ref, i, block):
    n = (i + 1) * block
    rows = slice(i * block, n)
    return (
        lax.broadcasted_iota(jnp.int32, (n, block), 0)
        <= lax.broadcasted_iota(jnp.int32, (n, block), 1) + i * block
    ) & (seg_col_ref[:n, :] == seg_row_ref[:, rows])


def key_softmax(score):
    exponent = jnp.exp(score - jnp.max(score, axis=0, keepdims=True))
    return exponent * (1.0 / jnp.sum(exponent, axis=0, keepdims=True))


def attn_forward_kernel(*refs, experts, heads, block, scale):
    routes_ref, gates_ref, seg_col_ref, seg_row_ref, cos_ref, sin_ref, keys_ref, values_ref = refs[:8]
    raw_refs = refs[8 : 8 + experts]
    q_ref, k_ref, v_ref, o_ref, gated_ref = refs[8 + experts :]
    length = cos_ref.shape[0]
    width = HEAD_WIDTH
    cosine = cos_ref[...]
    sine = sin_ref[...]
    routes = [routes_ref[:, c : c + 1] for c in range(2)]
    for h in range(heads):
        cols = slice(h * width, (h + 1) * width)
        k_ref[h] = rope_in(keys_ref[:, cols], cosine, sine).astype(BF16)
        v_ref[h] = values_ref[:, cols]
        for choice in range(2):
            raw = raw_refs[0][:, cols].astype(F32)
            for e in range(1, experts):
                raw = jnp.where(routes[choice] == e, raw_refs[e][:, cols].astype(F32), raw)
            q_ref[h, choice] = rope_in(raw, cosine, sine).astype(BF16)
    for i in range(length // block):
        rows = slice(i * block, (i + 1) * block)
        n = (i + 1) * block
        mask = block_mask(seg_col_ref, seg_row_ref, i, block)
        for h in range(heads):
            for choice in range(2):
                score = contract(k_ref[h, :n], q_ref[h, choice, rows], 1, 1) * scale
                probs = key_softmax(jnp.where(mask, score, NEGATIVE)).astype(BF16)
                o_ref[h, choice, rows] = contract(probs, v_ref[h, :n], 0, 0).astype(BF16)
    for h in range(heads):
        first = o_ref[h, 0].astype(F32) * gates_ref[:, 0:1]
        second = o_ref[h, 1].astype(F32) * gates_ref[:, 1:2]
        for e in range(experts):
            part = jnp.where(routes[0] == e, first, 0.0)
            part = jnp.where(routes[1] == e, second, part)
            at = (e * heads + h) * width
            gated_ref[:, at : at + width] = part.astype(BF16)


def attn_backward_kernel(
    routes_ref, gates_ref, seg_col_ref, seg_row_ref, cos_ref, sin_ref, q_ref, k_ref, v_ref, o_ref, up_ref,
    grad_ref, dctx_ref, dq_ref, dk_ref, dv_ref, *, experts, heads, block, scale,
):
    length = cos_ref.shape[0]
    width = HEAD_WIDTH
    lanes = lax.broadcasted_iota(jnp.int32, (length, width), 1)
    routes = [routes_ref[:, c : c + 1] for c in range(2)]
    dgate = jnp.zeros((length, width), F32)
    for h in range(heads):
        for choice in range(2):
            up = up_ref[:, h * width : (h + 1) * width]
            for e in range(1, experts):
                at = (e * heads + h) * width
                up = jnp.where(routes[choice] == e, up_ref[:, at : at + width], up)
            part = jnp.sum(up * o_ref[h, choice].astype(F32), axis=1, keepdims=True)
            dgate = dgate + jnp.where(lanes == choice, part, 0.0)
            dctx_ref[h, choice] = (up * gates_ref[:, choice : choice + 1]).astype(BF16)
    grad_ref[:, (experts + 2) * heads * width :] = dgate.astype(BF16)
    dk_ref[...] = jnp.zeros_like(dk_ref)
    dv_ref[...] = jnp.zeros_like(dv_ref)
    for i in range(length // block):
        rows = slice(i * block, (i + 1) * block)
        n = (i + 1) * block
        mask = block_mask(seg_col_ref, seg_row_ref, i, block)
        for h in range(heads):
            for choice in range(2):
                query = q_ref[h, choice, rows]
                dctx = dctx_ref[h, choice, rows]
                score = contract(k_ref[h, :n], query, 1, 1) * scale
                probs = key_softmax(jnp.where(mask, score, NEGATIVE))
                dprobs = contract(v_ref[h, :n], dctx, 1, 1)
                dscore = probs * (dprobs - jnp.sum(probs * dprobs, axis=0, keepdims=True))
                dscore = dscore.astype(BF16)
                dv_ref[h, :n] += contract(probs.astype(BF16), dctx, 1, 0)
                dk_ref[h, :n] += contract(dscore, query, 1, 0)
                dq_ref[h, choice, rows] = contract(dscore, k_ref[h, :n], 0, 0)
    cosine = cos_ref[...]
    sine = -sin_ref[...]
    for h in range(heads):
        first = rope_in(dq_ref[h, 0] * scale, cosine, sine)
        second = rope_in(dq_ref[h, 1] * scale, cosine, sine)
        for e in range(experts):
            part = jnp.where(routes[0] == e, first, 0.0)
            part = jnp.where(routes[1] == e, second, part)
            at = (e * heads + h) * width
            grad_ref[:, at : at + width] = part.astype(BF16)
        at = (experts * heads + h) * width
        grad_ref[:, at : at + width] = rope_in(dk_ref[h] * scale, cosine, sine).astype(BF16)
        at = ((experts + 1) * heads + h) * width
        grad_ref[:, at : at + width] = dv_ref[h].astype(BF16)


def attn_forward(routes, gates, segments, cosine, sine, raws, keys, values):
    experts = len(raws)
    length, cols = raws[0].shape
    width = HEAD_WIDTH
    heads = cols // width
    scores = heads * length * length * 2
    return pl.pallas_call(
        functools.partial(
            attn_forward_kernel,
            experts=experts,
            heads=heads,
            block=min(256, length),
            scale=width**-0.5,
        ),
        out_shape=[
            jax.ShapeDtypeStruct((heads, 2, length, width), BF16),
            jax.ShapeDtypeStruct((heads, length, width), BF16),
            jax.ShapeDtypeStruct((heads, length, width), BF16),
            jax.ShapeDtypeStruct((heads, 2, length, width), BF16),
            jax.ShapeDtypeStruct((length, heads * experts * width), BF16),
        ],
        compiler_params=pltpu.CompilerParams(vmem_limit_bytes=48 * 2**20),
        cost_estimate=pl.CostEstimate(
            flops=scores * width * 8, bytes_accessed=12 * 2**20, transcendentals=scores
        ),
    )(routes, gates, segments[:, None], segments[None, :], cosine, sine, keys, values, *raws)


def attn_backward(routes, gates, segments, cosine, sine, q, k, v, o, up):
    heads, _, length, width = q.shape
    experts = up.shape[1] // (heads * width)
    scores = heads * length * length * 2
    return pl.pallas_call(
        functools.partial(
            attn_backward_kernel,
            experts=experts,
            heads=heads,
            block=min(256, length),
            scale=width**-0.5,
        ),
        out_shape=jax.ShapeDtypeStruct((length, (heads * (experts + 2) + 1) * width), BF16),
        scratch_shapes=[
            pltpu.VMEM((heads, 2, length, width), BF16),
            pltpu.VMEM((heads, 2, length, width), F32),
            pltpu.VMEM((heads, length, width), F32),
            pltpu.VMEM((heads, length, width), F32),
        ],
        compiler_params=pltpu.CompilerParams(vmem_limit_bytes=48 * 2**20),
        cost_estimate=pl.CostEstimate(
            flops=scores * width * 20, bytes_accessed=12 * 2**20, transcendentals=scores
        ),
    )(routes, gates, segments[:, None], segments[None, :], cosine, sine, q, k, v, o, up)


def mlp_kernel(
    place_ref, b_ref, cot_ref, other_ref, router_ref, gate_up_ref, down_ref,
    out_ref, grad_ref, hidden_ref, dhidden_ref,
):
    hidden_units = down_ref.shape[0]
    rows = b_ref[...]
    logits = contract(rows, router_ref[...], 1, 0)
    lanes = lax.broadcasted_iota(jnp.int32, logits.shape, 1)
    own = jnp.sum(jnp.where(lanes == place_ref[0], logits, 0.0), axis=1, keepdims=True)
    other = jnp.sum(jnp.where(lanes == other_ref[...], logits, 0.0), axis=1, keepdims=True)
    gates = jax.nn.sigmoid(own - other)
    both = contract(rows, gate_up_ref[...], 1, 1)
    gate_val = both[:, :hidden_units]
    up_val = both[:, hidden_units:]
    sigmoid = jax.nn.sigmoid(gate_val)
    silu = gate_val * sigmoid
    hidden = silu * up_val
    hidden_low = hidden.astype(BF16)
    hidden_ref[...] = (hidden * gates).astype(BF16)
    grad_plain = contract(cot_ref[...], down_ref[...], 1, 1)
    dgate = jnp.sum(grad_plain * hidden_low.astype(F32), axis=1, keepdims=True)
    width = out_ref.shape[1]
    grad_ref[:, width:] = jnp.broadcast_to(dgate, (dgate.shape[0], grad_ref.shape[1] - width)).astype(BF16)
    grad_hidden = grad_plain * gates
    dhidden_ref[:, :hidden_units] = (
        grad_hidden * up_val * sigmoid * (1.0 + gate_val * (1.0 - sigmoid))
    ).astype(BF16)
    dhidden_ref[:, hidden_units:] = (grad_hidden * silu).astype(BF16)
    out_ref[...] = contract(hidden_low, down_ref[...], 1, 0).astype(BF16)
    grad_ref[:, :width] = contract(dhidden_ref[...], gate_up_ref[...], 1, 0).astype(BF16)


def mlp_experts(place, b_rows, cot_rows, other_rows, router, gate_up, down, blocks):
    total, width = b_rows.shape
    hidden_units = down.shape[0]
    block = total // blocks
    by_row = lambda cols: pl.BlockSpec((block, cols), lambda i, place: (i, 0))
    fixed = lambda shape: pl.BlockSpec(shape, lambda i, place: (0, 0), pipeline_mode=pl.Buffered(1))
    return pl.pallas_call(
        mlp_kernel,
        grid_spec=pltpu.PrefetchScalarGridSpec(
            num_scalar_prefetch=1,
            grid=(blocks,),
            in_specs=[
                by_row(width),
                by_row(width),
                by_row(1),
                fixed(router.shape),
                fixed(gate_up.shape),
                fixed(down.shape),
            ],
            out_specs=[
                by_row(width),
                by_row(width + 128),
                by_row(hidden_units),
                by_row(2 * hidden_units),
            ],
        ),
        out_shape=[
            jax.ShapeDtypeStruct((total, width), BF16),
            jax.ShapeDtypeStruct((total, width + 128), BF16),
            jax.ShapeDtypeStruct((total, hidden_units), BF16),
            jax.ShapeDtypeStruct((total, 2 * hidden_units), BF16),
        ],
        compiler_params=pltpu.CompilerParams(vmem_limit_bytes=56 * 2**20),
        cost_estimate=pl.CostEstimate(
            flops=total * width * hidden_units * 12,
            bytes_accessed=4 * total * width * 2 + 6 * total * hidden_units + 6 * width * hidden_units,
            transcendentals=total * hidden_units,
        ),
    )(place, b_rows, cot_rows, other_rows, router, gate_up, down)


def rope_tables(positions, half_dim):
    frequency = THETA_BASE ** (-jnp.arange(half_dim, dtype=F32) / half_dim)
    angles = positions.astype(F32)[:, None] * frequency[None, :]
    return (jnp.cos(angles), jnp.sin(angles))


def norm_forward(values, gain_row):
    inverse = lax.rsqrt(jnp.mean(values * values, axis=-1, keepdims=True) + EPSILON)
    return (values * inverse * gain_row, inverse)


def norm_backward(values, inverse, gain_row, grad_normed):
    scaled = gain_row * grad_normed
    gain_term = jnp.sum(grad_normed * values * inverse, axis=0)
    grad_values = inverse * scaled - values * inverse**3 * jnp.mean(
        scaled * values, axis=-1, keepdims=True
    )
    return (grad_values, gain_term)


def route_onehot(routes, experts):
    return (routes[..., None] == jnp.arange(experts, dtype=jnp.int32)).astype(F32)


def gate_forward(logits, onehot):
    chosen = jnp.sum(logits[:, None, :] * onehot, axis=-1)
    return jax.nn.softmax(chosen, axis=-1)


def gate_backward(gate_probs, grad_gates, onehot):
    centered = gate_probs * (grad_gates - jnp.sum(gate_probs * grad_gates, axis=-1, keepdims=True))
    return jnp.sum(centered[..., None] * onehot, axis=1)


def slot_columns(routes, experts, capacity):
    flat_routes = routes.reshape(-1)
    onehot = (flat_routes[:, None] == jnp.arange(experts, dtype=jnp.int32)[None, :]).astype(
        jnp.int32
    )
    slot_rank = jnp.sum((jnp.cumsum(onehot, axis=0) - 1) * onehot, axis=1)
    return (flat_routes * capacity + slot_rank).reshape(routes.shape)


def dot_f32(left, right):
    return jnp.dot(left, right, preferred_element_type=F32)


def after(value, *others):
    return lax.optimization_barrier((value,) + others)[0]


def shift_planes(value, amount):
    planes = lax.axis_size("expert")
    return lax.ppermute(value, "expert", [(i, (i + amount) % planes) for i in range(planes)])


def exchange_planes(blocks, direction):
    arrived = [blocks[0]]
    for c in range(1, blocks.shape[0]):
        arrived.append(shift_planes(blocks[c], direction * c))
    return jnp.stack(arrived, axis=0)


def gather_planes(value, me, holds):
    planes = lax.axis_size("expert")
    right, left = value, value
    rights, lefts = [], []
    for d in range(1, planes):
        if d - 1 in holds:
            right, left = after(right, *holds[d - 1]), after(left, *holds[d - 1])
        right = lax.ppermute(right, "expert", [(i, i + 1) for i in range(d - 1, planes - 1)])
        left = lax.ppermute(left, "expert", [(i + 1, i) for i in range(0, planes - d)])
        rights.append(right)
        lefts.append(left)
    gathered = [value]
    for c in range(1, planes):
        gathered.append(jnp.where(me + c < planes, lefts[c - 1], rights[planes - c - 1]))
    return gathered


def reduce_planes(parts, holds):
    planes = len(parts)
    right, left = None, None
    for t in range(1, planes):
        send_right, send_left = parts[planes - t], parts[t]
        if right is not None:
            send_right = (send_right.astype(F32) + right.astype(F32)).astype(BF16)
            send_left = (send_left.astype(F32) + left.astype(F32)).astype(BF16)
        if t in holds:
            send_right, send_left = after(send_right, *holds[t]), after(send_left, *holds[t])
        right = lax.ppermute(send_right, "expert", [(i, i + 1) for i in range(0, t)])
        left = lax.ppermute(
            send_left, "expert", [(i, i - 1) for i in range(planes - t, planes)]
        )
    return parts[0].astype(F32) + right.astype(F32) + left.astype(F32)


def swap_dp(value, mask):
    size = lax.axis_size("dp")
    return lax.ppermute(value, "dp", [(i, i ^ mask) for i in range(size)])


def all_sum(value, axis):
    size = lax.axis_size(axis)
    mask = 1
    while mask < size:
        value = value + lax.ppermute(value, axis, [(i, i ^ mask) for i in range(size)])
        mask *= 2
    return value


def reduce_rows(left, matmul, me):
    size = lax.axis_size("dp")
    blocks = left.reshape(size // 2, 2, left.shape[0] // size, left.shape[1])
    core, chip = me % 2, me // 2

    def half(index):
        rows = lax.dynamic_index_in_dim(blocks, index, axis=1, keepdims=False)
        return matmul(rows.reshape(-1, left.shape[1])).reshape(size // 2, blocks.shape[2], -1)

    arrived = swap_dp(half(1 - core).astype(BF16), 1)
    mine = half(core) + arrived.astype(F32)
    low = mine.astype(BF16)
    total = lax.dynamic_index_in_dim(low, chip, axis=0, keepdims=False).astype(F32)
    for other in range(1, size // 2):
        send = lax.dynamic_index_in_dim(low, chip ^ other, axis=0, keepdims=False)
        total = total + swap_dp(send, 2 * other).astype(F32)
    return total


def from_plane_order(relative, plane):
    planes = relative.shape[0]
    return lax.dynamic_slice_in_dim(
        jnp.concatenate([relative, relative], axis=0), (planes - plane) % planes, planes, axis=0
    )


def per_device(
    tokens,
    segment_ids,
    attn_routes,
    mlp_routes,
    cotangent,
    attn_gain,
    kv_weights,
    attn_router,
    query_maps,
    output_maps,
    mlp_gain,
    mlp_router,
    gate_up,
    down_maps,
):
    micro_count, seq_count, local_len, width = tokens.shape
    units = micro_count * seq_count
    length = segment_ids.shape[2]
    experts = attn_router.shape[1]
    dp = lax.axis_size("dp")
    planes = lax.axis_size("expert")
    capacity = 2 * local_len // experts
    slots = experts * capacity
    head_cols = width // dp
    heads = head_cols // HEAD_WIDTH
    plane = lax.axis_index("expert")
    my_dp = lax.axis_index("dp")

    tokens = tokens.reshape(units, local_len, width)
    cotangent = cotangent.reshape(units, local_len, width)
    segments = segment_ids.reshape(units, length)
    attn_routes = attn_routes.reshape(units, local_len, 2)
    mlp_routes = mlp_routes.reshape(units, local_len, 2)

    slot_ids = jnp.arange(slots, dtype=jnp.int32)
    hits_list, tables, other_list = [], [], []
    for u in range(units):
        columns = slot_columns((mlp_routes[u] - plane) % experts, experts, capacity)
        hits = (columns[None] == slot_ids[:, None, None]).astype(F32)
        hits_list.append(hits)
        tables.append(jnp.sum(hits, axis=2).astype(BF16))
        other_list.append(jnp.sum(hits * mlp_routes[u][None, :, ::-1].astype(F32), axis=(1, 2)))

    def send_slots(slot_rows):
        moved = exchange_planes(slot_rows.reshape(planes, capacity, width), 1)
        return moved.reshape(slots, width)

    def gather_rows(moved):
        return lax.all_gather(moved, "dp", axis=0, tiled=True)

    def to_home(rows):
        return exchange_planes(rows.reshape(planes, capacity, -1), -1).reshape(slots, -1)

    kv_rows = kv_weights.shape[0]
    query_rows = query_maps.shape[1]
    packed = jnp.concatenate(
        [query_maps[0], kv_weights.transpose(1, 0, 2).reshape(2 * kv_rows, width)], axis=0
    )
    packed = packed.reshape(-1, dp, head_cols).transpose(1, 0, 2)
    packed = lax.all_to_all(packed, "dp", split_axis=0, concat_axis=0, tiled=True)
    cot_moved = [send_slots(dot_f32(tables[u], cotangent[u]).astype(BF16)) for u in range(units)]

    params = jnp.concatenate(
        [attn_gain[:, None], mlp_gain[:, None], attn_router, mlp_router], axis=1
    ).reshape(-1)
    param_count = params.shape[0]
    routes_count = 2 * local_len
    x_alls, infos = [], []
    for u in range(units):
        info = jnp.concatenate([attn_routes[u].astype(F32).reshape(-1), other_list[u]]).astype(BF16)
        info = jnp.concatenate([info, params])
        info = jnp.pad(info, (0, 16 * width - info.shape[0])).reshape(16, width)
        extended = jnp.concatenate([tokens[u], info], axis=0)
        gathered = lax.all_gather(extended, "dp", axis=0)
        x_alls.append(gathered[:, :local_len].reshape(length, width))
        infos.append(gathered[:, local_len])
    cot_rows_list = [gather_rows(part) for part in cot_moved]
    others = jnp.stack([i[:, routes_count : routes_count + slots] for i in infos], axis=0)
    others = others.reshape(units * dp, experts, capacity).transpose(1, 0, 2)
    others = exchange_planes(others, 1)
    other_rows = (
        others.reshape(planes, units, dp, capacity)
        .transpose(1, 2, 0, 3)
        .reshape(units, dp * slots)
        .astype(jnp.int32)
    )
    params = infos[0][:, routes_count + slots : routes_count + slots + param_count]
    params = [params] + [shift_planes(params, -c) for c in range(1, planes)]
    params = from_plane_order(jnp.stack(params, axis=0), plane)
    params = params.transpose(1, 0, 2).reshape(width, 2 + 2 * experts)
    gain_one = params[:, 0].astype(F32)
    gain_two = params[:, 1].astype(F32)
    router_one_low = params[:, 2 : 2 + experts]
    router_two_low = params[:, 2 + experts :]
    router_one = router_one_low.astype(F32)
    router_two = router_two_low.astype(F32)
    router_wide = jnp.pad(router_two_low, ((0, 0), (0, 128 - experts)))

    hidden_units = down_maps.shape[1]
    padding = ((0, -hidden_units % 128), (0, 0))
    gate_up_local = jnp.concatenate(
        [jnp.pad(gate_up[0, :, 0], padding), jnp.pad(gate_up[0, :, 1], padding)], axis=0
    )
    down_local = jnp.pad(down_maps[0], padding)
    hidden_padded = down_local.shape[0]
    place = plane.astype(jnp.int32)[None]

    cosine, sine_table = rope_tables(jnp.arange(length, dtype=jnp.int32), HEAD_WIDTH // 2)
    cosine = jnp.concatenate([cosine, cosine], axis=1)
    sine_table = jnp.concatenate([-sine_table, sine_table], axis=1)

    mixed_parts = []
    input_parts = []
    gain_one_sum = jnp.zeros((width,), F32)
    gain_two_sum = jnp.zeros((width,), F32)
    each = range(units)

    inputs, a_home, inverse_one, a_all, routes_here, gates_all, kept, gated, states = (
        [], [], [], [], [], [], [], [], []
    )
    for u in each:
        inputs.append(tokens[u].astype(F32))
        normed, inverse = norm_forward(inputs[u], gain_one)
        a_home.append(normed.astype(BF16))
        inverse_one.append(inverse)
        a_all.append(norm_forward(x_alls[u].astype(F32), gain_one)[0].astype(BF16))

    packed = gather_planes(packed, plane, {1: tuple(cot_moved), 2: tuple(a_all)})
    query_cols = [p[:, :query_rows].reshape(width, head_cols) for p in packed]
    kv_cols = from_plane_order(jnp.stack([p[:, query_rows:] for p in packed], axis=0), plane)
    kv_cols = kv_cols.transpose(1, 0, 2, 3)
    key_cols = kv_cols[:, :, :kv_rows].reshape(width, head_cols)
    value_cols = kv_cols[:, :, kv_rows:].reshape(width, head_cols)
    for u in each:
        routes_all = infos[u][:, :routes_count].reshape(length, 2).astype(jnp.int32)
        routes_here.append((routes_all - plane) % experts)
        gates_all.append(
            gate_forward(dot_f32(a_all[u], router_one_low), route_onehot(routes_all, experts))
        )
        a_now = after(a_all[u], *gated)
        raws = [dot_f32(a_now, cols).astype(BF16) for cols in query_cols]
        keys = dot_f32(a_now, key_cols)
        values = dot_f32(a_now, value_cols).astype(BF16)
        *saved, context_gated = attn_forward(
            routes_here[u], gates_all[u], segments[u], cosine, sine_table, raws, keys, values
        )
        kept.append(saved)
        gated.append(context_gated)
    output_list = after(output_maps[0], packed[1], packed[-1])
    output_list = gather_planes(output_list, plane, {1: (gated[0], cot_rows_list[0]), 2: (gated[-1], cot_rows_list[-1])})
    output_rows = jnp.concatenate(output_list, axis=0)
    for u in each:
        states.append(
            inputs[u] + reduce_rows(gated[u], lambda rows: dot_f32(rows, output_rows), my_dp)
        )

    b_home, inverse_two, onehot_mlp, gates_mlp, moved = [], [], [], [], []
    for u in each:
        normed, inverse = norm_forward(states[u], gain_two)
        b_home.append(normed.astype(BF16))
        inverse_two.append(inverse)
        onehot_mlp.append(route_onehot(mlp_routes[u], experts))
        gates_mlp.append(gate_forward(dot_f32(b_home[u], router_two_low), onehot_mlp[u]))
        moved.append(send_slots(dot_f32(tables[u], b_home[u]).astype(BF16)))
    b_rows_list, hid_list, dhid_list, out_parts, grad_b_rows = [], [], [], [], []
    for u in each:
        b_rows_list.append(gather_rows(moved[u]))
        b_rows = b_rows_list[u]
        b_rows = after(b_rows, *moved[1:], *out_parts)
        out_part, grad_part, hidden, dhidden = mlp_experts(
            place,
            b_rows,
            cot_rows_list[u],
            other_rows[u][:, None],
            router_wide,
            gate_up_local,
            down_local,
            dp,
        )
        hid_list.append(hidden)
        dhid_list.append(dhidden)
        out_parts.append(out_part)
        grad_b_rows.append(lax.psum_scatter(grad_part, "dp", scatter_dimension=0, tiled=True))

    dlm_list, grad_states, dh_list = [], [], []
    down_grad, both_grad, last = 0.0, 0.0, out_parts[-1]
    for u in each:
        down_grad = down_grad + jnp.einsum(
            "rf,rd->fd", after(hid_list[u], last), cot_rows_list[u], preferred_element_type=F32
        )
        both_grad = both_grad + jnp.einsum(
            "rf,rd->fd", after(dhid_list[u], down_grad), b_rows_list[u], preferred_element_type=F32
        )
        grad_b_slots = after(to_home(after(grad_b_rows[u], *grad_states)), both_grad)
        hits = hits_list[u]
        cot = cotangent[u]
        dgm_slots = grad_b_slots[:, width].astype(F32)
        grad_b_slots = grad_b_slots[:, :width]
        dlm = gate_backward(
            gates_mlp[u], jnp.sum(hits * dgm_slots[:, None, None], axis=0), onehot_mlp[u]
        )
        dlm_list.append(dlm)
        grad_b = jnp.einsum(
            "st,sd->td", tables[u], grad_b_slots, preferred_element_type=F32
        ) + jnp.einsum("re,de->rd", dlm, router_two, precision=PRECISION_TOP)
        grad_state, gain_two_term = norm_backward(states[u], inverse_two[u], gain_two, grad_b)
        gain_two_sum = gain_two_sum + gain_two_term
        grad_states.append(cot.astype(F32) + grad_state)
        last = grad_states[u]
        dh_list.append(lax.all_gather(grad_states[u].astype(BF16), "dp", axis=0, tiled=True))

    qkv_cols = jnp.concatenate(
        [after(cols, *moved) for cols in query_cols + [key_cols, value_cols]], axis=1
    )
    qkv_cols = jnp.concatenate(
        [
            jnp.pad(qkv_cols, ((0, 0), (0, 128))),
            jnp.pad(jnp.eye(128, dtype=BF16), ((0, 0), (qkv_cols.shape[1], 0))),
        ],
        axis=0,
    )
    g_list, dla_list, output_part = [], [], 0.0
    for u in each:
        dh_now = after(dh_list[u], *(g_list[-1:] or grad_states[-1:]))
        output_part = output_part + jnp.einsum(
            "tc,td->cd", gated[u], dh_now, preferred_element_type=F32
        )
        grad_context = jnp.einsum("td,cd->tc", dh_now, output_rows, preferred_element_type=F32)
        if u == units - 1:
            output_part = output_part.astype(BF16)
            grad_context = after(grad_context, output_part)
        grad_qkv = attn_backward(
            routes_here[u],
            gates_all[u],
            segments[u],
            cosine,
            sine_table,
            *kept[u],
            grad_context,
        )
        g_list.append(grad_qkv)
        grad_a = reduce_rows(
            grad_qkv,
            lambda rows: jnp.einsum("tc,dc->td", rows, qkv_cols, preferred_element_type=F32),
            my_dp,
        )
        dga = grad_a[:, width : width + 2]
        grad_a = grad_a[:, :width]
        gates_home = lax.dynamic_slice_in_dim(gates_all[u], my_dp * local_len, local_len, axis=0)
        dla = gate_backward(gates_home, dga, route_onehot(attn_routes[u], experts))
        dla_list.append(dla)
        grad_a = grad_a + jnp.einsum("re,de->rd", dla, router_one, precision=PRECISION_TOP)
        grad_inputs, gain_one_term = norm_backward(inputs[u], inverse_one[u], gain_one, grad_a)
        gain_one_sum = gain_one_sum + gain_one_term
        input_parts.append(grad_states[u] + grad_inputs)

    both_grad = after(both_grad, g_list[-1])
    gate_up_grad = jnp.stack(
        [both_grad[:hidden_units], both_grad[hidden_padded : hidden_padded + hidden_units]], axis=1
    )
    def cols_grad(c):
        total = 0.0
        for u in each:
            piece = g_list[u][:, c * head_cols : (c + 1) * head_cols]
            total = total + jnp.einsum("td,tc->dc", a_all[u], piece, preferred_element_type=F32)
        return total.astype(BF16)

    query_parts = [cols_grad(c).reshape(dp, query_rows, head_cols) for c in range(planes)]
    kv_part = jnp.concatenate(
        [cols_grad(experts + i).reshape(dp, planes, kv_rows, head_cols) for i in range(2)], axis=2
    )
    kv_parts = [
        lax.dynamic_index_in_dim(kv_part, (plane + c) % planes, axis=1, keepdims=False)
        for c in range(planes)
    ]
    for u in each:
        out_part = after(out_parts[u], output_part)
        out_rows = lax.psum_scatter(out_part, "dp", scatter_dimension=0, tiled=True)
        out_slots = to_home(out_rows)
        gated_table = jnp.sum(hits_list[u] * gates_mlp[u][None], axis=2).T
        gated_high = gated_table.astype(BF16)
        gated_low = (gated_table - gated_high.astype(F32)).astype(BF16)
        mlp_sum = dot_f32(gated_high, out_slots) + dot_f32(gated_low, out_slots)
        mixed_parts.append((states[u] + mlp_sum).astype(BF16))

    output_grad = lax.psum_scatter(
        from_plane_order(output_part.reshape(planes, head_cols, width), plane),
        "expert",
        scatter_dimension=0,
        tiled=False,
    ).astype(F32)

    def to_rows(grads):
        grads = lax.all_to_all(grads.astype(BF16), "dp", split_axis=0, concat_axis=0, tiled=True)
        return grads.transpose(1, 0, 2).reshape(-1, width).astype(F32)

    query_grad = reduce_planes(query_parts, {3: (gate_up_grad, mixed_parts[0])})
    kv_grad = reduce_planes(kv_parts, {1: (query_grad,), 3: (mixed_parts[-1],)})
    query_grad = to_rows(query_grad)
    kv_grad = to_rows(kv_grad)
    kv_grad = kv_grad.reshape(2, kv_rows, width).transpose(1, 0, 2)

    down_grad = down_grad[:hidden_units]
    router_one_grad = jnp.einsum(
        "re,rd->ed",
        jnp.concatenate(dla_list, axis=0),
        jnp.concatenate(a_home, axis=0).astype(F32),
        precision=PRECISION_TOP,
    )
    router_two_grad = jnp.einsum(
        "re,rd->ed",
        jnp.concatenate(dlm_list, axis=0),
        jnp.concatenate(b_home, axis=0).astype(F32),
        precision=PRECISION_TOP,
    )
    small_grad = jnp.concatenate(
        [gain_one_sum[None], gain_two_sum[None], router_one_grad, router_two_grad], axis=0
    )
    small_grad = all_sum(all_sum(small_grad, "dp"), "expert")
    small_grad = lax.dynamic_index_in_dim(
        small_grad.reshape(-1, dp * planes, kv_rows), my_dp * planes + plane, axis=1, keepdims=False
    )

    shape = (micro_count, seq_count, local_len, width)
    return (
        jnp.stack(mixed_parts, axis=0).reshape(shape),
        jnp.stack(input_parts, axis=0).reshape(shape),
        small_grad[0],
        kv_grad,
        small_grad[2 : 2 + experts].T,
        query_grad[None],
        output_grad[None],
        small_grad[1],
        small_grad[2 + experts :].T,
        gate_up_grad[None],
        down_grad[None],
    )


def solution(mesh):
    in_specs = (
        P(None, "expert", "dp", None),
        P(None, "expert", None),
        P(None, "expert", "dp", None),
        P(None, "expert", "dp", None),
        P(None, "expert", "dp", None),
        P(("dp", "expert")),
        P(("dp", "expert"), None, None),
        P(("dp", "expert"), None),
        P("expert", "dp", None),
        P("expert", "dp", None),
        P(("dp", "expert")),
        P(("dp", "expert"), None),
        P("expert", "dp", None, None),
        P("expert", "dp", None),
    )
    out_specs = (
        P(None, "expert", "dp", None),
        P(None, "expert", "dp", None),
        P(("dp", "expert")),
        P(("dp", "expert"), None, None),
        P(("dp", "expert"), None),
        P("expert", "dp", None),
        P("expert", "dp", None),
        P(("dp", "expert")),
        P(("dp", "expert"), None),
        P("expert", "dp", None, None),
        P("expert", "dp", None),
    )
    return jax.shard_map(
        per_device, mesh=mesh, in_specs=in_specs, out_specs=out_specs, check_vma=False
    )
```

```python
import functools

import jax
import jax.numpy as jnp
from jax import lax
from jax.experimental import pallas as pl
from jax.experimental.pallas import tpu as pltpu
from jax.sharding import PartitionSpec as P

HEAD_WIDTH = 128


EPSILON = 1e-05
THETA_BASE = 10000.0
NEGATIVE = -1000000000.0
PRECISION_TOP = lax.Precision.HIGHEST
BF16 = jnp.bfloat16
F32 = jnp.float32


def rope_in(values, cosine, sine_signed):
    return values * cosine + pltpu.roll(values, HEAD_WIDTH // 2, 1) * sine_signed


def contract(left, right, left_dim, right_dim):
    return lax.dot_general(
        left, right, (((left_dim,), (right_dim,)), ((), ())), preferred_element_type=F32
    )


def block_mask(seg_col_ref, seg_row_ref, i, block):
    n = (i + 1) * block
    rows = slice(i * block, n)
    return (
        lax.broadcasted_iota(jnp.int32, (n, block), 0)
        <= lax.broadcasted_iota(jnp.int32, (n, block), 1) + i * block
    ) & (seg_col_ref[:n, :] == seg_row_ref[:, rows])


def key_softmax(score):
    exponent = jnp.exp(score - jnp.max(score, axis=0, keepdims=True))
    return exponent * (1.0 / jnp.sum(exponent, axis=0, keepdims=True))


def attn_forward_kernel(*refs, experts, heads, block, scale):
    routes_ref, gates_ref, seg_col_ref, seg_row_ref, cos_ref, sin_ref, keys_ref, values_ref = refs[:8]
    raw_refs = refs[8 : 8 + experts]
    q_ref, k_ref, v_ref, o_ref, gated_ref = refs[8 + experts :]
    length = cos_ref.shape[0]
    width = HEAD_WIDTH
    cosine = cos_ref[...]
    sine = sin_ref[...]
    routes = [routes_ref[:, c : c + 1] for c in range(2)]
    for h in range(heads):
        cols = slice(h * width, (h + 1) * width)
        k_ref[h] = rope_in(keys_ref[:, cols], cosine, sine).astype(BF16)
        v_ref[h] = values_ref[:, cols]
        for choice in range(2):
            raw = raw_refs[0][:, cols].astype(F32)
            for e in range(1, experts):
                raw = jnp.where(routes[choice] == e, raw_refs[e][:, cols].astype(F32), raw)
            q_ref[h, choice] = rope_in(raw, cosine, sine).astype(BF16)
    for i in range(length // block):
        rows = slice(i * block, (i + 1) * block)
        n = (i + 1) * block
        mask = block_mask(seg_col_ref, seg_row_ref, i, block)
        for h in range(heads):
            for choice in range(2):
                score = contract(k_ref[h, :n], q_ref[h, choice, rows], 1, 1) * scale
                probs = key_softmax(jnp.where(mask, score, NEGATIVE)).astype(BF16)
                o_ref[h, choice, rows] = contract(probs, v_ref[h, :n], 0, 0).astype(BF16)
    for h in range(heads):
        first = o_ref[h, 0].astype(F32) * gates_ref[:, 0:1]
        second = o_ref[h, 1].astype(F32) * gates_ref[:, 1:2]
        for e in range(experts):
            part = jnp.where(routes[0] == e, first, 0.0)
            part = jnp.where(routes[1] == e, second, part)
            at = (e * heads + h) * width
            gated_ref[:, at : at + width] = part.astype(BF16)


def attn_backward_kernel(
    routes_ref, gates_ref, seg_col_ref, seg_row_ref, cos_ref, sin_ref, q_ref, k_ref, v_ref, o_ref, up_ref,
    grad_ref, dctx_ref, dq_ref, dk_ref, dv_ref, *, experts, heads, block, scale,
):
    length = cos_ref.shape[0]
    width = HEAD_WIDTH
    lanes = lax.broadcasted_iota(jnp.int32, (length, width), 1)
    routes = [routes_ref[:, c : c + 1] for c in range(2)]
    dgate = jnp.zeros((length, width), F32)
    for h in range(heads):
        for choice in range(2):
            up = up_ref[:, h * width : (h + 1) * width]
            for e in range(1, experts):
                at = (e * heads + h) * width
                up = jnp.where(routes[choice] == e, up_ref[:, at : at + width], up)
            part = jnp.sum(up * o_ref[h, choice].astype(F32), axis=1, keepdims=True)
            dgate = dgate + jnp.where(lanes == choice, part, 0.0)
            dctx_ref[h, choice] = (up * gates_ref[:, choice : choice + 1]).astype(BF16)
    grad_ref[:, (experts + 2) * heads * width :] = dgate.astype(BF16)
    dk_ref[...] = jnp.zeros_like(dk_ref)
    dv_ref[...] = jnp.zeros_like(dv_ref)
    for i in range(length // block):
        rows = slice(i * block, (i + 1) * block)
        n = (i + 1) * block
        mask = block_mask(seg_col_ref, seg_row_ref, i, block)
        for h in range(heads):
            for choice in range(2):
                query = q_ref[h, choice, rows]
                dctx = dctx_ref[h, choice, rows]
                score = contract(k_ref[h, :n], query, 1, 1) * scale
                probs = key_softmax(jnp.where(mask, score, NEGATIVE))
                dprobs = contract(v_ref[h, :n], dctx, 1, 1)
                dscore = probs * (dprobs - jnp.sum(probs * dprobs, axis=0, keepdims=True))
                dscore = dscore.astype(BF16)
                dv_ref[h, :n] += contract(probs.astype(BF16), dctx, 1, 0)
                dk_ref[h, :n] += contract(dscore, query, 1, 0)
                dq_ref[h, choice, rows] = contract(dscore, k_ref[h, :n], 0, 0)
    cosine = cos_ref[...]
    sine = -sin_ref[...]
    for h in range(heads):
        first = rope_in(dq_ref[h, 0] * scale, cosine, sine)
        second = rope_in(dq_ref[h, 1] * scale, cosine, sine)
        for e in range(experts):
            part = jnp.where(routes[0] == e, first, 0.0)
            part = jnp.where(routes[1] == e, second, part)
            at = (e * heads + h) * width
            grad_ref[:, at : at + width] = part.astype(BF16)
        at = (experts * heads + h) * width
        grad_ref[:, at : at + width] = rope_in(dk_ref[h] * scale, cosine, sine).astype(BF16)
        at = ((experts + 1) * heads + h) * width
        grad_ref[:, at : at + width] = dv_ref[h].astype(BF16)


def attn_forward(routes, gates, segments, cosine, sine, raws, keys, values):
    experts = len(raws)
    length, cols = raws[0].shape
    width = HEAD_WIDTH
    heads = cols // width
    scores = heads * length * length * 2
    return pl.pallas_call(
        functools.partial(
            attn_forward_kernel,
            experts=experts,
            heads=heads,
            block=min(256, length),
            scale=width**-0.5,
        ),
        out_shape=[
            jax.ShapeDtypeStruct((heads, 2, length, width), BF16),
            jax.ShapeDtypeStruct((heads, length, width), BF16),
            jax.ShapeDtypeStruct((heads, length, width), BF16),
            jax.ShapeDtypeStruct((heads, 2, length, width), BF16),
            jax.ShapeDtypeStruct((length, heads * experts * width), BF16),
        ],
        compiler_params=pltpu.CompilerParams(vmem_limit_bytes=48 * 2**20),
        cost_estimate=pl.CostEstimate(
            flops=scores * width * 8, bytes_accessed=12 * 2**20, transcendentals=scores
        ),
    )(routes, gates, segments[:, None], segments[None, :], cosine, sine, keys, values, *raws)


def attn_backward(routes, gates, segments, cosine, sine, q, k, v, o, up):
    heads, _, length, width = q.shape
    experts = up.shape[1] // (heads * width)
    scores = heads * length * length * 2
    return pl.pallas_call(
        functools.partial(
            attn_backward_kernel,
            experts=experts,
            heads=heads,
            block=min(256, length),
            scale=width**-0.5,
        ),
        out_shape=jax.ShapeDtypeStruct((length, (heads * (experts + 2) + 1) * width), BF16),
        scratch_shapes=[
            pltpu.VMEM((heads, 2, length, width), BF16),
            pltpu.VMEM((heads, 2, length, width), F32),
            pltpu.VMEM((heads, length, width), F32),
            pltpu.VMEM((heads, length, width), F32),
        ],
        compiler_params=pltpu.CompilerParams(vmem_limit_bytes=48 * 2**20),
        cost_estimate=pl.CostEstimate(
            flops=scores * width * 20, bytes_accessed=12 * 2**20, transcendentals=scores
        ),
    )(routes, gates, segments[:, None], segments[None, :], cosine, sine, q, k, v, o, up)


def mlp_kernel(
    place_ref, b_ref, cot_ref, other_ref, router_ref, gate_up_ref, down_ref,
    *rest,
):
    out_ref, grad_ref, hidden_ref, dhidden_ref = rest[-4:]
    hidden_units = down_ref.shape[0]
    rows = b_ref[...]
    logits = contract(rows, router_ref[...], 1, 0)
    lanes = lax.broadcasted_iota(jnp.int32, logits.shape, 1)
    own = jnp.sum(jnp.where(lanes == place_ref[0], logits, 0.0), axis=1, keepdims=True)
    other = jnp.sum(jnp.where(lanes == other_ref[...], logits, 0.0), axis=1, keepdims=True)
    gates = jax.nn.sigmoid(own - other)
    both = contract(rows, gate_up_ref[...], 1, 1)
    gate_val = both[:, :hidden_units]
    up_val = both[:, hidden_units:]
    sigmoid = jax.nn.sigmoid(gate_val)
    silu = gate_val * sigmoid
    hidden = silu * up_val
    hidden_low = hidden.astype(BF16)
    hidden_ref[...] = (hidden * gates).astype(BF16)
    grad_plain = contract(cot_ref[...], down_ref[...], 1, 1)
    dgate = jnp.sum(grad_plain * hidden_low.astype(F32), axis=1, keepdims=True)
    width = b_ref.shape[1]
    grad_ref[:, width:] = jnp.broadcast_to(dgate, (dgate.shape[0], grad_ref.shape[1] - width)).astype(BF16)
    grad_hidden = grad_plain * gates
    dhidden_ref[:, :hidden_units] = (
        grad_hidden * up_val * sigmoid * (1.0 + gate_val * (1.0 - sigmoid))
    ).astype(BF16)
    dhidden_ref[:, hidden_units:] = (grad_hidden * silu).astype(BF16)
    out_ref[...] = contract(hidden_low, down_ref[...], 1, 0).astype(BF16)
    grad_ref[:, :width] = contract(dhidden_ref[...], gate_up_ref[...], 1, 0).astype(BF16)


def mlp_experts(place, b_rows, cot_rows, other_rows, router, gate_up, down, blocks, unit, units, outs):
    total, width = b_rows.shape
    hidden_units = down.shape[0]
    block = total // blocks
    by_row = lambda cols: pl.BlockSpec((block, cols), lambda i, place: (i, 0))
    fixed = lambda shape: pl.BlockSpec(shape, lambda i, place: (0, 0), pipeline_mode=pl.Buffered(1))
    return pl.pallas_call(
        mlp_kernel,
        grid_spec=pltpu.PrefetchScalarGridSpec(
            num_scalar_prefetch=1,
            grid=(blocks,),
            in_specs=[
                by_row(width),
                by_row(width),
                by_row(1),
                fixed(router.shape),
                fixed(gate_up.shape),
                fixed(down.shape),
            ]
            + [pl.BlockSpec(memory_space=pl.ANY)] * len(outs),
            out_specs=[
                pl.BlockSpec((block, width), lambda i, place: (i, unit)),
                by_row(width + 128),
                by_row(hidden_units),
                by_row(2 * hidden_units),
            ],
        ),
        out_shape=[
            jax.ShapeDtypeStruct((total, units * width), BF16),
            jax.ShapeDtypeStruct((total, width + 128), BF16),
            jax.ShapeDtypeStruct((total, hidden_units), BF16),
            jax.ShapeDtypeStruct((total, 2 * hidden_units), BF16),
        ],
        compiler_params=pltpu.CompilerParams(vmem_limit_bytes=56 * 2**20),
        cost_estimate=pl.CostEstimate(
            flops=total * width * hidden_units * 12,
            bytes_accessed=4 * total * width * 2 + 6 * total * hidden_units + 6 * width * hidden_units,
            transcendentals=total * hidden_units,
        ),
        input_output_aliases={7: 0} if outs else {},
    )(place, b_rows, cot_rows, other_rows, router, gate_up, down, *outs)


def weave_kernel(first_ref, second_ref, out_ref):
    out_ref[0, :, 0, :] = first_ref[...]
    out_ref[0, :, 1, :] = second_ref[...]


def weave_rows(both, units):
    total, width = both.shape
    block = 32
    half = total // 2 // block
    return pl.pallas_call(
        weave_kernel,
        grid=(units // block,),
        in_specs=[
            pl.BlockSpec((block, width), lambda i: (i, 0)),
            pl.BlockSpec((block, width), lambda i: (i + half, 0)),
        ],
        out_specs=pl.BlockSpec((1, block, 2, width), lambda i: (0, i, 0, 0)),
        out_shape=jax.ShapeDtypeStruct((1, units, 2, width), F32),
        cost_estimate=pl.CostEstimate(
            flops=0, bytes_accessed=16 * units * width, transcendentals=0
        ),
    )(both, both)


def norm_kernel(x_ref, gain_ref, out_ref):
    values = x_ref[0].astype(F32)
    inverse = lax.rsqrt(jnp.mean(values * values, axis=1, keepdims=True) + EPSILON)
    out_ref[...] = (values * inverse * gain_ref[...]).astype(BF16)


def norm_sequence(gathered, unit, gain, rows):
    blocks, _, width = gathered.shape
    return pl.pallas_call(
        norm_kernel,
        grid=(blocks,),
        in_specs=[
            pl.BlockSpec((1, rows, width), lambda i: (i, unit, 0)),
            pl.BlockSpec((1, width), lambda i: (0, 0)),
        ],
        out_specs=pl.BlockSpec((rows, width), lambda i: (i, 0)),
        out_shape=jax.ShapeDtypeStruct((blocks * rows, width), BF16),
        cost_estimate=pl.CostEstimate(
            flops=blocks * rows * width * 6, bytes_accessed=blocks * rows * width * 4, transcendentals=0
        ),
    )(gathered, gain[None])


def rope_tables(positions, half_dim):
    frequency = THETA_BASE ** (-jnp.arange(half_dim, dtype=F32) / half_dim)
    angles = positions.astype(F32)[:, None] * frequency[None, :]
    return (jnp.cos(angles), jnp.sin(angles))


def norm_forward(values, gain_row):
    inverse = lax.rsqrt(jnp.mean(values * values, axis=-1, keepdims=True) + EPSILON)
    return (values * inverse * gain_row, inverse)


def norm_backward(values, inverse, gain_row, grad_normed):
    scaled = gain_row * grad_normed
    gain_term = jnp.sum(grad_normed * values * inverse, axis=0)
    grad_values = inverse * scaled - values * inverse**3 * jnp.mean(
        scaled * values, axis=-1, keepdims=True
    )
    return (grad_values, gain_term)


def route_onehot(routes, experts):
    return (routes[..., None] == jnp.arange(experts, dtype=jnp.int32)).astype(F32)


def gate_forward(logits, onehot):
    chosen = jnp.sum(logits[:, None, :] * onehot, axis=-1)
    return jax.nn.softmax(chosen, axis=-1)


def gate_backward(gate_probs, grad_gates, onehot):
    centered = gate_probs * (grad_gates - jnp.sum(gate_probs * grad_gates, axis=-1, keepdims=True))
    return jnp.sum(centered[..., None] * onehot, axis=1)


def slot_columns(routes, experts, capacity):
    flat_routes = routes.reshape(-1)
    onehot = (flat_routes[:, None] == jnp.arange(experts, dtype=jnp.int32)[None, :]).astype(
        jnp.int32
    )
    slot_rank = jnp.sum((jnp.cumsum(onehot, axis=0) - 1) * onehot, axis=1)
    return (flat_routes * capacity + slot_rank).reshape(routes.shape)


def dot_f32(left, right):
    return jnp.dot(left, right, preferred_element_type=F32)


def after(value, *others):
    return lax.optimization_barrier((value,) + others)[0]


def shift_planes(value, amount):
    planes = lax.axis_size("expert")
    return lax.ppermute(value, "expert", [(i, (i + amount) % planes) for i in range(planes)])


def exchange_planes(blocks, direction):
    arrived = [blocks[0]]
    for c in range(1, blocks.shape[0]):
        arrived.append(shift_planes(blocks[c], direction * c))
    return jnp.stack(arrived, axis=0)


def gather_planes(value, me, holds):
    planes = lax.axis_size("expert")
    right, left = value, value
    rights, lefts = [], []
    for d in range(1, planes):
        if d - 1 in holds:
            right, left = after(right, *holds[d - 1]), after(left, *holds[d - 1])
        right = lax.ppermute(right, "expert", [(i, i + 1) for i in range(d - 1, planes - 1)])
        left = lax.ppermute(left, "expert", [(i + 1, i) for i in range(0, planes - d)])
        rights.append(right)
        lefts.append(left)
    gathered = [value]
    for c in range(1, planes):
        gathered.append(jnp.where(me + c < planes, lefts[c - 1], rights[planes - c - 1]))
    return gathered


def reduce_planes(parts, holds):
    planes = len(parts)
    right, left = None, None
    for t in range(1, planes):
        send_right, send_left = parts[planes - t], parts[t]
        if right is not None:
            send_right = (send_right.astype(F32) + right.astype(F32)).astype(BF16)
            send_left = (send_left.astype(F32) + left.astype(F32)).astype(BF16)
        if t in holds:
            send_right, send_left = after(send_right, *holds[t]), after(send_left, *holds[t])
        right = lax.ppermute(send_right, "expert", [(i, i + 1) for i in range(0, t)])
        left = lax.ppermute(
            send_left, "expert", [(i, i - 1) for i in range(planes - t, planes)]
        )
    return parts[0].astype(F32) + right.astype(F32) + left.astype(F32)


def swap_dp(value, mask):
    size = lax.axis_size("dp")
    return lax.ppermute(value, "dp", [(i, i ^ mask) for i in range(size)])


def all_sum(value, axis):
    size = lax.axis_size(axis)
    mask = 1
    while mask < size:
        value = value + lax.ppermute(value, axis, [(i, i ^ mask) for i in range(size)])
        mask *= 2
    return value


def reduce_rows(left, matmul, me, hold=None):
    size = lax.axis_size("dp")
    blocks = left.reshape(size // 2, 2, left.shape[0] // size, left.shape[1])
    core, chip = me % 2, me // 2

    def half(index):
        rows = lax.dynamic_index_in_dim(blocks, index, axis=1, keepdims=False)
        return matmul(rows.reshape(-1, left.shape[1])).reshape(size // 2, blocks.shape[2], -1)

    arrived = swap_dp(half(1 - core).astype(BF16), 1)
    mine = half(core) + arrived.astype(F32)
    low = mine.astype(BF16)
    total = lax.dynamic_index_in_dim(low, chip, axis=0, keepdims=False)
    total = (total if hold is None else after(total, hold)).astype(F32)
    for other in range(1, size // 2):
        send = lax.dynamic_index_in_dim(low, chip ^ other, axis=0, keepdims=False)
        total = total + swap_dp(send, 2 * other).astype(F32)
    return total, low


def from_plane_order(relative, plane):
    planes = relative.shape[0]
    return lax.dynamic_slice_in_dim(
        jnp.concatenate([relative, relative], axis=0), (planes - plane) % planes, planes, axis=0
    )


def per_device(
    tokens,
    segment_ids,
    attn_routes,
    mlp_routes,
    cotangent,
    attn_gain,
    kv_weights,
    attn_router,
    query_maps,
    output_maps,
    mlp_gain,
    mlp_router,
    gate_up,
    down_maps,
):
    micro_count, seq_count, local_len, width = tokens.shape
    units = micro_count * seq_count
    length = segment_ids.shape[2]
    experts = attn_router.shape[1]
    dp = lax.axis_size("dp")
    planes = lax.axis_size("expert")
    capacity = 2 * local_len // experts
    slots = experts * capacity
    head_cols = width // dp
    heads = head_cols // HEAD_WIDTH
    plane = lax.axis_index("expert")
    my_dp = lax.axis_index("dp")

    tokens = tokens.reshape(units, local_len, width)
    cotangent = cotangent.reshape(units, local_len, width)
    segments = segment_ids.reshape(units, length)
    attn_routes = attn_routes.reshape(units, local_len, 2)
    mlp_routes = mlp_routes.reshape(units, local_len, 2)

    slot_ids = jnp.arange(slots, dtype=jnp.int32)
    hits_list, tables, other_list = [], [], []
    for u in range(units):
        columns = slot_columns((mlp_routes[u] - plane) % experts, experts, capacity)
        hits = (columns[None] == slot_ids[:, None, None]).astype(F32)
        hits_list.append(hits)
        tables.append(jnp.sum(hits, axis=2).astype(BF16))
        other_list.append(jnp.sum(hits * mlp_routes[u][None, :, ::-1].astype(F32), axis=(1, 2)))

    def send_slots(slot_rows):
        moved = exchange_planes(slot_rows.reshape(planes, capacity, width), 1)
        return moved.reshape(slots, width)

    def gather_rows(moved):
        return lax.all_gather(moved, "dp", axis=0, tiled=True)

    def to_home(rows):
        return exchange_planes(rows.reshape(planes, capacity, -1), -1).reshape(slots, -1)

    kv_rows = kv_weights.shape[0]
    query_rows = query_maps.shape[1]
    packed = jnp.concatenate(
        [query_maps[0], kv_weights.transpose(1, 0, 2).reshape(2 * kv_rows, width)], axis=0
    )
    params = jnp.concatenate([attn_gain, mlp_gain, attn_router.reshape(-1), mlp_router.reshape(-1)])
    sizes = [units * local_len * 2, units * slots, params.shape[0]]
    info = jnp.concatenate(
        [attn_routes.astype(BF16).reshape(-1)] + [o.astype(BF16) for o in other_list] + [params]
    )
    info = jnp.pad(info, (0, -info.shape[0] % (16 * head_cols))).reshape(1, -1, head_cols)
    packed = packed.reshape(-1, dp, head_cols).transpose(1, 0, 2)
    weight_rows = packed.shape[1]
    packed = jnp.concatenate([packed, jnp.broadcast_to(info, (dp,) + info.shape[1:])], axis=1)
    packed = lax.all_to_all(packed, "dp", split_axis=0, concat_axis=0, tiled=True)
    info = packed[:, weight_rows:].reshape(dp, -1)
    cot_moved = [send_slots(dot_f32(tables[u], cotangent[u]).astype(BF16)) for u in range(units)]
    cot_rows_list = [gather_rows(part) for part in cot_moved]

    x_all = lax.all_gather(tokens.reshape(units * local_len, width), "dp", axis=0)

    routes_info = info[:, : sizes[0]].reshape(dp, units, local_len, 2).transpose(1, 0, 2, 3)
    routes_info = routes_info.reshape(units, length, 2).astype(jnp.int32)
    others = info[:, sizes[0] : sizes[0] + sizes[1]].reshape(dp, units, experts, capacity)
    others = exchange_planes(others.transpose(2, 1, 0, 3), 1)
    other_rows = others.transpose(1, 2, 0, 3).reshape(units, dp * slots).astype(jnp.int32)
    params = info[:, sizes[0] + sizes[1] : sum(sizes)]
    params = [params] + [shift_planes(params, -c) for c in range(1, planes)]
    params = from_plane_order(jnp.stack(params, axis=0), plane)

    def param(start, each):
        part = params[:, :, start : start + kv_rows * each]
        return part.reshape(planes, dp, kv_rows, each).transpose(1, 0, 2, 3).reshape(width, each)

    gain_one = param(0, 1).reshape(-1).astype(F32)
    gain_two = param(kv_rows, 1).reshape(-1).astype(F32)
    router_one_low = param(2 * kv_rows, experts)
    router_two_low = param((2 + experts) * kv_rows, experts)
    router_one = router_one_low.astype(F32)
    router_two = router_two_low.astype(F32)
    router_wide = jnp.pad(router_two_low, ((0, 0), (0, 128 - experts)))

    hidden_units = down_maps.shape[1]
    padding = ((0, -hidden_units % 128), (0, 0))
    gate_up_local = jnp.concatenate(
        [jnp.pad(gate_up[0, :, 0], padding), jnp.pad(gate_up[0, :, 1], padding)], axis=0
    )
    down_local = jnp.pad(down_maps[0], padding)
    hidden_padded = down_local.shape[0]
    place = plane.astype(jnp.int32)[None]

    cosine, sine_table = rope_tables(jnp.arange(length, dtype=jnp.int32), HEAD_WIDTH // 2)
    cosine = jnp.concatenate([cosine, cosine], axis=1)
    sine_table = jnp.concatenate([-sine_table, sine_table], axis=1)

    mixed_parts = []
    input_parts = []
    gain_one_sum = jnp.zeros((width,), F32)
    gain_two_sum = jnp.zeros((width,), F32)
    each = range(units)

    inputs, a_home, inverse_one, a_all, routes_here, gates_all, kept, gated, states = (
        [], [], [], [], [], [], [], [], []
    )
    for u in each:
        inputs.append(tokens[u].astype(F32))
        normed, inverse = norm_forward(inputs[u], gain_one)
        a_home.append(normed.astype(BF16))
        inverse_one.append(inverse)
        a_all.append(norm_sequence(x_all, u, gain_one, local_len))
        gates_all.append(
            gate_forward(dot_f32(a_all[u], router_one_low), route_onehot(routes_info[u], experts))
        )

    packed = gather_planes(packed, plane, {1: tuple(cot_moved + a_all), 2: tuple(gates_all)})
    query_cols = [p[:, :query_rows].reshape(width, head_cols) for p in packed]
    kv_cols = from_plane_order(jnp.stack([p[:, query_rows:weight_rows] for p in packed], axis=0), plane)
    kv_cols = kv_cols.transpose(1, 0, 2, 3)
    key_cols = kv_cols[:, :, :kv_rows].reshape(width, head_cols)
    value_cols = kv_cols[:, :, kv_rows:].reshape(width, head_cols)
    for u in each:
        routes_here.append((routes_info[u] - plane) % experts)
        a_now = after(a_all[u], *gated)
        raws = [dot_f32(a_now, cols).astype(BF16) for cols in query_cols]
        keys = dot_f32(a_now, key_cols)
        values = dot_f32(a_now, value_cols).astype(BF16)
        *saved, context_gated = attn_forward(
            routes_here[u], gates_all[u], segments[u], cosine, sine_table, raws, keys, values
        )
        kept.append(saved)
        gated.append(context_gated)
    output_list = after(output_maps[0], packed[1], packed[-1])
    output_list = gather_planes(output_list, plane, {1: (gated[0], cot_rows_list[0]), 2: (gated[-1], cot_rows_list[-1])})
    output_rows = jnp.concatenate(output_list, axis=0)
    b_home, inverse_two, onehot_mlp, gates_mlp, moved, sent = [], [], [], [], [], []
    for u in each:
        gated_now = after(gated[u], *sent)
        attn_sum, low = reduce_rows(
            gated_now, lambda rows: dot_f32(rows, output_rows), my_dp, moved[-1] if moved else None
        )
        sent.append(low)
        states.append(inputs[u] + attn_sum)
        normed, inverse = norm_forward(states[u], gain_two)
        b_home.append(normed.astype(BF16))
        inverse_two.append(inverse)
        onehot_mlp.append(route_onehot(mlp_routes[u], experts))
        gates_mlp.append(gate_forward(dot_f32(b_home[u], router_two_low), onehot_mlp[u]))
        moved.append(send_slots(dot_f32(tables[u], b_home[u]).astype(BF16)))

    b_rows_list, hid_list, dhid_list, grad_b_rows, outs = [], [], [], [], []
    for u in each:
        b_rows_list.append(gather_rows(moved[u]))
        b_rows = b_rows_list[u]
        b_rows = after(b_rows, *moved[1:], *hid_list)
        outs, grad_part, hidden, dhidden = mlp_experts(
            place,
            b_rows,
            cot_rows_list[u],
            other_rows[u][:, None],
            router_wide,
            gate_up_local,
            down_local,
            dp,
            u,
            units,
            outs,
        )
        outs = [outs]
        hid_list.append(hidden)
        dhid_list.append(dhidden)
        grad_b_rows.append(lax.psum_scatter(grad_part, "dp", scatter_dimension=0, tiled=True))

    dlm_list, grad_states, dh_list = [], [], []
    down_grad, both_grad, last = 0.0, 0.0, hid_list[-1]
    for u in each:
        down_grad = down_grad + jnp.einsum(
            "rf,rd->fd",
            after(hid_list[u], last),
            cot_rows_list[u],
            preferred_element_type=F32,
        )
        both_grad = both_grad + jnp.einsum(
            "rf,rd->fd", after(dhid_list[u], down_grad), b_rows_list[u], preferred_element_type=F32
        )
        grad_b_slots = after(to_home(after(grad_b_rows[u], *grad_states)), both_grad, *dh_list)
        hits = hits_list[u]
        cot = cotangent[u]
        dgm_slots = grad_b_slots[:, width].astype(F32)
        grad_b_slots = grad_b_slots[:, :width]
        dlm = gate_backward(
            gates_mlp[u], jnp.sum(hits * dgm_slots[:, None, None], axis=0), onehot_mlp[u]
        )
        dlm_list.append(dlm)
        grad_b = jnp.einsum(
            "st,sd->td", tables[u], grad_b_slots, preferred_element_type=F32
        ) + jnp.einsum("re,de->rd", dlm, router_two, precision=PRECISION_TOP)
        grad_state, gain_two_term = norm_backward(states[u], inverse_two[u], gain_two, grad_b)
        gain_two_sum = gain_two_sum + gain_two_term
        grad_states.append(cot.astype(F32) + grad_state)
        last = grad_states[u]
        dh_list.append(lax.all_gather(grad_states[u].astype(BF16), "dp", axis=0, tiled=True))

    qkv_cols = jnp.concatenate(
        [after(cols, *moved) for cols in query_cols + [key_cols, value_cols]], axis=1
    )
    qkv_cols = jnp.concatenate(
        [
            jnp.pad(qkv_cols, ((0, 0), (0, 128))),
            jnp.pad(jnp.eye(128, dtype=BF16), ((0, 0), (qkv_cols.shape[1], 0))),
        ],
        axis=0,
    )
    g_list = []
    for u in each:
        dh_now = after(dh_list[u], *(g_list[-1:] or grad_states[-1:]))
        grad_context = jnp.einsum("td,cd->tc", dh_now, output_rows, preferred_element_type=F32)
        g_list.append(
            attn_backward(
                routes_here[u],
                gates_all[u],
                segments[u],
                cosine,
                sine_table,
                *kept[u],
                grad_context,
            )
        )

    dla_list = []

    def cols_grad(c, hold):
        total = 0.0
        for u in each:
            piece = lax.dynamic_slice_in_dim(
                after(g_list[u], hold), c * head_cols, head_cols, axis=1
            )
            total = total + jnp.einsum("td,tc->dc", a_all[u], piece, preferred_element_type=F32)
        return total.astype(BF16)

    def finish_inputs(u, hold):
        nonlocal gain_one_sum
        grad_a, low = reduce_rows(
            after(g_list[u], hold),
            lambda rows: jnp.einsum("tc,dc->td", rows, qkv_cols, preferred_element_type=F32),
            my_dp,
        )
        dga = grad_a[:, width : width + 2]
        grad_a = grad_a[:, :width]
        gates_home = lax.dynamic_slice_in_dim(gates_all[u], my_dp * local_len, local_len, axis=0)
        dla = gate_backward(gates_home, dga, route_onehot(attn_routes[u], experts))
        dla_list.append(dla)
        grad_a = grad_a + jnp.einsum("re,de->rd", dla, router_one, precision=PRECISION_TOP)
        grad_inputs, gain_one_term = norm_backward(inputs[u], inverse_one[u], gain_one, grad_a)
        gain_one_sum = gain_one_sum + gain_one_term
        input_parts.append(grad_states[u] + grad_inputs)
        return low

    done = g_list[-1]
    query_parts = []
    for e in range(planes):
        done = cols_grad((e - plane) % planes, done)
        query_parts.append(done.reshape(dp, query_rows, head_cols))
    kv_part = []
    for i in range(2):
        done = cols_grad(experts + i, done)
        kv_part.append(done.reshape(dp, planes, kv_rows, head_cols))
    packed_grad = jnp.concatenate(
        [jnp.stack(query_parts, axis=0)] + [part.transpose(1, 0, 2, 3) for part in kv_part], axis=2
    )
    packed_grad = lax.psum_scatter(packed_grad, "expert", scatter_dimension=0, tiled=False)
    for u in each[:-1]:
        done = finish_inputs(u, done)
    done = finish_inputs(units - 1, done)
    output_part = 0.0
    for u in each:
        output_part = output_part + jnp.einsum(
            "tc,td->cd", after(gated[u], done), dh_list[u], preferred_element_type=F32
        )
    output_part = output_part.astype(BF16)

    both_grad = after(both_grad, output_part)
    gate_up_grad = weave_rows(both_grad, hidden_units)
    down_grad = after(down_grad, output_part)[:hidden_units]

    out_rows = lax.psum_scatter(after(outs[0], dh_list[-1]), "dp", scatter_dimension=0, tiled=True)
    for u in each:
        out_slots = to_home(out_rows[:, u * width : (u + 1) * width])
        gated_table = jnp.sum(hits_list[u] * gates_mlp[u][None], axis=2).T
        gated_high = gated_table.astype(BF16)
        gated_low = (gated_table - gated_high.astype(F32)).astype(BF16)
        mlp_sum = dot_f32(gated_high, out_slots) + dot_f32(gated_low, out_slots)
        mixed_parts.append((states[u] + mlp_sum).astype(BF16))

    output_grad = reduce_planes(
        [output_part[c * head_cols : (c + 1) * head_cols] for c in range(planes)], {}
    )
    packed_grad = lax.all_to_all(packed_grad, "dp", split_axis=0, concat_axis=0, tiled=True)
    packed_grad = packed_grad.transpose(1, 0, 2).reshape(-1, width).astype(F32)
    query_grad = packed_grad[:query_rows]
    kv_grad = packed_grad[query_rows:].reshape(2, kv_rows, width).transpose(1, 0, 2)

    router_one_grad = jnp.einsum(
        "re,rd->ed",
        jnp.concatenate(dla_list, axis=0),
        jnp.concatenate(a_home, axis=0).astype(F32),
        precision=PRECISION_TOP,
    )
    router_two_grad = jnp.einsum(
        "re,rd->ed",
        jnp.concatenate(dlm_list, axis=0),
        jnp.concatenate(b_home, axis=0).astype(F32),
        precision=PRECISION_TOP,
    )
    small_grad = jnp.concatenate(
        [gain_one_sum[None], gain_two_sum[None], router_one_grad, router_two_grad], axis=0
    )
    small_grad = all_sum(all_sum(small_grad, "dp"), "expert")
    small_grad = lax.dynamic_index_in_dim(
        small_grad.reshape(-1, dp * planes, kv_rows), my_dp * planes + plane, axis=1, keepdims=False
    )

    shape = (micro_count, seq_count, local_len, width)
    return (
        jnp.stack(mixed_parts, axis=0).reshape(shape),
        jnp.stack(input_parts, axis=0).reshape(shape),
        small_grad[0],
        kv_grad,
        small_grad[2 : 2 + experts].T,
        query_grad[None],
        output_grad[None],
        small_grad[1],
        small_grad[2 + experts :].T,
        gate_up_grad,
        down_grad[None],
    )


def solution(mesh):
    in_specs = (
        P(None, "expert", "dp", None),
        P(None, "expert", None),
        P(None, "expert", "dp", None),
        P(None, "expert", "dp", None),
        P(None, "expert", "dp", None),
        P(("dp", "expert")),
        P(("dp", "expert"), None, None),
        P(("dp", "expert"), None),
        P("expert", "dp", None),
        P("expert", "dp", None),
        P(("dp", "expert")),
        P(("dp", "expert"), None),
        P("expert", "dp", None, None),
        P("expert", "dp", None),
    )
    out_specs = (
        P(None, "expert", "dp", None),
        P(None, "expert", "dp", None),
        P(("dp", "expert")),
        P(("dp", "expert"), None, None),
        P(("dp", "expert"), None),
        P("expert", "dp", None),
        P("expert", "dp", None),
        P(("dp", "expert")),
        P(("dp", "expert"), None),
        P("expert", "dp", None, None),
        P("expert", "dp", None),
    )
    return jax.shard_map(
        per_device, mesh=mesh, in_specs=in_specs, out_specs=out_specs, check_vma=False
    )
```

```python
import functools

import jax
import jax.numpy as jnp
from jax import lax
from jax.experimental import pallas as pl
from jax.experimental.pallas import tpu as pltpu
from jax.sharding import PartitionSpec as P

HEAD_WIDTH = 128


EPSILON = 1e-05
THETA_BASE = 10000.0
NEGATIVE = -1000000000.0
PRECISION_TOP = lax.Precision.HIGHEST
BF16 = jnp.bfloat16
F32 = jnp.float32


def rope_in(values, cosine, sine_signed):
    return values * cosine + pltpu.roll(values, HEAD_WIDTH // 2, 1) * sine_signed


def contract(left, right, left_dim, right_dim):
    return lax.dot_general(
        left, right, (((left_dim,), (right_dim,)), ((), ())), preferred_element_type=F32
    )


def block_mask(seg_col_ref, seg_row_ref, i, block):
    n = (i + 1) * block
    rows = slice(i * block, n)
    return (
        lax.broadcasted_iota(jnp.int32, (n, block), 0)
        <= lax.broadcasted_iota(jnp.int32, (n, block), 1) + i * block
    ) & (seg_col_ref[:n, :] == seg_row_ref[:, rows])


def key_softmax(score):
    exponent = jnp.exp(score - jnp.max(score, axis=0, keepdims=True))
    return exponent * (1.0 / jnp.sum(exponent, axis=0, keepdims=True))


def attn_forward_kernel(*refs, experts, heads, block, scale):
    routes_ref, gates_ref, seg_col_ref, seg_row_ref, cos_ref, sin_ref, keys_ref, values_ref = refs[:8]
    raw_refs = refs[8 : 8 + experts]
    q_ref, k_ref, v_ref, o_ref, gated_ref = refs[8 + experts :]
    length = cos_ref.shape[0]
    width = HEAD_WIDTH
    cosine = cos_ref[...]
    sine = sin_ref[...]
    routes = [routes_ref[:, c : c + 1] for c in range(2)]
    for h in range(heads):
        cols = slice(h * width, (h + 1) * width)
        k_ref[h] = rope_in(keys_ref[:, cols], cosine, sine).astype(BF16)
        v_ref[h] = values_ref[:, cols]
        for choice in range(2):
            raw = raw_refs[0][:, cols].astype(F32)
            for e in range(1, experts):
                raw = jnp.where(routes[choice] == e, raw_refs[e][:, cols].astype(F32), raw)
            q_ref[h, choice] = rope_in(raw, cosine, sine).astype(BF16)
    for i in range(length // block):
        rows = slice(i * block, (i + 1) * block)
        n = (i + 1) * block
        mask = block_mask(seg_col_ref, seg_row_ref, i, block)
        for h in range(heads):
            for choice in range(2):
                score = contract(k_ref[h, :n], q_ref[h, choice, rows], 1, 1) * scale
                probs = key_softmax(jnp.where(mask, score, NEGATIVE)).astype(BF16)
                o_ref[h, choice, rows] = contract(probs, v_ref[h, :n], 0, 0).astype(BF16)
    for h in range(heads):
        first = o_ref[h, 0].astype(F32) * gates_ref[:, 0:1]
        second = o_ref[h, 1].astype(F32) * gates_ref[:, 1:2]
        for e in range(experts):
            part = jnp.where(routes[0] == e, first, 0.0)
            part = jnp.where(routes[1] == e, second, part)
            at = (e * heads + h) * width
            gated_ref[:, at : at + width] = part.astype(BF16)


def attn_backward_kernel(
    routes_ref, gates_ref, seg_col_ref, seg_row_ref, cos_ref, sin_ref, q_ref, k_ref, v_ref, o_ref, up_ref,
    grad_ref, dctx_ref, dq_ref, dk_ref, dv_ref, *, experts, heads, block, scale,
):
    length = cos_ref.shape[0]
    width = HEAD_WIDTH
    lanes = lax.broadcasted_iota(jnp.int32, (length, width), 1)
    routes = [routes_ref[:, c : c + 1] for c in range(2)]
    dgate = jnp.zeros((length, width), F32)
    for h in range(heads):
        for choice in range(2):
            up = up_ref[:, h * width : (h + 1) * width]
            for e in range(1, experts):
                at = (e * heads + h) * width
                up = jnp.where(routes[choice] == e, up_ref[:, at : at + width], up)
            part = jnp.sum(up * o_ref[h, choice].astype(F32), axis=1, keepdims=True)
            dgate = dgate + jnp.where(lanes == choice, part, 0.0)
            dctx_ref[h, choice] = (up * gates_ref[:, choice : choice + 1]).astype(BF16)
    grad_ref[:, (experts + 2) * heads * width :] = dgate.astype(BF16)
    dk_ref[...] = jnp.zeros_like(dk_ref)
    dv_ref[...] = jnp.zeros_like(dv_ref)
    for i in range(length // block):
        rows = slice(i * block, (i + 1) * block)
        n = (i + 1) * block
        mask = block_mask(seg_col_ref, seg_row_ref, i, block)
        for h in range(heads):
            for choice in range(2):
                query = q_ref[h, choice, rows]
                dctx = dctx_ref[h, choice, rows]
                score = contract(k_ref[h, :n], query, 1, 1) * scale
                probs = key_softmax(jnp.where(mask, score, NEGATIVE))
                dprobs = contract(v_ref[h, :n], dctx, 1, 1)
                dscore = probs * (dprobs - jnp.sum(probs * dprobs, axis=0, keepdims=True))
                dscore = dscore.astype(BF16)
                dv_ref[h, :n] += contract(probs.astype(BF16), dctx, 1, 0)
                dk_ref[h, :n] += contract(dscore, query, 1, 0)
                dq_ref[h, choice, rows] = contract(dscore, k_ref[h, :n], 0, 0)
    cosine = cos_ref[...]
    sine = -sin_ref[...]
    for h in range(heads):
        first = rope_in(dq_ref[h, 0] * scale, cosine, sine)
        second = rope_in(dq_ref[h, 1] * scale, cosine, sine)
        for e in range(experts):
            part = jnp.where(routes[0] == e, first, 0.0)
            part = jnp.where(routes[1] == e, second, part)
            at = (e * heads + h) * width
            grad_ref[:, at : at + width] = part.astype(BF16)
        at = (experts * heads + h) * width
        grad_ref[:, at : at + width] = rope_in(dk_ref[h] * scale, cosine, sine).astype(BF16)
        at = ((experts + 1) * heads + h) * width
        grad_ref[:, at : at + width] = dv_ref[h].astype(BF16)


def attn_forward(routes, gates, segments, cosine, sine, raws, keys, values):
    experts = len(raws)
    length, cols = raws[0].shape
    width = HEAD_WIDTH
    heads = cols // width
    scores = heads * length * length * 2
    return pl.pallas_call(
        functools.partial(
            attn_forward_kernel,
            experts=experts,
            heads=heads,
            block=min(256, length),
            scale=width**-0.5,
        ),
        out_shape=[
            jax.ShapeDtypeStruct((heads, 2, length, width), BF16),
            jax.ShapeDtypeStruct((heads, length, width), BF16),
            jax.ShapeDtypeStruct((heads, length, width), BF16),
            jax.ShapeDtypeStruct((heads, 2, length, width), BF16),
            jax.ShapeDtypeStruct((length, heads * experts * width), BF16),
        ],
        compiler_params=pltpu.CompilerParams(vmem_limit_bytes=48 * 2**20),
        cost_estimate=pl.CostEstimate(
            flops=scores * width * 8, bytes_accessed=12 * 2**20, transcendentals=scores
        ),
    )(routes, gates, segments[:, None], segments[None, :], cosine, sine, keys, values, *raws)


def attn_backward(routes, gates, segments, cosine, sine, q, k, v, o, up):
    heads, _, length, width = q.shape
    experts = up.shape[1] // (heads * width)
    scores = heads * length * length * 2
    return pl.pallas_call(
        functools.partial(
            attn_backward_kernel,
            experts=experts,
            heads=heads,
            block=min(256, length),
            scale=width**-0.5,
        ),
        out_shape=jax.ShapeDtypeStruct((length, (heads * (experts + 2) + 1) * width), BF16),
        scratch_shapes=[
            pltpu.VMEM((heads, 2, length, width), BF16),
            pltpu.VMEM((heads, 2, length, width), F32),
            pltpu.VMEM((heads, length, width), F32),
            pltpu.VMEM((heads, length, width), F32),
        ],
        compiler_params=pltpu.CompilerParams(vmem_limit_bytes=48 * 2**20),
        cost_estimate=pl.CostEstimate(
            flops=scores * width * 20, bytes_accessed=12 * 2**20, transcendentals=scores
        ),
    )(routes, gates, segments[:, None], segments[None, :], cosine, sine, q, k, v, o, up)


def mlp_kernel(
    place_ref, b_ref, cot_ref, other_ref, router_ref, gate_up_ref, down_ref,
    *rest,
):
    out_ref, grad_ref, hidden_ref, dhidden_ref = rest[-4:]
    hidden_units = down_ref.shape[0]
    rows = b_ref[...]
    logits = contract(rows, router_ref[...], 1, 0)
    lanes = lax.broadcasted_iota(jnp.int32, logits.shape, 1)
    own = jnp.sum(jnp.where(lanes == place_ref[0], logits, 0.0), axis=1, keepdims=True)
    other = jnp.sum(jnp.where(lanes == other_ref[...], logits, 0.0), axis=1, keepdims=True)
    gates = jax.nn.sigmoid(own - other)
    both = contract(rows, gate_up_ref[...], 1, 1)
    gate_val = both[:, :hidden_units]
    up_val = both[:, hidden_units:]
    sigmoid = jax.nn.sigmoid(gate_val)
    silu = gate_val * sigmoid
    hidden = silu * up_val
    hidden_low = hidden.astype(BF16)
    hidden_ref[...] = (hidden * gates).astype(BF16)
    grad_plain = contract(cot_ref[...], down_ref[...], 1, 1)
    dgate = jnp.sum(grad_plain * hidden_low.astype(F32), axis=1, keepdims=True)
    width = b_ref.shape[1]
    grad_ref[:, width:] = jnp.broadcast_to(dgate, (dgate.shape[0], grad_ref.shape[1] - width)).astype(BF16)
    grad_hidden = grad_plain * gates
    dhidden_ref[:, :hidden_units] = (
        grad_hidden * up_val * sigmoid * (1.0 + gate_val * (1.0 - sigmoid))
    ).astype(BF16)
    dhidden_ref[:, hidden_units:] = (grad_hidden * silu).astype(BF16)
    out_ref[...] = contract(hidden_low, down_ref[...], 1, 0).astype(BF16)
    grad_ref[:, :width] = contract(dhidden_ref[...], gate_up_ref[...], 1, 0).astype(BF16)


def mlp_experts(place, b_rows, cot_rows, other_rows, router, gate_up, down, blocks, unit, units, outs):
    total, width = b_rows.shape
    hidden_units = down.shape[0]
    block = total // blocks
    by_row = lambda cols: pl.BlockSpec((block, cols), lambda i, place: (i, 0))
    fixed = lambda shape: pl.BlockSpec(shape, lambda i, place: (0, 0), pipeline_mode=pl.Buffered(1))
    return pl.pallas_call(
        mlp_kernel,
        grid_spec=pltpu.PrefetchScalarGridSpec(
            num_scalar_prefetch=1,
            grid=(blocks,),
            in_specs=[
                by_row(width),
                by_row(width),
                by_row(1),
                fixed(router.shape),
                fixed(gate_up.shape),
                fixed(down.shape),
            ]
            + [pl.BlockSpec(memory_space=pl.ANY)] * len(outs),
            out_specs=[
                pl.BlockSpec((block, width), lambda i, place: (i, unit)),
                by_row(width + 128),
                by_row(hidden_units),
                by_row(2 * hidden_units),
            ],
        ),
        out_shape=[
            jax.ShapeDtypeStruct((total, units * width), BF16),
            jax.ShapeDtypeStruct((total, width + 128), BF16),
            jax.ShapeDtypeStruct((total, hidden_units), BF16),
            jax.ShapeDtypeStruct((total, 2 * hidden_units), BF16),
        ],
        compiler_params=pltpu.CompilerParams(vmem_limit_bytes=56 * 2**20),
        cost_estimate=pl.CostEstimate(
            flops=total * width * hidden_units * 12,
            bytes_accessed=4 * total * width * 2 + 6 * total * hidden_units + 6 * width * hidden_units,
            transcendentals=total * hidden_units,
        ),
        input_output_aliases={7: 0} if outs else {},
    )(place, b_rows, cot_rows, other_rows, router, gate_up, down, *outs)


def weave_kernel(first_ref, second_ref, out_ref):
    out_ref[0, :, 0, :] = first_ref[...]
    out_ref[0, :, 1, :] = second_ref[...]


def weave_rows(both, units):
    total, width = both.shape
    block = 32
    half = total // 2 // block
    return pl.pallas_call(
        weave_kernel,
        grid=(units // block,),
        in_specs=[
            pl.BlockSpec((block, width), lambda i: (i, 0)),
            pl.BlockSpec((block, width), lambda i: (i + half, 0)),
        ],
        out_specs=pl.BlockSpec((1, block, 2, width), lambda i: (0, i, 0, 0)),
        out_shape=jax.ShapeDtypeStruct((1, units, 2, width), F32),
        cost_estimate=pl.CostEstimate(
            flops=0, bytes_accessed=16 * units * width, transcendentals=0
        ),
    )(both, both)


def norm_kernel(x_ref, gain_ref, out_ref):
    values = x_ref[0].astype(F32)
    inverse = lax.rsqrt(jnp.mean(values * values, axis=1, keepdims=True) + EPSILON)
    out_ref[...] = (values * inverse * gain_ref[...]).astype(BF16)


def norm_sequence(gathered, unit, gain, rows):
    blocks, _, width = gathered.shape
    return pl.pallas_call(
        norm_kernel,
        grid=(blocks,),
        in_specs=[
            pl.BlockSpec((1, rows, width), lambda i: (i, unit, 0)),
            pl.BlockSpec((1, width), lambda i: (0, 0)),
        ],
        out_specs=pl.BlockSpec((rows, width), lambda i: (i, 0)),
        out_shape=jax.ShapeDtypeStruct((blocks * rows, width), BF16),
        cost_estimate=pl.CostEstimate(
            flops=blocks * rows * width * 6, bytes_accessed=blocks * rows * width * 4, transcendentals=0
        ),
    )(gathered, gain[None])


def rope_tables(positions, half_dim):
    frequency = THETA_BASE ** (-jnp.arange(half_dim, dtype=F32) / half_dim)
    angles = positions.astype(F32)[:, None] * frequency[None, :]
    return (jnp.cos(angles), jnp.sin(angles))


def norm_forward(values, gain_row):
    inverse = lax.rsqrt(jnp.mean(values * values, axis=-1, keepdims=True) + EPSILON)
    return (values * inverse * gain_row, inverse)


def norm_backward(values, inverse, gain_row, grad_normed):
    scaled = gain_row * grad_normed
    gain_term = jnp.sum(grad_normed * values * inverse, axis=0)
    grad_values = inverse * scaled - values * inverse**3 * jnp.mean(
        scaled * values, axis=-1, keepdims=True
    )
    return (grad_values, gain_term)


def route_onehot(routes, experts):
    return (routes[..., None] == jnp.arange(experts, dtype=jnp.int32)).astype(F32)


def gate_forward(logits, onehot):
    chosen = jnp.sum(logits[:, None, :] * onehot, axis=-1)
    return jax.nn.softmax(chosen, axis=-1)


def gate_backward(gate_probs, grad_gates, onehot):
    centered = gate_probs * (grad_gates - jnp.sum(gate_probs * grad_gates, axis=-1, keepdims=True))
    return jnp.sum(centered[..., None] * onehot, axis=1)


def slot_columns(routes, experts, capacity):
    flat_routes = routes.reshape(-1)
    onehot = (flat_routes[:, None] == jnp.arange(experts, dtype=jnp.int32)[None, :]).astype(
        jnp.int32
    )
    slot_rank = jnp.sum((jnp.cumsum(onehot, axis=0) - 1) * onehot, axis=1)
    return (flat_routes * capacity + slot_rank).reshape(routes.shape)


def dot_f32(left, right):
    return jnp.dot(left, right, preferred_element_type=F32)


def after(value, *others):
    return lax.optimization_barrier((value,) + others)[0]


def shift_planes(value, amount):
    planes = lax.axis_size("expert")
    return lax.ppermute(value, "expert", [(i, (i + amount) % planes) for i in range(planes)])


def exchange_planes(blocks, direction):
    arrived = [blocks[0]]
    for c in range(1, blocks.shape[0]):
        arrived.append(shift_planes(blocks[c], direction * c))
    return jnp.stack(arrived, axis=0)


def gather_planes(value, me, holds):
    planes = lax.axis_size("expert")
    right, left = value, value
    rights, lefts = [], []
    for d in range(1, planes):
        if d - 1 in holds:
            right, left = after(right, *holds[d - 1]), after(left, *holds[d - 1])
        right = lax.ppermute(right, "expert", [(i, i + 1) for i in range(d - 1, planes - 1)])
        left = lax.ppermute(left, "expert", [(i + 1, i) for i in range(0, planes - d)])
        rights.append(right)
        lefts.append(left)
    gathered = [value]
    for c in range(1, planes):
        gathered.append(jnp.where(me + c < planes, lefts[c - 1], rights[planes - c - 1]))
    return gathered


def reduce_planes(parts):
    planes = len(parts)
    right, left = None, None
    arrivals = []
    for t in range(1, planes):
        send_right, send_left = parts[planes - t], parts[t]
        if right is not None:
            send_right = (send_right.astype(F32) + right.astype(F32)).astype(BF16)
            send_left = (send_left.astype(F32) + left.astype(F32)).astype(BF16)
        right = lax.ppermute(send_right, "expert", [(i, i + 1) for i in range(0, t)])
        left = lax.ppermute(
            send_left, "expert", [(i, i - 1) for i in range(planes - t, planes)]
        )
        arrivals.append((right, left))
    return parts[0].astype(F32) + right.astype(F32) + left.astype(F32), arrivals


def swap_dp(value, mask):
    size = lax.axis_size("dp")
    return lax.ppermute(value, "dp", [(i, i ^ mask) for i in range(size)])


def all_sum(value, axis):
    size = lax.axis_size(axis)
    mask = 1
    while mask < size:
        value = value + lax.ppermute(value, axis, [(i, i ^ mask) for i in range(size)])
        mask *= 2
    return value


def reduce_rows(left, matmul, me, holds=()):
    size = lax.axis_size("dp")
    blocks = left.reshape(size // 2, 2, left.shape[0] // size, left.shape[1])
    core, chip = me % 2, me // 2

    def half(index):
        rows = lax.dynamic_index_in_dim(blocks, index, axis=1, keepdims=False)
        return matmul(rows.reshape(-1, left.shape[1])).reshape(size // 2, blocks.shape[2], -1)

    arrived = swap_dp(half(1 - core).astype(BF16), 1)
    mine = half(core) + arrived.astype(F32)
    low = mine.astype(BF16)
    total = lax.dynamic_index_in_dim(low, chip, axis=0, keepdims=False)
    total = after(total, *holds).astype(F32)
    for other in range(1, size // 2):
        send = lax.dynamic_index_in_dim(low, chip ^ other, axis=0, keepdims=False)
        total = total + swap_dp(send, 2 * other).astype(F32)
    return total, low


def from_plane_order(relative, plane):
    planes = relative.shape[0]
    return lax.dynamic_slice_in_dim(
        jnp.concatenate([relative, relative], axis=0), (planes - plane) % planes, planes, axis=0
    )


def per_device(
    tokens,
    segment_ids,
    attn_routes,
    mlp_routes,
    cotangent,
    attn_gain,
    kv_weights,
    attn_router,
    query_maps,
    output_maps,
    mlp_gain,
    mlp_router,
    gate_up,
    down_maps,
):
    micro_count, seq_count, local_len, width = tokens.shape
    units = micro_count * seq_count
    length = segment_ids.shape[2]
    experts = attn_router.shape[1]
    dp = lax.axis_size("dp")
    planes = lax.axis_size("expert")
    capacity = 2 * local_len // experts
    slots = experts * capacity
    head_cols = width // dp
    heads = head_cols // HEAD_WIDTH
    plane = lax.axis_index("expert")
    my_dp = lax.axis_index("dp")

    tokens = tokens.reshape(units, local_len, width)
    cotangent = cotangent.reshape(units, local_len, width)
    segments = segment_ids.reshape(units, length)
    attn_routes = attn_routes.reshape(units, local_len, 2)
    mlp_routes = mlp_routes.reshape(units, local_len, 2)

    slot_ids = jnp.arange(slots, dtype=jnp.int32)
    hits_list, tables, other_list = [], [], []
    for u in range(units):
        columns = slot_columns((mlp_routes[u] - plane) % experts, experts, capacity)
        hits = (columns[None] == slot_ids[:, None, None]).astype(F32)
        hits_list.append(hits)
        tables.append(jnp.sum(hits, axis=2).astype(BF16))
        other_list.append(jnp.sum(hits * mlp_routes[u][None, :, ::-1].astype(F32), axis=(1, 2)))

    def send_slots(slot_rows):
        moved = exchange_planes(slot_rows.reshape(planes, capacity, width), 1)
        return moved.reshape(slots, width)

    def gather_rows(moved):
        return lax.all_gather(moved, "dp", axis=0, tiled=True)

    def to_home(rows):
        return exchange_planes(rows.reshape(planes, capacity, -1), -1).reshape(slots, -1)

    kv_rows = kv_weights.shape[0]
    query_rows = query_maps.shape[1]
    packed = jnp.concatenate(
        [query_maps[0], kv_weights.transpose(1, 0, 2).reshape(2 * kv_rows, width)], axis=0
    )
    params = jnp.concatenate([attn_gain, mlp_gain, attn_router.reshape(-1), mlp_router.reshape(-1)])
    sizes = [units * local_len * 2, units * slots, params.shape[0]]
    info = jnp.concatenate(
        [attn_routes.astype(BF16).reshape(-1)] + [o.astype(BF16) for o in other_list] + [params]
    )
    info = jnp.pad(info, (0, -info.shape[0] % (16 * head_cols))).reshape(1, -1, head_cols)
    packed = packed.reshape(-1, dp, head_cols).transpose(1, 0, 2)
    weight_rows = packed.shape[1]
    packed = jnp.concatenate([packed, jnp.broadcast_to(info, (dp,) + info.shape[1:])], axis=1)
    packed = lax.all_to_all(packed, "dp", split_axis=0, concat_axis=0, tiled=True)
    info = packed[:, weight_rows:].reshape(dp, -1)
    cot_moved = [send_slots(dot_f32(tables[u], cotangent[u]).astype(BF16)) for u in range(units)]
    cot_rows_list = [gather_rows(part) for part in cot_moved]

    x_all = lax.all_gather(tokens.reshape(units * local_len, width), "dp", axis=0)

    routes_info = info[:, : sizes[0]].reshape(dp, units, local_len, 2).transpose(1, 0, 2, 3)
    routes_info = routes_info.reshape(units, length, 2).astype(jnp.int32)
    others = info[:, sizes[0] : sizes[0] + sizes[1]].reshape(dp, units, experts, capacity)
    others = exchange_planes(others.transpose(2, 1, 0, 3), 1)
    other_rows = others.transpose(1, 2, 0, 3).reshape(units, dp * slots).astype(jnp.int32)
    params = info[:, sizes[0] + sizes[1] : sum(sizes)]
    params = [params] + [shift_planes(params, -c) for c in range(1, planes)]
    params = from_plane_order(jnp.stack(params, axis=0), plane)

    def param(start, each):
        part = params[:, :, start : start + kv_rows * each]
        return part.reshape(planes, dp, kv_rows, each).transpose(1, 0, 2, 3).reshape(width, each)

    gain_one = param(0, 1).reshape(-1).astype(F32)
    gain_two = param(kv_rows, 1).reshape(-1).astype(F32)
    router_one_low = param(2 * kv_rows, experts)
    router_two_low = param((2 + experts) * kv_rows, experts)
    router_one = router_one_low.astype(F32)
    router_two = router_two_low.astype(F32)
    router_wide = jnp.pad(router_two_low, ((0, 0), (0, 128 - experts)))

    hidden_units = down_maps.shape[1]
    place = plane.astype(jnp.int32)[None]

    cosine, sine_table = rope_tables(jnp.arange(length, dtype=jnp.int32), HEAD_WIDTH // 2)
    cosine = jnp.concatenate([cosine, cosine], axis=1)
    sine_table = jnp.concatenate([-sine_table, sine_table], axis=1)

    mixed_parts = []
    input_parts = []
    gain_one_sum = jnp.zeros((width,), F32)
    gain_two_sum = jnp.zeros((width,), F32)
    each = range(units)

    inputs, a_home, inverse_one, a_all, routes_here, gates_all, kept, gated, states = (
        [], [], [], [], [], [], [], [], []
    )
    for u in each:
        inputs.append(tokens[u].astype(F32))
        normed, inverse = norm_forward(inputs[u], gain_one)
        a_home.append(normed.astype(BF16))
        inverse_one.append(inverse)
        a_all.append(norm_sequence(x_all, u, gain_one, local_len))
        gates_all.append(
            gate_forward(dot_f32(a_all[u], router_one_low), route_onehot(routes_info[u], experts))
        )

    packed = gather_planes(packed, plane, {1: tuple(cot_moved + a_all), 2: tuple(gates_all)})
    query_cols = [p[:, :query_rows].reshape(width, head_cols) for p in packed]
    kv_cols = from_plane_order(jnp.stack([p[:, query_rows:weight_rows] for p in packed], axis=0), plane)
    kv_cols = kv_cols.transpose(1, 0, 2, 3)
    key_cols = kv_cols[:, :, :kv_rows].reshape(width, head_cols)
    value_cols = kv_cols[:, :, kv_rows:].reshape(width, head_cols)
    for u in each:
        routes_here.append((routes_info[u] - plane) % experts)
        a_now = after(a_all[u], *gated)
        raws = [dot_f32(a_now, cols).astype(BF16) for cols in query_cols]
        keys = dot_f32(a_now, key_cols)
        values = dot_f32(a_now, value_cols).astype(BF16)
        *saved, context_gated = attn_forward(
            routes_here[u], gates_all[u], segments[u], cosine, sine_table, raws, keys, values
        )
        kept.append(saved)
        gated.append(context_gated)
    output_list = after(output_maps[0], packed[1], packed[-1])
    output_list = gather_planes(output_list, plane, {1: (gated[0], cot_rows_list[0]), 2: (gated[-1], cot_rows_list[-1])})
    output_rows = jnp.concatenate(output_list, axis=0)
    padding = ((0, -hidden_units % 128), (0, 0))
    gate_up_now = after(gate_up, gated[-1])
    gate_up_local = jnp.concatenate(
        [jnp.pad(gate_up_now[0, :, 0], padding), jnp.pad(gate_up_now[0, :, 1], padding)], axis=0
    )
    down_local = jnp.pad(after(down_maps, gated[-1])[0], padding)

    b_home, inverse_two, onehot_mlp, gates_mlp, moved, sent = [], [], [], [], [], []
    for u in each:
        gated_now = after(gated[u], *sent)
        attn_sum, low = reduce_rows(
            gated_now, lambda rows: dot_f32(rows, output_rows), my_dp, moved[-1:] + [gate_up_local, down_local] if moved else []
        )
        sent.append(low)
        states.append(inputs[u] + attn_sum)
        normed, inverse = norm_forward(states[u], gain_two)
        b_home.append(normed.astype(BF16))
        inverse_two.append(inverse)
        onehot_mlp.append(route_onehot(mlp_routes[u], experts))
        gates_mlp.append(gate_forward(dot_f32(b_home[u], router_two_low), onehot_mlp[u]))
        moved.append(send_slots(dot_f32(tables[u], b_home[u]).astype(BF16)))

    b_rows_list, hid_list, dhid_list, grad_b_rows, outs = [], [], [], [], []
    for u in each:
        b_rows_list.append(gather_rows(moved[u]))
        b_rows = b_rows_list[u]
        b_rows = after(b_rows, *moved[1:], *hid_list)
        outs, grad_part, hidden, dhidden = mlp_experts(
            place,
            b_rows,
            cot_rows_list[u],
            other_rows[u][:, None],
            router_wide,
            gate_up_local,
            down_local,
            dp,
            u,
            units,
            outs,
        )
        outs = [outs]
        hid_list.append(hidden)
        dhid_list.append(dhidden)
        grad_b_rows.append(lax.psum_scatter(grad_part, "dp", scatter_dimension=0, tiled=True))

    dlm_list, grad_states, dh_list = [], [], []
    down_grad, both_grad, last = 0.0, 0.0, hid_list[-1]
    for u in each:
        down_grad = down_grad + jnp.einsum(
            "rf,rd->fd",
            after(hid_list[u], last),
            cot_rows_list[u],
            preferred_element_type=F32,
        )
        both_grad = both_grad + jnp.einsum(
            "rf,rd->fd", after(dhid_list[u], down_grad), b_rows_list[u], preferred_element_type=F32
        )
        grad_b_slots = after(to_home(after(grad_b_rows[u], *grad_states)), both_grad, *dh_list)
        hits = hits_list[u]
        cot = cotangent[u]
        dgm_slots = grad_b_slots[:, width].astype(F32)
        grad_b_slots = grad_b_slots[:, :width]
        dlm = gate_backward(
            gates_mlp[u], jnp.sum(hits * dgm_slots[:, None, None], axis=0), onehot_mlp[u]
        )
        dlm_list.append(dlm)
        grad_b = jnp.einsum(
            "st,sd->td", tables[u], grad_b_slots, preferred_element_type=F32
        ) + jnp.einsum("re,de->rd", dlm, router_two, precision=PRECISION_TOP)
        grad_state, gain_two_term = norm_backward(states[u], inverse_two[u], gain_two, grad_b)
        gain_two_sum = gain_two_sum + gain_two_term
        grad_states.append(cot.astype(F32) + grad_state)
        last = grad_states[u]
        dh_list.append(lax.all_gather(grad_states[u].astype(BF16), "dp", axis=0, tiled=True))

    qkv_cols = jnp.concatenate(
        [after(cols, *moved) for cols in query_cols + [key_cols, value_cols]], axis=1
    )
    qkv_cols = jnp.concatenate(
        [
            jnp.pad(qkv_cols, ((0, 0), (0, 128))),
            jnp.pad(jnp.eye(128, dtype=BF16), ((0, 0), (qkv_cols.shape[1], 0))),
        ],
        axis=0,
    )
    g_list, output_part = [], 0.0
    for u in each:
        dh_now = after(dh_list[u], *(g_list[-1:] or grad_states[-1:]))
        grad_context = jnp.einsum("td,cd->tc", dh_now, output_rows, preferred_element_type=F32)
        if u == units - 1:
            for v in each:
                output_part = output_part + jnp.einsum(
                    "tc,td->cd", gated[v], after(dh_list[v], dh_now), preferred_element_type=F32
                )
            output_part = output_part.astype(BF16)
            grad_context = after(grad_context, output_part)
        g_list.append(
            attn_backward(
                routes_here[u],
                gates_all[u],
                segments[u],
                cosine,
                sine_table,
                *kept[u],
                grad_context,
            )
        )

    out_rows = lax.psum_scatter(after(outs[0], g_list[0]), "dp", scatter_dimension=0, tiled=True)

    dla_list = []

    def cols_grad(c, hold):
        total = 0.0
        for u in each:
            piece = lax.dynamic_slice_in_dim(
                after(g_list[u], hold), c * head_cols, head_cols, axis=1
            )
            total = total + jnp.einsum("td,tc->dc", a_all[u], piece, preferred_element_type=F32)
        return total.astype(BF16)

    def finish_inputs(u, hold):
        nonlocal gain_one_sum
        grad_a, low = reduce_rows(
            after(g_list[u], hold),
            lambda rows: jnp.einsum("tc,dc->td", rows, qkv_cols, preferred_element_type=F32),
            my_dp,
        )
        dga = grad_a[:, width : width + 2]
        grad_a = grad_a[:, :width]
        gates_home = lax.dynamic_slice_in_dim(gates_all[u], my_dp * local_len, local_len, axis=0)
        dla = gate_backward(gates_home, dga, route_onehot(attn_routes[u], experts))
        dla_list.append(dla)
        grad_a = grad_a + jnp.einsum("re,de->rd", dla, router_one, precision=PRECISION_TOP)
        grad_inputs, gain_one_term = norm_backward(inputs[u], inverse_one[u], gain_one, grad_a)
        gain_one_sum = gain_one_sum + gain_one_term
        input_parts.append(grad_states[u] + grad_inputs)
        return low

    output_grad, arrivals = reduce_planes(
        [output_part[c * head_cols : (c + 1) * head_cols] for c in range(planes)]
    )
    done = after(g_list[-1], *arrivals[0])
    query_parts = []
    for e in range(planes):
        done = cols_grad((e - plane) % planes, done)
        query_parts.append(done.reshape(dp, query_rows, head_cols))
    kv_part = []
    for i in range(2):
        done = cols_grad(experts + i, done)
        kv_part.append(done.reshape(dp, planes, kv_rows, head_cols))
    packed_grad = jnp.concatenate(
        [jnp.stack(query_parts, axis=0)] + [part.transpose(1, 0, 2, 3) for part in kv_part], axis=2
    )
    both_grad = after(both_grad, done)
    gate_up_grad = weave_rows(both_grad, hidden_units)
    down_grad = after(down_grad, done)[:hidden_units]

    packed_grad = after(packed_grad, out_rows, output_grad, gate_up_grad)
    packed_grad = lax.psum_scatter(packed_grad, "expert", scatter_dimension=0, tiled=False)

    for u in each:
        out_slots = to_home(out_rows[:, u * width : (u + 1) * width])
        gated_table = jnp.sum(hits_list[u] * gates_mlp[u][None], axis=2).T
        gated_high = gated_table.astype(BF16)
        gated_low = (gated_table - gated_high.astype(F32)).astype(BF16)
        mlp_sum = dot_f32(gated_high, out_slots) + dot_f32(gated_low, out_slots)
        mixed_parts.append((states[u] + mlp_sum).astype(BF16))

    for u in each:
        done = after(done, *mixed_parts[: u])
        done = finish_inputs(u, done)
    packed_grad = lax.all_to_all(packed_grad, "dp", split_axis=0, concat_axis=0, tiled=True)
    packed_grad = packed_grad.transpose(1, 0, 2).reshape(-1, width).astype(F32)
    query_grad = packed_grad[:query_rows]
    kv_grad = packed_grad[query_rows:].reshape(2, kv_rows, width).transpose(1, 0, 2)

    router_one_grad = jnp.einsum(
        "re,rd->ed",
        jnp.concatenate(dla_list, axis=0),
        jnp.concatenate(a_home, axis=0).astype(F32),
        precision=PRECISION_TOP,
    )
    router_two_grad = jnp.einsum(
        "re,rd->ed",
        jnp.concatenate(dlm_list, axis=0),
        jnp.concatenate(b_home, axis=0).astype(F32),
        precision=PRECISION_TOP,
    )
    small_grad = jnp.concatenate(
        [gain_one_sum[None], gain_two_sum[None], router_one_grad, router_two_grad], axis=0
    )
    small_grad = all_sum(all_sum(small_grad, "dp"), "expert")
    small_grad = lax.dynamic_index_in_dim(
        small_grad.reshape(-1, dp * planes, kv_rows), my_dp * planes + plane, axis=1, keepdims=False
    )

    shape = (micro_count, seq_count, local_len, width)
    return (
        jnp.stack(mixed_parts, axis=0).reshape(shape),
        jnp.stack(input_parts, axis=0).reshape(shape),
        small_grad[0],
        kv_grad,
        small_grad[2 : 2 + experts].T,
        query_grad[None],
        output_grad[None],
        small_grad[1],
        small_grad[2 + experts :].T,
        gate_up_grad,
        down_grad[None],
    )


def solution(mesh):
    in_specs = (
        P(None, "expert", "dp", None),
        P(None, "expert", None),
        P(None, "expert", "dp", None),
        P(None, "expert", "dp", None),
        P(None, "expert", "dp", None),
        P(("dp", "expert")),
        P(("dp", "expert"), None, None),
        P(("dp", "expert"), None),
        P("expert", "dp", None),
        P("expert", "dp", None),
        P(("dp", "expert")),
        P(("dp", "expert"), None),
        P("expert", "dp", None, None),
        P("expert", "dp", None),
    )
    out_specs = (
        P(None, "expert", "dp", None),
        P(None, "expert", "dp", None),
        P(("dp", "expert")),
        P(("dp", "expert"), None, None),
        P(("dp", "expert"), None),
        P("expert", "dp", None),
        P("expert", "dp", None),
        P(("dp", "expert")),
        P(("dp", "expert"), None),
        P("expert", "dp", None, None),
        P("expert", "dp", None),
    )
    return jax.shard_map(
        per_device, mesh=mesh, in_specs=in_specs, out_specs=out_specs, check_vma=False
    )
```

```python
import functools

import jax
import jax.numpy as jnp
from jax import lax
from jax.experimental import pallas as pl
from jax.experimental.pallas import tpu as pltpu
from jax.sharding import PartitionSpec as P

HEAD_WIDTH = 128


EPSILON = 1e-05
THETA_BASE = 10000.0
NEGATIVE = -1000000000.0
PRECISION_TOP = lax.Precision.HIGHEST
BF16 = jnp.bfloat16
F32 = jnp.float32


def rope_in(values, cosine, sine_signed):
    return values * cosine + pltpu.roll(values, HEAD_WIDTH // 2, 1) * sine_signed


def contract(left, right, left_dim, right_dim):
    return lax.dot_general(
        left, right, (((left_dim,), (right_dim,)), ((), ())), preferred_element_type=F32
    )


def block_mask(seg_col_ref, seg_row_ref, i, block):
    n = (i + 1) * block
    rows = slice(i * block, n)
    return (
        lax.broadcasted_iota(jnp.int32, (n, block), 0)
        <= lax.broadcasted_iota(jnp.int32, (n, block), 1) + i * block
    ) & (seg_col_ref[:n, :] == seg_row_ref[:, rows])


def key_softmax(score):
    exponent = jnp.exp(score - jnp.max(score, axis=0, keepdims=True))
    return exponent * (1.0 / jnp.sum(exponent, axis=0, keepdims=True))


def attn_forward_kernel(*refs, experts, heads, block, scale):
    routes_ref, gates_ref, seg_col_ref, seg_row_ref, cos_ref, sin_ref, keys_ref, values_ref = refs[:8]
    raw_refs = refs[8 : 8 + experts]
    q_ref, k_ref, v_ref, o_ref, gated_ref = refs[8 + experts :]
    length = cos_ref.shape[0]
    width = HEAD_WIDTH
    cosine = cos_ref[...]
    sine = sin_ref[...]
    routes = [routes_ref[:, c : c + 1] for c in range(2)]
    for h in range(heads):
        cols = slice(h * width, (h + 1) * width)
        k_ref[h] = rope_in(keys_ref[:, cols], cosine, sine).astype(BF16)
        v_ref[h] = values_ref[:, cols]
        for choice in range(2):
            raw = raw_refs[0][:, cols].astype(F32)
            for e in range(1, experts):
                raw = jnp.where(routes[choice] == e, raw_refs[e][:, cols].astype(F32), raw)
            q_ref[h, choice] = rope_in(raw, cosine, sine).astype(BF16)
    for i in range(length // block):
        rows = slice(i * block, (i + 1) * block)
        n = (i + 1) * block
        mask = block_mask(seg_col_ref, seg_row_ref, i, block)
        for h in range(heads):
            for choice in range(2):
                score = contract(k_ref[h, :n], q_ref[h, choice, rows], 1, 1) * scale
                probs = key_softmax(jnp.where(mask, score, NEGATIVE)).astype(BF16)
                o_ref[h, choice, rows] = contract(probs, v_ref[h, :n], 0, 0).astype(BF16)
    for h in range(heads):
        first = o_ref[h, 0].astype(F32) * gates_ref[:, 0:1]
        second = o_ref[h, 1].astype(F32) * gates_ref[:, 1:2]
        for e in range(experts):
            part = jnp.where(routes[0] == e, first, 0.0)
            part = jnp.where(routes[1] == e, second, part)
            at = (e * heads + h) * width
            gated_ref[:, at : at + width] = part.astype(BF16)


def attn_backward_kernel(
    routes_ref, gates_ref, seg_col_ref, seg_row_ref, cos_ref, sin_ref, q_ref, k_ref, v_ref, o_ref, up_ref,
    grad_ref, dctx_ref, dq_ref, dk_ref, dv_ref, *, experts, heads, block, scale,
):
    length = cos_ref.shape[0]
    width = HEAD_WIDTH
    lanes = lax.broadcasted_iota(jnp.int32, (length, width), 1)
    routes = [routes_ref[:, c : c + 1] for c in range(2)]
    dgate = jnp.zeros((length, width), F32)
    for h in range(heads):
        for choice in range(2):
            up = up_ref[:, h * width : (h + 1) * width]
            for e in range(1, experts):
                at = (e * heads + h) * width
                up = jnp.where(routes[choice] == e, up_ref[:, at : at + width], up)
            part = jnp.sum(up * o_ref[h, choice].astype(F32), axis=1, keepdims=True)
            dgate = dgate + jnp.where(lanes == choice, part, 0.0)
            dctx_ref[h, choice] = (up * gates_ref[:, choice : choice + 1]).astype(BF16)
    grad_ref[:, (experts + 2) * heads * width :] = dgate.astype(BF16)
    dk_ref[...] = jnp.zeros_like(dk_ref)
    dv_ref[...] = jnp.zeros_like(dv_ref)
    for i in range(length // block):
        rows = slice(i * block, (i + 1) * block)
        n = (i + 1) * block
        mask = block_mask(seg_col_ref, seg_row_ref, i, block)
        for h in range(heads):
            for choice in range(2):
                query = q_ref[h, choice, rows]
                dctx = dctx_ref[h, choice, rows]
                score = contract(k_ref[h, :n], query, 1, 1) * scale
                probs = key_softmax(jnp.where(mask, score, NEGATIVE))
                dprobs = contract(v_ref[h, :n], dctx, 1, 1)
                dscore = probs * (dprobs - jnp.sum(probs * dprobs, axis=0, keepdims=True))
                dscore = dscore.astype(BF16)
                dv_ref[h, :n] += contract(probs.astype(BF16), dctx, 1, 0)
                dk_ref[h, :n] += contract(dscore, query, 1, 0)
                dq_ref[h, choice, rows] = contract(dscore, k_ref[h, :n], 0, 0)
    cosine = cos_ref[...]
    sine = -sin_ref[...]
    for h in range(heads):
        first = rope_in(dq_ref[h, 0] * scale, cosine, sine)
        second = rope_in(dq_ref[h, 1] * scale, cosine, sine)
        for e in range(experts):
            part = jnp.where(routes[0] == e, first, 0.0)
            part = jnp.where(routes[1] == e, second, part)
            at = (e * heads + h) * width
            grad_ref[:, at : at + width] = part.astype(BF16)
        at = (experts * heads + h) * width
        grad_ref[:, at : at + width] = rope_in(dk_ref[h] * scale, cosine, sine).astype(BF16)
        at = ((experts + 1) * heads + h) * width
        grad_ref[:, at : at + width] = dv_ref[h].astype(BF16)


def attn_forward(routes, gates, segments, cosine, sine, raws, keys, values):
    experts = len(raws)
    length, cols = raws[0].shape
    width = HEAD_WIDTH
    heads = cols // width
    scores = heads * length * length * 2
    return pl.pallas_call(
        functools.partial(
            attn_forward_kernel,
            experts=experts,
            heads=heads,
            block=min(256, length),
            scale=width**-0.5,
        ),
        out_shape=[
            jax.ShapeDtypeStruct((heads, 2, length, width), BF16),
            jax.ShapeDtypeStruct((heads, length, width), BF16),
            jax.ShapeDtypeStruct((heads, length, width), BF16),
            jax.ShapeDtypeStruct((heads, 2, length, width), BF16),
            jax.ShapeDtypeStruct((length, heads * experts * width), BF16),
        ],
        compiler_params=pltpu.CompilerParams(vmem_limit_bytes=48 * 2**20),
        cost_estimate=pl.CostEstimate(
            flops=scores * width * 8, bytes_accessed=12 * 2**20, transcendentals=scores
        ),
    )(routes, gates, segments[:, None], segments[None, :], cosine, sine, keys, values, *raws)


def attn_backward(routes, gates, segments, cosine, sine, q, k, v, o, up):
    heads, _, length, width = q.shape
    experts = up.shape[1] // (heads * width)
    scores = heads * length * length * 2
    return pl.pallas_call(
        functools.partial(
            attn_backward_kernel,
            experts=experts,
            heads=heads,
            block=min(256, length),
            scale=width**-0.5,
        ),
        out_shape=jax.ShapeDtypeStruct((length, (heads * (experts + 2) + 1) * width), BF16),
        scratch_shapes=[
            pltpu.VMEM((heads, 2, length, width), BF16),
            pltpu.VMEM((heads, 2, length, width), F32),
            pltpu.VMEM((heads, length, width), F32),
            pltpu.VMEM((heads, length, width), F32),
        ],
        compiler_params=pltpu.CompilerParams(vmem_limit_bytes=48 * 2**20),
        cost_estimate=pl.CostEstimate(
            flops=scores * width * 20, bytes_accessed=12 * 2**20, transcendentals=scores
        ),
    )(routes, gates, segments[:, None], segments[None, :], cosine, sine, q, k, v, o, up)


def mlp_kernel(
    place_ref, b_ref, cot_ref, other_ref, router_ref, gate_up_ref, down_ref,
    *rest,
):
    out_ref, grad_ref, hidden_ref, dhidden_ref = rest[-4:]
    hidden_units = down_ref.shape[0]
    rows = b_ref[...]
    logits = contract(rows, router_ref[...], 1, 0)
    lanes = lax.broadcasted_iota(jnp.int32, logits.shape, 1)
    own = jnp.sum(jnp.where(lanes == place_ref[0], logits, 0.0), axis=1, keepdims=True)
    other = jnp.sum(jnp.where(lanes == other_ref[...], logits, 0.0), axis=1, keepdims=True)
    gates = jax.nn.sigmoid(own - other)
    both = contract(rows, gate_up_ref[...], 1, 1)
    gate_val = both[:, :hidden_units]
    up_val = both[:, hidden_units:]
    sigmoid = jax.nn.sigmoid(gate_val)
    silu = gate_val * sigmoid
    hidden = silu * up_val
    hidden_low = hidden.astype(BF16)
    hidden_ref[...] = (hidden * gates).astype(BF16)
    grad_plain = contract(cot_ref[...], down_ref[...], 1, 1)
    dgate = jnp.sum(grad_plain * hidden_low.astype(F32), axis=1, keepdims=True)
    width = b_ref.shape[1]
    grad_ref[:, width:] = jnp.broadcast_to(dgate, (dgate.shape[0], grad_ref.shape[1] - width)).astype(BF16)
    grad_hidden = grad_plain * gates
    dhidden_ref[:, :hidden_units] = (
        grad_hidden * up_val * sigmoid * (1.0 + gate_val * (1.0 - sigmoid))
    ).astype(BF16)
    dhidden_ref[:, hidden_units:] = (grad_hidden * silu).astype(BF16)
    out_ref[...] = contract(hidden_low, down_ref[...], 1, 0).astype(BF16)
    grad_ref[:, :width] = contract(dhidden_ref[...], gate_up_ref[...], 1, 0).astype(BF16)


def mlp_experts(place, b_rows, cot_rows, other_rows, router, gate_up, down, blocks, unit, units, outs):
    total, width = b_rows.shape
    hidden_units = down.shape[0]
    block = total // blocks
    by_row = lambda cols: pl.BlockSpec((block, cols), lambda i, place: (i, 0))
    fixed = lambda shape: pl.BlockSpec(shape, lambda i, place: (0, 0), pipeline_mode=pl.Buffered(1))
    return pl.pallas_call(
        mlp_kernel,
        grid_spec=pltpu.PrefetchScalarGridSpec(
            num_scalar_prefetch=1,
            grid=(blocks,),
            in_specs=[
                by_row(width),
                by_row(width),
                by_row(1),
                fixed(router.shape),
                fixed(gate_up.shape),
                fixed(down.shape),
            ]
            + [pl.BlockSpec(memory_space=pl.ANY)] * len(outs),
            out_specs=[
                pl.BlockSpec((block, width), lambda i, place: (i, unit)),
                by_row(width + 128),
                by_row(hidden_units),
                by_row(2 * hidden_units),
            ],
        ),
        out_shape=[
            jax.ShapeDtypeStruct((total, units * width), BF16),
            jax.ShapeDtypeStruct((total, width + 128), BF16),
            jax.ShapeDtypeStruct((total, hidden_units), BF16),
            jax.ShapeDtypeStruct((total, 2 * hidden_units), BF16),
        ],
        compiler_params=pltpu.CompilerParams(vmem_limit_bytes=56 * 2**20),
        cost_estimate=pl.CostEstimate(
            flops=total * width * hidden_units * 12,
            bytes_accessed=4 * total * width * 2 + 6 * total * hidden_units + 6 * width * hidden_units,
            transcendentals=total * hidden_units,
        ),
        input_output_aliases={7: 0} if outs else {},
    )(place, b_rows, cot_rows, other_rows, router, gate_up, down, *outs)


def weave_kernel(first_ref, second_ref, out_ref):
    out_ref[0, :, 0, :] = first_ref[...]
    out_ref[0, :, 1, :] = second_ref[...]


def weave_rows(both, units):
    total, width = both.shape
    block = 32
    half = total // 2 // block
    return pl.pallas_call(
        weave_kernel,
        grid=(units // block,),
        in_specs=[
            pl.BlockSpec((block, width), lambda i: (i, 0)),
            pl.BlockSpec((block, width), lambda i: (i + half, 0)),
        ],
        out_specs=pl.BlockSpec((1, block, 2, width), lambda i: (0, i, 0, 0)),
        out_shape=jax.ShapeDtypeStruct((1, units, 2, width), F32),
        cost_estimate=pl.CostEstimate(
            flops=0, bytes_accessed=16 * units * width, transcendentals=0
        ),
    )(both, both)


def norm_kernel(x_ref, gain_ref, out_ref):
    values = x_ref[0].astype(F32)
    inverse = lax.rsqrt(jnp.mean(values * values, axis=1, keepdims=True) + EPSILON)
    out_ref[...] = (values * inverse * gain_ref[...]).astype(BF16)


def norm_sequence(gathered, unit, gain, rows):
    blocks, _, width = gathered.shape
    return pl.pallas_call(
        norm_kernel,
        grid=(blocks,),
        in_specs=[
            pl.BlockSpec((1, rows, width), lambda i: (i, unit, 0)),
            pl.BlockSpec((1, width), lambda i: (0, 0)),
        ],
        out_specs=pl.BlockSpec((rows, width), lambda i: (i, 0)),
        out_shape=jax.ShapeDtypeStruct((blocks * rows, width), BF16),
        cost_estimate=pl.CostEstimate(
            flops=blocks * rows * width * 6, bytes_accessed=blocks * rows * width * 4, transcendentals=0
        ),
    )(gathered, gain[None])


def rope_tables(positions, half_dim):
    frequency = THETA_BASE ** (-jnp.arange(half_dim, dtype=F32) / half_dim)
    angles = positions.astype(F32)[:, None] * frequency[None, :]
    return (jnp.cos(angles), jnp.sin(angles))


def norm_forward(values, gain_row):
    inverse = lax.rsqrt(jnp.mean(values * values, axis=-1, keepdims=True) + EPSILON)
    return (values * inverse * gain_row, inverse)


def norm_backward(values, inverse, gain_row, grad_normed):
    scaled = gain_row * grad_normed
    gain_term = jnp.sum(grad_normed * values * inverse, axis=0)
    grad_values = inverse * scaled - values * inverse**3 * jnp.mean(
        scaled * values, axis=-1, keepdims=True
    )
    return (grad_values, gain_term)


def route_onehot(routes, experts):
    return (routes[..., None] == jnp.arange(experts, dtype=jnp.int32)).astype(F32)


def gate_forward(logits, onehot):
    chosen = jnp.sum(logits[:, None, :] * onehot, axis=-1)
    return jax.nn.softmax(chosen, axis=-1)


def gate_backward(gate_probs, grad_gates, onehot):
    centered = gate_probs * (grad_gates - jnp.sum(gate_probs * grad_gates, axis=-1, keepdims=True))
    return jnp.sum(centered[..., None] * onehot, axis=1)


def slot_columns(routes, experts, capacity):
    flat_routes = routes.reshape(-1)
    onehot = (flat_routes[:, None] == jnp.arange(experts, dtype=jnp.int32)[None, :]).astype(
        jnp.int32
    )
    slot_rank = jnp.sum((jnp.cumsum(onehot, axis=0) - 1) * onehot, axis=1)
    return (flat_routes * capacity + slot_rank).reshape(routes.shape)


def dot_f32(left, right):
    return jnp.dot(left, right, preferred_element_type=F32)


def after(value, *others):
    return lax.optimization_barrier((value,) + others)[0]


def shift_planes(value, amount):
    planes = lax.axis_size("expert")
    return lax.ppermute(value, "expert", [(i, (i + amount) % planes) for i in range(planes)])


def exchange_planes(blocks, direction):
    arrived = [blocks[0]]
    for c in range(1, blocks.shape[0]):
        arrived.append(shift_planes(blocks[c], direction * c))
    return jnp.stack(arrived, axis=0)


def gather_planes(value, me, holds):
    planes = lax.axis_size("expert")
    right, left = value, value
    rights, lefts = [], []
    for d in range(1, planes):
        if d - 1 in holds:
            right, left = after(right, *holds[d - 1]), after(left, *holds[d - 1])
        right = lax.ppermute(right, "expert", [(i, i + 1) for i in range(d - 1, planes - 1)])
        left = lax.ppermute(left, "expert", [(i + 1, i) for i in range(0, planes - d)])
        rights.append(right)
        lefts.append(left)
    gathered = [value]
    for c in range(1, planes):
        gathered.append(jnp.where(me + c < planes, lefts[c - 1], rights[planes - c - 1]))
    return gathered


def reduce_planes(parts):
    planes = len(parts)
    right, left = None, None
    arrivals = []
    for t in range(1, planes):
        send_right, send_left = parts[planes - t], parts[t]
        if right is not None:
            send_right = (send_right.astype(F32) + right.astype(F32)).astype(BF16)
            send_left = (send_left.astype(F32) + left.astype(F32)).astype(BF16)
        right = lax.ppermute(send_right, "expert", [(i, i + 1) for i in range(0, t)])
        left = lax.ppermute(
            send_left, "expert", [(i, i - 1) for i in range(planes - t, planes)]
        )
        arrivals.append((right, left))
    return parts[0].astype(F32) + right.astype(F32) + left.astype(F32), arrivals


def swap_dp(value, mask):
    size = lax.axis_size("dp")
    return lax.ppermute(value, "dp", [(i, i ^ mask) for i in range(size)])


def all_sum(value, axis):
    size = lax.axis_size(axis)
    mask = 1
    while mask < size:
        value = value + lax.ppermute(value, axis, [(i, i ^ mask) for i in range(size)])
        mask *= 2
    return value


def reduce_rows(left, matmul, me, holds=()):
    size = lax.axis_size("dp")
    blocks = left.reshape(size // 2, 2, left.shape[0] // size, left.shape[1])
    core, chip = me % 2, me // 2

    def half(index):
        rows = lax.dynamic_index_in_dim(blocks, index, axis=1, keepdims=False)
        return matmul(rows.reshape(-1, left.shape[1])).reshape(size // 2, blocks.shape[2], -1)

    arrived = swap_dp(half(1 - core).astype(BF16), 1)
    mine = half(core) + arrived.astype(F32)
    low = mine.astype(BF16)
    total = lax.dynamic_index_in_dim(low, chip, axis=0, keepdims=False)
    total = after(total, *holds).astype(F32)
    for other in range(1, size // 2):
        send = lax.dynamic_index_in_dim(low, chip ^ other, axis=0, keepdims=False)
        total = total + swap_dp(send, 2 * other).astype(F32)
    return total, low


def from_plane_order(relative, plane):
    planes = relative.shape[0]
    return lax.dynamic_slice_in_dim(
        jnp.concatenate([relative, relative], axis=0), (planes - plane) % planes, planes, axis=0
    )


def per_device(
    tokens,
    segment_ids,
    attn_routes,
    mlp_routes,
    cotangent,
    attn_gain,
    kv_weights,
    attn_router,
    query_maps,
    output_maps,
    mlp_gain,
    mlp_router,
    gate_up,
    down_maps,
):
    micro_count, seq_count, local_len, width = tokens.shape
    units = micro_count * seq_count
    length = segment_ids.shape[2]
    experts = attn_router.shape[1]
    dp = lax.axis_size("dp")
    planes = lax.axis_size("expert")
    capacity = 2 * local_len // experts
    slots = experts * capacity
    head_cols = width // dp
    heads = head_cols // HEAD_WIDTH
    plane = lax.axis_index("expert")
    my_dp = lax.axis_index("dp")

    tokens = tokens.reshape(units, local_len, width)
    cotangent = cotangent.reshape(units, local_len, width)
    segments = segment_ids.reshape(units, length)
    attn_routes = attn_routes.reshape(units, local_len, 2)
    mlp_routes = mlp_routes.reshape(units, local_len, 2)

    slot_ids = jnp.arange(slots, dtype=jnp.int32)
    hits_list, tables, other_list = [], [], []
    for u in range(units):
        columns = slot_columns((mlp_routes[u] - plane) % experts, experts, capacity)
        hits = (columns[None] == slot_ids[:, None, None]).astype(F32)
        hits_list.append(hits)
        tables.append(jnp.sum(hits, axis=2).astype(BF16))
        other_list.append(jnp.sum(hits * mlp_routes[u][None, :, ::-1].astype(F32), axis=(1, 2)))

    def send_slots(slot_rows):
        moved = exchange_planes(slot_rows.reshape(planes, capacity, width), 1)
        return moved.reshape(slots, width)

    def gather_rows(moved):
        return lax.all_gather(moved, "dp", axis=0, tiled=True)

    def to_home(rows):
        return exchange_planes(rows.reshape(planes, capacity, -1), -1).reshape(slots, -1)

    kv_rows = kv_weights.shape[0]
    query_rows = query_maps.shape[1]
    packed = jnp.concatenate(
        [query_maps[0], kv_weights.transpose(1, 0, 2).reshape(2 * kv_rows, width)], axis=0
    )
    params = jnp.concatenate([attn_gain, mlp_gain, attn_router.reshape(-1), mlp_router.reshape(-1)])
    sizes = [units * local_len * 2, units * slots, params.shape[0]]
    info = jnp.concatenate(
        [attn_routes.astype(BF16).reshape(-1)] + [o.astype(BF16) for o in other_list] + [params]
    )
    info = jnp.pad(info, (0, -info.shape[0] % (16 * head_cols))).reshape(1, -1, head_cols)
    packed = packed.reshape(-1, dp, head_cols).transpose(1, 0, 2)
    weight_rows = packed.shape[1]
    packed = jnp.concatenate([packed, jnp.broadcast_to(info, (dp,) + info.shape[1:])], axis=1)
    packed = lax.all_to_all(packed, "dp", split_axis=0, concat_axis=0, tiled=True)
    info = packed[:, weight_rows:].reshape(dp, -1)
    cot_moved = [send_slots(dot_f32(tables[u], cotangent[u]).astype(BF16)) for u in range(units)]
    cot_rows_list = [gather_rows(part) for part in cot_moved]

    x_all = lax.all_gather(tokens.reshape(units * local_len, width), "dp", axis=0)

    routes_info = info[:, : sizes[0]].reshape(dp, units, local_len, 2).transpose(1, 0, 2, 3)
    routes_info = routes_info.reshape(units, length, 2).astype(jnp.int32)
    others = info[:, sizes[0] : sizes[0] + sizes[1]].reshape(dp, units, experts, capacity)
    others = exchange_planes(others.transpose(2, 1, 0, 3), 1)
    other_rows = others.transpose(1, 2, 0, 3).reshape(units, dp * slots).astype(jnp.int32)
    params = info[:, sizes[0] + sizes[1] : sum(sizes)]
    params = [params] + [shift_planes(params, -c) for c in range(1, planes)]
    params = from_plane_order(jnp.stack(params, axis=0), plane)

    def param(start, each):
        part = params[:, :, start : start + kv_rows * each]
        return part.reshape(planes, dp, kv_rows, each).transpose(1, 0, 2, 3).reshape(width, each)

    gain_one = param(0, 1).reshape(-1).astype(F32)
    gain_two = param(kv_rows, 1).reshape(-1).astype(F32)
    router_one_low = param(2 * kv_rows, experts)
    router_two_low = param((2 + experts) * kv_rows, experts)
    router_one = router_one_low.astype(F32)
    router_two = router_two_low.astype(F32)
    router_wide = jnp.pad(router_two_low, ((0, 0), (0, 128 - experts)))

    hidden_units = down_maps.shape[1]
    place = plane.astype(jnp.int32)[None]

    cosine, sine_table = rope_tables(jnp.arange(length, dtype=jnp.int32), HEAD_WIDTH // 2)
    cosine = jnp.concatenate([cosine, cosine], axis=1)
    sine_table = jnp.concatenate([-sine_table, sine_table], axis=1)

    mixed_parts = []
    input_parts = []
    gain_one_sum = jnp.zeros((width,), F32)
    gain_two_sum = jnp.zeros((width,), F32)
    each = range(units)

    inputs, a_home, inverse_one, a_all, routes_here, gates_all, kept, gated, states = (
        [], [], [], [], [], [], [], [], []
    )
    for u in each:
        inputs.append(tokens[u].astype(F32))
        normed, inverse = norm_forward(inputs[u], gain_one)
        a_home.append(normed.astype(BF16))
        inverse_one.append(inverse)
        a_all.append(norm_sequence(x_all, u, gain_one, local_len))
        gates_all.append(
            gate_forward(dot_f32(a_all[u], router_one_low), route_onehot(routes_info[u], experts))
        )

    packed = gather_planes(packed, plane, {1: tuple(cot_moved + a_all), 2: tuple(gates_all)})
    query_cols = [p[:, :query_rows].reshape(width, head_cols) for p in packed]
    kv_cols = from_plane_order(jnp.stack([p[:, query_rows:weight_rows] for p in packed], axis=0), plane)
    kv_cols = kv_cols.transpose(1, 0, 2, 3)
    key_cols = kv_cols[:, :, :kv_rows].reshape(width, head_cols)
    value_cols = kv_cols[:, :, kv_rows:].reshape(width, head_cols)
    for u in each:
        routes_here.append((routes_info[u] - plane) % experts)
        a_now = after(a_all[u], *gated)
        raws = [dot_f32(a_now, cols).astype(BF16) for cols in query_cols]
        keys = dot_f32(a_now, key_cols)
        values = dot_f32(a_now, value_cols).astype(BF16)
        *saved, context_gated = attn_forward(
            routes_here[u], gates_all[u], segments[u], cosine, sine_table, raws, keys, values
        )
        kept.append(saved)
        gated.append(context_gated)
    output_list = after(output_maps[0], packed[1], packed[-1])
    output_list = gather_planes(output_list, plane, {1: (gated[0], cot_rows_list[0]), 2: (gated[-1], cot_rows_list[-1])})
    output_rows = jnp.concatenate(output_list, axis=0)
    padding = ((0, -hidden_units % 128), (0, 0))
    gate_up_now = after(gate_up, gated[-1])
    gate_up_local = jnp.concatenate(
        [jnp.pad(gate_up_now[0, :, 0], padding), jnp.pad(gate_up_now[0, :, 1], padding)], axis=0
    )
    down_local = jnp.pad(after(down_maps, gated[-1])[0], padding)

    b_home, inverse_two, onehot_mlp, gates_mlp, moved, sent = [], [], [], [], [], []
    for u in each:
        gated_now = after(gated[u], *sent)
        attn_sum, low = reduce_rows(
            gated_now, lambda rows: dot_f32(rows, output_rows), my_dp, moved[-1:] + [gate_up_local, down_local] if moved else []
        )
        sent.append(low)
        states.append(inputs[u] + attn_sum)
        normed, inverse = norm_forward(states[u], gain_two)
        b_home.append(normed.astype(BF16))
        inverse_two.append(inverse)
        onehot_mlp.append(route_onehot(mlp_routes[u], experts))
        gates_mlp.append(gate_forward(dot_f32(b_home[u], router_two_low), onehot_mlp[u]))
        moved.append(send_slots(dot_f32(tables[u], b_home[u]).astype(BF16)))

    b_rows_list, hid_list, dhid_list, grad_b_rows, outs = [], [], [], [], []
    for u in each:
        b_rows_list.append(gather_rows(moved[u]))
        b_rows = b_rows_list[u]
        b_rows = after(b_rows, *moved[1:], *hid_list)
        outs, grad_part, hidden, dhidden = mlp_experts(
            place,
            b_rows,
            cot_rows_list[u],
            other_rows[u][:, None],
            router_wide,
            gate_up_local,
            down_local,
            dp,
            u,
            units,
            outs,
        )
        outs = [outs]
        hid_list.append(hidden)
        dhid_list.append(dhidden)
        grad_b_rows.append(lax.psum_scatter(grad_part, "dp", scatter_dimension=0, tiled=True))

    dlm_list, grad_states, dh_list = [], [], []
    down_grad, both_grad, last = 0.0, 0.0, hid_list[-1]
    for u in each:
        down_grad = down_grad + jnp.einsum(
            "rf,rd->fd",
            after(hid_list[u], last),
            cot_rows_list[u],
            preferred_element_type=F32,
        )
        both_grad = both_grad + jnp.einsum(
            "rf,rd->fd", after(dhid_list[u], down_grad), b_rows_list[u], preferred_element_type=F32
        )
        grad_b_slots = after(to_home(after(grad_b_rows[u], *grad_states)), both_grad, *dh_list)
        hits = hits_list[u]
        cot = cotangent[u]
        dgm_slots = grad_b_slots[:, width].astype(F32)
        grad_b_slots = grad_b_slots[:, :width]
        dlm = gate_backward(
            gates_mlp[u], jnp.sum(hits * dgm_slots[:, None, None], axis=0), onehot_mlp[u]
        )
        dlm_list.append(dlm)
        grad_b = jnp.einsum(
            "st,sd->td", tables[u], grad_b_slots, preferred_element_type=F32
        ) + jnp.einsum("re,de->rd", dlm, router_two, precision=PRECISION_TOP)
        grad_state, gain_two_term = norm_backward(states[u], inverse_two[u], gain_two, grad_b)
        gain_two_sum = gain_two_sum + gain_two_term
        grad_states.append(cot.astype(F32) + grad_state)
        last = grad_states[u]
        dh_list.append(lax.all_gather(grad_states[u].astype(BF16), "dp", axis=0, tiled=True))

    qkv_cols = jnp.concatenate(
        [after(cols, *moved) for cols in query_cols + [key_cols, value_cols]], axis=1
    )
    qkv_cols = jnp.concatenate(
        [
            jnp.pad(qkv_cols, ((0, 0), (0, 128))),
            jnp.pad(jnp.eye(128, dtype=BF16), ((0, 0), (qkv_cols.shape[1], 0))),
        ],
        axis=0,
    )
    g_list, output_part = [], 0.0
    for u in each:
        dh_now = after(dh_list[u], *(g_list[-1:] or grad_states[-1:]))
        grad_context = jnp.einsum("td,cd->tc", dh_now, output_rows, preferred_element_type=F32)
        if u == units - 1:
            for v in each:
                output_part = output_part + jnp.einsum(
                    "tc,td->cd", gated[v], after(dh_list[v], dh_now), preferred_element_type=F32
                )
            output_part = output_part.astype(BF16)
            grad_context = after(grad_context, output_part)
        g_list.append(
            attn_backward(
                routes_here[u],
                gates_all[u],
                segments[u],
                cosine,
                sine_table,
                *kept[u],
                grad_context,
            )
        )

    out_rows = lax.psum_scatter(after(outs[0], g_list[0]), "dp", scatter_dimension=0, tiled=True)

    dla_list = []

    def cols_grad(c, hold):
        total = 0.0
        for u in each:
            piece = lax.dynamic_slice_in_dim(
                after(g_list[u], hold), c * head_cols, head_cols, axis=1
            )
            total = total + jnp.einsum("td,tc->dc", a_all[u], piece, preferred_element_type=F32)
        return total.astype(BF16)

    def finish_inputs(u, hold):
        nonlocal gain_one_sum
        grad_a, low = reduce_rows(
            after(g_list[u], hold),
            lambda rows: jnp.einsum("tc,dc->td", rows, qkv_cols, preferred_element_type=F32),
            my_dp,
        )
        dga = grad_a[:, width : width + 2]
        grad_a = grad_a[:, :width]
        gates_home = lax.dynamic_slice_in_dim(gates_all[u], my_dp * local_len, local_len, axis=0)
        dla = gate_backward(gates_home, dga, route_onehot(attn_routes[u], experts))
        dla_list.append(dla)
        grad_a = grad_a + jnp.einsum("re,de->rd", dla, router_one, precision=PRECISION_TOP)
        grad_inputs, gain_one_term = norm_backward(inputs[u], inverse_one[u], gain_one, grad_a)
        gain_one_sum = gain_one_sum + gain_one_term
        input_parts.append(grad_states[u] + grad_inputs)
        return low

    output_grad, arrivals = reduce_planes(
        [output_part[c * head_cols : (c + 1) * head_cols] for c in range(planes)]
    )
    done = after(g_list[-1], *arrivals[0])
    query_parts = []
    for e in range(planes):
        done = cols_grad((e - plane) % planes, done)
        query_parts.append(done.reshape(dp, query_rows, head_cols))
    kv_part = []
    for i in range(2):
        done = cols_grad(experts + i, done)
        kv_part.append(done.reshape(dp, planes, kv_rows, head_cols))
    packed_grad = jnp.concatenate(
        [jnp.stack(query_parts, axis=0)] + [part.transpose(1, 0, 2, 3) for part in kv_part], axis=2
    )
    packed_grad = after(packed_grad, out_rows, output_grad)
    packed_grad = lax.psum_scatter(packed_grad, "expert", scatter_dimension=0, tiled=False)

    for u in each:
        out_slots = to_home(out_rows[:, u * width : (u + 1) * width])
        gated_table = jnp.sum(hits_list[u] * gates_mlp[u][None], axis=2).T
        gated_high = gated_table.astype(BF16)
        gated_low = (gated_table - gated_high.astype(F32)).astype(BF16)
        mlp_sum = dot_f32(gated_high, out_slots) + dot_f32(gated_low, out_slots)
        mixed_parts.append((states[u] + mlp_sum).astype(BF16))

    for u in each:
        done = after(done, *mixed_parts[: u])
        done = finish_inputs(u, done)
    both_grad = after(both_grad, done)
    gate_up_grad = weave_rows(both_grad, hidden_units)
    down_grad = after(down_grad, done)[:hidden_units]

    packed_grad = lax.all_to_all(packed_grad, "dp", split_axis=0, concat_axis=0, tiled=True)
    arrived = packed_grad
    packed_grad = packed_grad.transpose(1, 0, 2).reshape(-1, width).astype(F32)
    query_grad = packed_grad[:query_rows]
    kv_grad = packed_grad[query_rows:].reshape(2, kv_rows, width).transpose(1, 0, 2)

    router_one_grad = jnp.einsum(
        "re,rd->ed",
        jnp.concatenate(dla_list, axis=0),
        jnp.concatenate(a_home, axis=0).astype(F32),
        precision=PRECISION_TOP,
    )
    router_two_grad = jnp.einsum(
        "re,rd->ed",
        jnp.concatenate(dlm_list, axis=0),
        jnp.concatenate(b_home, axis=0).astype(F32),
        precision=PRECISION_TOP,
    )
    small_grad = jnp.concatenate(
        [gain_one_sum[None], gain_two_sum[None], router_one_grad, router_two_grad], axis=0
    )
    small_grad = all_sum(after(all_sum(small_grad, "dp"), arrived), "expert")
    small_grad = lax.dynamic_index_in_dim(
        small_grad.reshape(-1, dp * planes, kv_rows), my_dp * planes + plane, axis=1, keepdims=False
    )

    shape = (micro_count, seq_count, local_len, width)
    return (
        jnp.stack(mixed_parts, axis=0).reshape(shape),
        jnp.stack(input_parts, axis=0).reshape(shape),
        small_grad[0],
        kv_grad,
        small_grad[2 : 2 + experts].T,
        query_grad[None],
        output_grad[None],
        small_grad[1],
        small_grad[2 + experts :].T,
        gate_up_grad,
        down_grad[None],
    )


def solution(mesh):
    in_specs = (
        P(None, "expert", "dp", None),
        P(None, "expert", None),
        P(None, "expert", "dp", None),
        P(None, "expert", "dp", None),
        P(None, "expert", "dp", None),
        P(("dp", "expert")),
        P(("dp", "expert"), None, None),
        P(("dp", "expert"), None),
        P("expert", "dp", None),
        P("expert", "dp", None),
        P(("dp", "expert")),
        P(("dp", "expert"), None),
        P("expert", "dp", None, None),
        P("expert", "dp", None),
    )
    out_specs = (
        P(None, "expert", "dp", None),
        P(None, "expert", "dp", None),
        P(("dp", "expert")),
        P(("dp", "expert"), None, None),
        P(("dp", "expert"), None),
        P("expert", "dp", None),
        P("expert", "dp", None),
        P(("dp", "expert")),
        P(("dp", "expert"), None),
        P("expert", "dp", None, None),
        P("expert", "dp", None),
    )
    return jax.shard_map(
        per_device, mesh=mesh, in_specs=in_specs, out_specs=out_specs, check_vma=False
    )
```

```python
import functools

import jax
import jax.numpy as jnp
from jax import lax
from jax.experimental import pallas as pl
from jax.experimental.pallas import tpu as pltpu
from jax.sharding import PartitionSpec as P

HEAD_WIDTH = 128


EPSILON = 1e-05
THETA_BASE = 10000.0
NEGATIVE = -1000000000.0
PRECISION_TOP = lax.Precision.HIGHEST
BF16 = jnp.bfloat16
F32 = jnp.float32


def rope_in(values, cosine, sine_signed):
    return values * cosine + pltpu.roll(values, HEAD_WIDTH // 2, 1) * sine_signed


def contract(left, right, left_dim, right_dim):
    return lax.dot_general(
        left, right, (((left_dim,), (right_dim,)), ((), ())), preferred_element_type=F32
    )


def block_mask(seg_col_ref, seg_row_ref, i, block):
    n = (i + 1) * block
    rows = slice(i * block, n)
    return (
        lax.broadcasted_iota(jnp.int32, (n, block), 0)
        <= lax.broadcasted_iota(jnp.int32, (n, block), 1) + i * block
    ) & (seg_col_ref[:n, :] == seg_row_ref[:, rows])


def key_softmax(score):
    exponent = jnp.exp(score - jnp.max(score, axis=0, keepdims=True))
    return exponent * (1.0 / jnp.sum(exponent, axis=0, keepdims=True))


def attn_forward_kernel(*refs, experts, heads, block, scale):
    routes_ref, gates_ref, seg_col_ref, seg_row_ref, cos_ref, sin_ref, keys_ref, values_ref = refs[:8]
    raw_refs = refs[8 : 8 + experts]
    q_ref, k_ref, v_ref, o_ref, gated_ref = refs[8 + experts :]
    length = cos_ref.shape[0]
    width = HEAD_WIDTH
    cosine = cos_ref[...]
    sine = sin_ref[...]
    routes = [routes_ref[:, c : c + 1] for c in range(2)]
    for h in range(heads):
        cols = slice(h * width, (h + 1) * width)
        k_ref[h] = rope_in(keys_ref[:, cols], cosine, sine).astype(BF16)
        v_ref[h] = values_ref[:, cols]
        for choice in range(2):
            raw = raw_refs[0][:, cols].astype(F32)
            for e in range(1, experts):
                raw = jnp.where(routes[choice] == e, raw_refs[e][:, cols].astype(F32), raw)
            q_ref[h, choice] = rope_in(raw, cosine, sine).astype(BF16)
    for i in range(length // block):
        rows = slice(i * block, (i + 1) * block)
        n = (i + 1) * block
        mask = block_mask(seg_col_ref, seg_row_ref, i, block)
        for h in range(heads):
            for choice in range(2):
                score = contract(k_ref[h, :n], q_ref[h, choice, rows], 1, 1) * scale
                probs = key_softmax(jnp.where(mask, score, NEGATIVE)).astype(BF16)
                o_ref[h, choice, rows] = contract(probs, v_ref[h, :n], 0, 0).astype(BF16)
    for h in range(heads):
        first = o_ref[h, 0].astype(F32) * gates_ref[:, 0:1]
        second = o_ref[h, 1].astype(F32) * gates_ref[:, 1:2]
        for e in range(experts):
            part = jnp.where(routes[0] == e, first, 0.0)
            part = jnp.where(routes[1] == e, second, part)
            at = (e * heads + h) * width
            gated_ref[:, at : at + width] = part.astype(BF16)


def attn_backward_kernel(
    routes_ref, gates_ref, seg_col_ref, seg_row_ref, cos_ref, sin_ref, q_ref, k_ref, v_ref, o_ref, up_ref,
    grad_ref, dctx_ref, dq_ref, dk_ref, dv_ref, *, experts, heads, block, scale,
):
    length = cos_ref.shape[0]
    width = HEAD_WIDTH
    lanes = lax.broadcasted_iota(jnp.int32, (length, width), 1)
    routes = [routes_ref[:, c : c + 1] for c in range(2)]
    dgate = jnp.zeros((length, width), F32)
    for h in range(heads):
        for choice in range(2):
            up = up_ref[:, h * width : (h + 1) * width]
            for e in range(1, experts):
                at = (e * heads + h) * width
                up = jnp.where(routes[choice] == e, up_ref[:, at : at + width], up)
            part = jnp.sum(up * o_ref[h, choice].astype(F32), axis=1, keepdims=True)
            dgate = dgate + jnp.where(lanes == choice, part, 0.0)
            dctx_ref[h, choice] = (up * gates_ref[:, choice : choice + 1]).astype(BF16)
    grad_ref[:, (experts + 2) * heads * width :] = dgate.astype(BF16)
    dk_ref[...] = jnp.zeros_like(dk_ref)
    dv_ref[...] = jnp.zeros_like(dv_ref)
    for i in range(length // block):
        rows = slice(i * block, (i + 1) * block)
        n = (i + 1) * block
        mask = block_mask(seg_col_ref, seg_row_ref, i, block)
        for h in range(heads):
            for choice in range(2):
                query = q_ref[h, choice, rows]
                dctx = dctx_ref[h, choice, rows]
                score = contract(k_ref[h, :n], query, 1, 1) * scale
                probs = key_softmax(jnp.where(mask, score, NEGATIVE))
                dprobs = contract(v_ref[h, :n], dctx, 1, 1)
                dscore = probs * (dprobs - jnp.sum(probs * dprobs, axis=0, keepdims=True))
                dscore = dscore.astype(BF16)
                dv_ref[h, :n] += contract(probs.astype(BF16), dctx, 1, 0)
                dk_ref[h, :n] += contract(dscore, query, 1, 0)
                dq_ref[h, choice, rows] = contract(dscore, k_ref[h, :n], 0, 0)
    cosine = cos_ref[...]
    sine = -sin_ref[...]
    for h in range(heads):
        first = rope_in(dq_ref[h, 0] * scale, cosine, sine)
        second = rope_in(dq_ref[h, 1] * scale, cosine, sine)
        for e in range(experts):
            part = jnp.where(routes[0] == e, first, 0.0)
            part = jnp.where(routes[1] == e, second, part)
            at = (e * heads + h) * width
            grad_ref[:, at : at + width] = part.astype(BF16)
        at = (experts * heads + h) * width
        grad_ref[:, at : at + width] = rope_in(dk_ref[h] * scale, cosine, sine).astype(BF16)
        at = ((experts + 1) * heads + h) * width
        grad_ref[:, at : at + width] = dv_ref[h].astype(BF16)


def attn_forward(routes, gates, segments, cosine, sine, raws, keys, values):
    experts = len(raws)
    length, cols = raws[0].shape
    width = HEAD_WIDTH
    heads = cols // width
    scores = heads * length * length * 2
    return pl.pallas_call(
        functools.partial(
            attn_forward_kernel,
            experts=experts,
            heads=heads,
            block=min(256, length),
            scale=width**-0.5,
        ),
        out_shape=[
            jax.ShapeDtypeStruct((heads, 2, length, width), BF16),
            jax.ShapeDtypeStruct((heads, length, width), BF16),
            jax.ShapeDtypeStruct((heads, length, width), BF16),
            jax.ShapeDtypeStruct((heads, 2, length, width), BF16),
            jax.ShapeDtypeStruct((length, heads * experts * width), BF16),
        ],
        compiler_params=pltpu.CompilerParams(vmem_limit_bytes=48 * 2**20),
        cost_estimate=pl.CostEstimate(
            flops=scores * width * 8, bytes_accessed=12 * 2**20, transcendentals=scores
        ),
    )(routes, gates, segments[:, None], segments[None, :], cosine, sine, keys, values, *raws)


def attn_backward(routes, gates, segments, cosine, sine, q, k, v, o, up):
    heads, _, length, width = q.shape
    experts = up.shape[1] // (heads * width)
    scores = heads * length * length * 2
    return pl.pallas_call(
        functools.partial(
            attn_backward_kernel,
            experts=experts,
            heads=heads,
            block=min(256, length),
            scale=width**-0.5,
        ),
        out_shape=jax.ShapeDtypeStruct((length, (heads * (experts + 2) + 1) * width), BF16),
        scratch_shapes=[
            pltpu.VMEM((heads, 2, length, width), BF16),
            pltpu.VMEM((heads, 2, length, width), F32),
            pltpu.VMEM((heads, length, width), F32),
            pltpu.VMEM((heads, length, width), F32),
        ],
        compiler_params=pltpu.CompilerParams(vmem_limit_bytes=48 * 2**20),
        cost_estimate=pl.CostEstimate(
            flops=scores * width * 20, bytes_accessed=12 * 2**20, transcendentals=scores
        ),
    )(routes, gates, segments[:, None], segments[None, :], cosine, sine, q, k, v, o, up)


def mlp_kernel(
    place_ref, b_ref, cot_ref, other_ref, router_ref, gate_up_ref, down_ref,
    *rest,
):
    out_ref, grad_ref, hidden_ref, dhidden_ref = rest[-4:]
    hidden_units = down_ref.shape[0]
    rows = b_ref[...]
    logits = contract(rows, router_ref[...], 1, 0)
    lanes = lax.broadcasted_iota(jnp.int32, logits.shape, 1)
    own = jnp.sum(jnp.where(lanes == place_ref[0], logits, 0.0), axis=1, keepdims=True)
    other = jnp.sum(jnp.where(lanes == other_ref[...], logits, 0.0), axis=1, keepdims=True)
    gates = jax.nn.sigmoid(own - other)
    both = contract(rows, gate_up_ref[...], 1, 1)
    gate_val = both[:, :hidden_units]
    up_val = both[:, hidden_units:]
    sigmoid = jax.nn.sigmoid(gate_val)
    silu = gate_val * sigmoid
    hidden = silu * up_val
    hidden_low = hidden.astype(BF16)
    hidden_ref[...] = (hidden * gates).astype(BF16)
    grad_plain = contract(cot_ref[...], down_ref[...], 1, 1)
    dgate = jnp.sum(grad_plain * hidden_low.astype(F32), axis=1, keepdims=True)
    width = b_ref.shape[1]
    grad_ref[:, width:] = jnp.broadcast_to(dgate, (dgate.shape[0], grad_ref.shape[1] - width)).astype(BF16)
    grad_hidden = grad_plain * gates
    dhidden_ref[:, :hidden_units] = (
        grad_hidden * up_val * sigmoid * (1.0 + gate_val * (1.0 - sigmoid))
    ).astype(BF16)
    dhidden_ref[:, hidden_units:] = (grad_hidden * silu).astype(BF16)
    out_ref[...] = contract(hidden_low, down_ref[...], 1, 0).astype(BF16)
    grad_ref[:, :width] = contract(dhidden_ref[...], gate_up_ref[...], 1, 0).astype(BF16)


def mlp_experts(place, b_rows, cot_rows, other_rows, router, gate_up, down, blocks, unit, units, outs):
    total, width = b_rows.shape
    hidden_units = down.shape[0]
    block = total // blocks
    by_row = lambda cols: pl.BlockSpec((block, cols), lambda i, place: (i, 0))
    fixed = lambda shape: pl.BlockSpec(shape, lambda i, place: (0, 0), pipeline_mode=pl.Buffered(1))
    return pl.pallas_call(
        mlp_kernel,
        grid_spec=pltpu.PrefetchScalarGridSpec(
            num_scalar_prefetch=1,
            grid=(blocks,),
            in_specs=[
                by_row(width),
                by_row(width),
                by_row(1),
                fixed(router.shape),
                fixed(gate_up.shape),
                fixed(down.shape),
            ]
            + [pl.BlockSpec(memory_space=pl.ANY)] * len(outs),
            out_specs=[
                pl.BlockSpec((block, width), lambda i, place: (i, unit)),
                by_row(width + 128),
                by_row(hidden_units),
                by_row(2 * hidden_units),
            ],
        ),
        out_shape=[
            jax.ShapeDtypeStruct((total, units * width), BF16),
            jax.ShapeDtypeStruct((total, width + 128), BF16),
            jax.ShapeDtypeStruct((total, hidden_units), BF16),
            jax.ShapeDtypeStruct((total, 2 * hidden_units), BF16),
        ],
        compiler_params=pltpu.CompilerParams(vmem_limit_bytes=56 * 2**20),
        cost_estimate=pl.CostEstimate(
            flops=total * width * hidden_units * 12,
            bytes_accessed=4 * total * width * 2 + 6 * total * hidden_units + 6 * width * hidden_units,
            transcendentals=total * hidden_units,
        ),
        input_output_aliases={7: 0} if outs else {},
    )(place, b_rows, cot_rows, other_rows, router, gate_up, down, *outs)


def weave_kernel(first_ref, second_ref, out_ref):
    out_ref[0, :, 0, :] = first_ref[...]
    out_ref[0, :, 1, :] = second_ref[...]


def weave_rows(both, units):
    total, width = both.shape
    block = 32
    half = total // 2 // block
    return pl.pallas_call(
        weave_kernel,
        grid=(units // block,),
        in_specs=[
            pl.BlockSpec((block, width), lambda i: (i, 0)),
            pl.BlockSpec((block, width), lambda i: (i + half, 0)),
        ],
        out_specs=pl.BlockSpec((1, block, 2, width), lambda i: (0, i, 0, 0)),
        out_shape=jax.ShapeDtypeStruct((1, units, 2, width), F32),
        cost_estimate=pl.CostEstimate(
            flops=0, bytes_accessed=16 * units * width, transcendentals=0
        ),
    )(both, both)


def norm_kernel(x_ref, gain_ref, out_ref):
    values = x_ref[0].astype(F32)
    inverse = lax.rsqrt(jnp.mean(values * values, axis=1, keepdims=True) + EPSILON)
    out_ref[...] = (values * inverse * gain_ref[...]).astype(BF16)


def norm_sequence(gathered, unit, gain, rows):
    blocks, _, width = gathered.shape
    return pl.pallas_call(
        norm_kernel,
        grid=(blocks,),
        in_specs=[
            pl.BlockSpec((1, rows, width), lambda i: (i, unit, 0)),
            pl.BlockSpec((1, width), lambda i: (0, 0)),
        ],
        out_specs=pl.BlockSpec((rows, width), lambda i: (i, 0)),
        out_shape=jax.ShapeDtypeStruct((blocks * rows, width), BF16),
        cost_estimate=pl.CostEstimate(
            flops=blocks * rows * width * 6, bytes_accessed=blocks * rows * width * 4, transcendentals=0
        ),
    )(gathered, gain[None])


def rope_tables(positions, half_dim):
    frequency = THETA_BASE ** (-jnp.arange(half_dim, dtype=F32) / half_dim)
    angles = positions.astype(F32)[:, None] * frequency[None, :]
    return (jnp.cos(angles), jnp.sin(angles))


def norm_forward(values, gain_row):
    inverse = lax.rsqrt(jnp.mean(values * values, axis=-1, keepdims=True) + EPSILON)
    return (values * inverse * gain_row, inverse)


def norm_backward(values, inverse, gain_row, grad_normed):
    scaled = gain_row * grad_normed
    gain_term = jnp.sum(grad_normed * values * inverse, axis=0)
    grad_values = inverse * scaled - values * inverse**3 * jnp.mean(
        scaled * values, axis=-1, keepdims=True
    )
    return (grad_values, gain_term)


def route_onehot(routes, experts):
    return (routes[..., None] == jnp.arange(experts, dtype=jnp.int32)).astype(F32)


def gate_forward(logits, onehot):
    chosen = jnp.sum(logits[:, None, :] * onehot, axis=-1)
    return jax.nn.softmax(chosen, axis=-1)


def gate_backward(gate_probs, grad_gates, onehot):
    centered = gate_probs * (grad_gates - jnp.sum(gate_probs * grad_gates, axis=-1, keepdims=True))
    return jnp.sum(centered[..., None] * onehot, axis=1)


def slot_columns(routes, experts, capacity):
    flat_routes = routes.reshape(-1)
    onehot = (flat_routes[:, None] == jnp.arange(experts, dtype=jnp.int32)[None, :]).astype(
        jnp.int32
    )
    slot_rank = jnp.sum((jnp.cumsum(onehot, axis=0) - 1) * onehot, axis=1)
    return (flat_routes * capacity + slot_rank).reshape(routes.shape)


def dot_f32(left, right):
    return jnp.dot(left, right, preferred_element_type=F32)


def after(value, *others):
    return lax.optimization_barrier((value,) + others)[0]


def shift_planes(value, amount):
    planes = lax.axis_size("expert")
    return lax.ppermute(value, "expert", [(i, (i + amount) % planes) for i in range(planes)])


def exchange_planes(blocks, direction):
    arrived = [blocks[0]]
    for c in range(1, blocks.shape[0]):
        arrived.append(shift_planes(blocks[c], direction * c))
    return jnp.stack(arrived, axis=0)


def gather_planes(value, me, holds):
    planes = lax.axis_size("expert")
    right, left = value, value
    rights, lefts = [], []
    for d in range(1, planes):
        if d - 1 in holds:
            right, left = after(right, *holds[d - 1]), after(left, *holds[d - 1])
        right = lax.ppermute(right, "expert", [(i, i + 1) for i in range(d - 1, planes - 1)])
        left = lax.ppermute(left, "expert", [(i + 1, i) for i in range(0, planes - d)])
        rights.append(right)
        lefts.append(left)
    gathered = [value]
    for c in range(1, planes):
        gathered.append(jnp.where(me + c < planes, lefts[c - 1], rights[planes - c - 1]))
    return gathered


def reduce_planes(parts):
    planes = len(parts)
    right, left = None, None
    arrivals = []
    for t in range(1, planes):
        send_right, send_left = parts[planes - t], parts[t]
        if right is not None:
            send_right = (send_right.astype(F32) + right.astype(F32)).astype(BF16)
            send_left = (send_left.astype(F32) + left.astype(F32)).astype(BF16)
        right = lax.ppermute(send_right, "expert", [(i, i + 1) for i in range(0, t)])
        left = lax.ppermute(
            send_left, "expert", [(i, i - 1) for i in range(planes - t, planes)]
        )
        arrivals.append((right, left))
    return parts[0].astype(F32) + right.astype(F32) + left.astype(F32), arrivals


def swap_dp(value, mask):
    size = lax.axis_size("dp")
    return lax.ppermute(value, "dp", [(i, i ^ mask) for i in range(size)])


def all_sum(value, axis):
    size = lax.axis_size(axis)
    mask = 1
    while mask < size:
        value = value + lax.ppermute(value, axis, [(i, i ^ mask) for i in range(size)])
        mask *= 2
    return value


def reduce_rows(left, matmul, me, holds=()):
    size = lax.axis_size("dp")
    blocks = left.reshape(size // 2, 2, left.shape[0] // size, left.shape[1])
    core, chip = me % 2, me // 2

    def half(index):
        rows = lax.dynamic_index_in_dim(blocks, index, axis=1, keepdims=False)
        return matmul(rows.reshape(-1, left.shape[1])).reshape(size // 2, blocks.shape[2], -1)

    arrived = swap_dp(half(1 - core).astype(BF16), 1)
    mine = half(core) + arrived.astype(F32)
    low = mine.astype(BF16)
    total = lax.dynamic_index_in_dim(low, chip, axis=0, keepdims=False)
    total = after(total, *holds).astype(F32)
    for other in range(1, size // 2):
        send = lax.dynamic_index_in_dim(low, chip ^ other, axis=0, keepdims=False)
        total = total + swap_dp(send, 2 * other).astype(F32)
    return total, low


def from_plane_order(relative, plane):
    planes = relative.shape[0]
    return lax.dynamic_slice_in_dim(
        jnp.concatenate([relative, relative], axis=0), (planes - plane) % planes, planes, axis=0
    )


def per_device(
    tokens,
    segment_ids,
    attn_routes,
    mlp_routes,
    cotangent,
    attn_gain,
    kv_weights,
    attn_router,
    query_maps,
    output_maps,
    mlp_gain,
    mlp_router,
    gate_up,
    down_maps,
):
    micro_count, seq_count, local_len, width = tokens.shape
    units = micro_count * seq_count
    length = segment_ids.shape[2]
    experts = attn_router.shape[1]
    dp = lax.axis_size("dp")
    planes = lax.axis_size("expert")
    capacity = 2 * local_len // experts
    slots = experts * capacity
    head_cols = width // dp
    heads = head_cols // HEAD_WIDTH
    plane = lax.axis_index("expert")
    my_dp = lax.axis_index("dp")

    tokens = tokens.reshape(units, local_len, width)
    cotangent = cotangent.reshape(units, local_len, width)
    segments = segment_ids.reshape(units, length)
    attn_routes = attn_routes.reshape(units, local_len, 2)
    mlp_routes = mlp_routes.reshape(units, local_len, 2)

    slot_ids = jnp.arange(slots, dtype=jnp.int32)
    hits_list, tables, other_list = [], [], []
    for u in range(units):
        columns = slot_columns((mlp_routes[u] - plane) % experts, experts, capacity)
        hits = (columns[None] == slot_ids[:, None, None]).astype(F32)
        hits_list.append(hits)
        tables.append(jnp.sum(hits, axis=2).astype(BF16))
        other_list.append(jnp.sum(hits * mlp_routes[u][None, :, ::-1].astype(F32), axis=(1, 2)))

    def send_slots(slot_rows):
        moved = exchange_planes(slot_rows.reshape(planes, capacity, width), 1)
        return moved.reshape(slots, width)

    def gather_rows(moved):
        return lax.all_gather(moved, "dp", axis=0, tiled=True)

    def to_home(rows):
        return exchange_planes(rows.reshape(planes, capacity, -1), -1).reshape(slots, -1)

    kv_rows = kv_weights.shape[0]
    query_rows = query_maps.shape[1]
    packed = jnp.concatenate(
        [query_maps[0], kv_weights.transpose(1, 0, 2).reshape(2 * kv_rows, width)], axis=0
    )
    params = jnp.concatenate([attn_gain, mlp_gain, attn_router.reshape(-1), mlp_router.reshape(-1)])
    sizes = [units * local_len * 2, units * slots, params.shape[0]]
    info = jnp.concatenate(
        [attn_routes.astype(BF16).reshape(-1)] + [o.astype(BF16) for o in other_list] + [params]
    )
    info = jnp.pad(info, (0, -info.shape[0] % (16 * head_cols))).reshape(1, -1, head_cols)
    packed = packed.reshape(-1, dp, head_cols).transpose(1, 0, 2)
    weight_rows = packed.shape[1]
    packed = jnp.concatenate([packed, jnp.broadcast_to(info, (dp,) + info.shape[1:])], axis=1)
    packed = lax.all_to_all(packed, "dp", split_axis=0, concat_axis=0, tiled=True)
    info = packed[:, weight_rows:].reshape(dp, -1)
    cot_moved = [send_slots(dot_f32(tables[u], cotangent[u]).astype(BF16)) for u in range(units)]
    cot_rows_list = [gather_rows(part) for part in cot_moved]

    x_all = lax.all_gather(tokens.reshape(units * local_len, width), "dp", axis=0)

    routes_info = info[:, : sizes[0]].reshape(dp, units, local_len, 2).transpose(1, 0, 2, 3)
    routes_info = routes_info.reshape(units, length, 2).astype(jnp.int32)
    others = info[:, sizes[0] : sizes[0] + sizes[1]].reshape(dp, units, experts, capacity)
    others = exchange_planes(others.transpose(2, 1, 0, 3), 1)
    other_rows = others.transpose(1, 2, 0, 3).reshape(units, dp * slots).astype(jnp.int32)
    params = info[:, sizes[0] + sizes[1] : sum(sizes)]
    params = [params] + [shift_planes(params, -c) for c in range(1, planes)]
    params = from_plane_order(jnp.stack(params, axis=0), plane)

    def param(start, each):
        part = params[:, :, start : start + kv_rows * each]
        return part.reshape(planes, dp, kv_rows, each).transpose(1, 0, 2, 3).reshape(width, each)

    gain_one = param(0, 1).reshape(-1).astype(F32)
    gain_two = param(kv_rows, 1).reshape(-1).astype(F32)
    router_one_low = param(2 * kv_rows, experts)
    router_two_low = param((2 + experts) * kv_rows, experts)
    router_one = router_one_low.astype(F32)
    router_two = router_two_low.astype(F32)
    router_wide = jnp.pad(router_two_low, ((0, 0), (0, 128 - experts)))

    hidden_units = down_maps.shape[1]
    place = plane.astype(jnp.int32)[None]

    cosine, sine_table = rope_tables(jnp.arange(length, dtype=jnp.int32), HEAD_WIDTH // 2)
    cosine = jnp.concatenate([cosine, cosine], axis=1)
    sine_table = jnp.concatenate([-sine_table, sine_table], axis=1)

    mixed_parts = []
    input_parts = []
    gain_one_sum = jnp.zeros((width,), F32)
    gain_two_sum = jnp.zeros((width,), F32)
    each = range(units)

    inputs, a_home, inverse_one, a_all, routes_here, gates_all, kept, gated, states = (
        [], [], [], [], [], [], [], [], []
    )
    for u in each:
        inputs.append(tokens[u].astype(F32))
        normed, inverse = norm_forward(inputs[u], gain_one)
        a_home.append(normed.astype(BF16))
        inverse_one.append(inverse)
        a_all.append(norm_sequence(x_all, u, gain_one, local_len))
        gates_all.append(
            gate_forward(dot_f32(a_all[u], router_one_low), route_onehot(routes_info[u], experts))
        )

    packed = gather_planes(packed, plane, {1: tuple(cot_moved + a_all), 2: tuple(gates_all)})
    query_cols = [p[:, :query_rows].reshape(width, head_cols) for p in packed]
    kv_cols = from_plane_order(jnp.stack([p[:, query_rows:weight_rows] for p in packed], axis=0), plane)
    kv_cols = kv_cols.transpose(1, 0, 2, 3)
    key_cols = kv_cols[:, :, :kv_rows].reshape(width, head_cols)
    value_cols = kv_cols[:, :, kv_rows:].reshape(width, head_cols)
    for u in each:
        routes_here.append((routes_info[u] - plane) % experts)
        a_now = after(a_all[u], *gated)
        raws = [dot_f32(a_now, cols).astype(BF16) for cols in query_cols]
        keys = dot_f32(a_now, key_cols)
        values = dot_f32(a_now, value_cols).astype(BF16)
        *saved, context_gated = attn_forward(
            routes_here[u], gates_all[u], segments[u], cosine, sine_table, raws, keys, values
        )
        kept.append(saved)
        gated.append(context_gated)
    output_list = after(output_maps[0], packed[1], packed[-1])
    output_list = gather_planes(output_list, plane, {1: (gated[0], cot_rows_list[0]), 2: (gated[-1], cot_rows_list[-1])})
    output_rows = jnp.concatenate(output_list, axis=0)
    padding = ((0, -hidden_units % 128), (0, 0))
    gate_up_now = after(gate_up, gated[-1])
    gate_up_local = jnp.concatenate(
        [jnp.pad(gate_up_now[0, :, 0], padding), jnp.pad(gate_up_now[0, :, 1], padding)], axis=0
    )
    down_local = jnp.pad(after(down_maps, gated[-1])[0], padding)

    b_home, inverse_two, onehot_mlp, gates_mlp, moved, sent = [], [], [], [], [], []
    for u in each:
        gated_now = after(gated[u], *sent)
        attn_sum, low = reduce_rows(
            gated_now, lambda rows: dot_f32(rows, output_rows), my_dp, moved[-1:] + [gate_up_local, down_local] if moved else []
        )
        sent.append(low)
        states.append(inputs[u] + attn_sum)
        normed, inverse = norm_forward(states[u], gain_two)
        b_home.append(normed.astype(BF16))
        inverse_two.append(inverse)
        onehot_mlp.append(route_onehot(mlp_routes[u], experts))
        gates_mlp.append(gate_forward(dot_f32(b_home[u], router_two_low), onehot_mlp[u]))
        moved.append(send_slots(dot_f32(tables[u], b_home[u]).astype(BF16)))

    b_rows_list, hid_list, dhid_list, grad_b_rows, outs = [], [], [], [], []
    for u in each:
        b_rows_list.append(gather_rows(moved[u]))
        b_rows = b_rows_list[u]
        b_rows = after(b_rows, *moved[1:], *hid_list)
        outs, grad_part, hidden, dhidden = mlp_experts(
            place,
            b_rows,
            cot_rows_list[u],
            other_rows[u][:, None],
            router_wide,
            gate_up_local,
            down_local,
            dp,
            u,
            units,
            outs,
        )
        outs = [outs]
        hid_list.append(hidden)
        dhid_list.append(dhidden)
        grad_b_rows.append(lax.psum_scatter(grad_part, "dp", scatter_dimension=0, tiled=True))

    dlm_list, grad_states, dh_list = [], [], []
    down_grad, both_grad, last = 0.0, 0.0, hid_list[-1]
    for u in each:
        down_grad = down_grad + jnp.einsum(
            "rf,rd->fd",
            after(hid_list[u], last),
            cot_rows_list[u],
            preferred_element_type=F32,
        )
        both_grad = both_grad + jnp.einsum(
            "rf,rd->fd", after(dhid_list[u], down_grad), b_rows_list[u], preferred_element_type=F32
        )
        grad_b_slots = after(to_home(after(grad_b_rows[u], *grad_states)), both_grad, *dh_list)
        hits = hits_list[u]
        cot = cotangent[u]
        dgm_slots = grad_b_slots[:, width].astype(F32)
        grad_b_slots = grad_b_slots[:, :width]
        dlm = gate_backward(
            gates_mlp[u], jnp.sum(hits * dgm_slots[:, None, None], axis=0), onehot_mlp[u]
        )
        dlm_list.append(dlm)
        grad_b = jnp.einsum(
            "st,sd->td", tables[u], grad_b_slots, preferred_element_type=F32
        ) + jnp.einsum("re,de->rd", dlm, router_two, precision=PRECISION_TOP)
        grad_state, gain_two_term = norm_backward(states[u], inverse_two[u], gain_two, grad_b)
        gain_two_sum = gain_two_sum + gain_two_term
        grad_states.append(cot.astype(F32) + grad_state)
        last = grad_states[u]
        dh_list.append(lax.all_gather(grad_states[u].astype(BF16), "dp", axis=0, tiled=True))

    qkv_cols = jnp.concatenate(
        [after(cols, *moved) for cols in query_cols + [key_cols, value_cols]], axis=1
    )
    qkv_cols = jnp.concatenate(
        [
            jnp.pad(qkv_cols, ((0, 0), (0, 128))),
            jnp.pad(jnp.eye(128, dtype=BF16), ((0, 0), (qkv_cols.shape[1], 0))),
        ],
        axis=0,
    )
    g_list, output_part = [], 0.0
    for u in each:
        dh_now = after(dh_list[u], *(g_list[-1:] or grad_states[-1:]))
        grad_context = jnp.einsum("td,cd->tc", dh_now, output_rows, preferred_element_type=F32)
        if u == units - 1:
            for v in each:
                output_part = output_part + jnp.einsum(
                    "tc,td->cd", gated[v], after(dh_list[v], dh_now), preferred_element_type=F32
                )
            output_part = output_part.astype(BF16)
            grad_context = after(grad_context, output_part)
        g_list.append(
            attn_backward(
                routes_here[u],
                gates_all[u],
                segments[u],
                cosine,
                sine_table,
                *kept[u],
                grad_context,
            )
        )

    out_rows = lax.psum_scatter(after(outs[0], g_list[0]), "dp", scatter_dimension=0, tiled=True)

    dla_list = []

    def cols_grad(c, hold):
        total = 0.0
        for u in each:
            piece = lax.dynamic_slice_in_dim(
                after(g_list[u], hold), c * head_cols, head_cols, axis=1
            )
            total = total + jnp.einsum("td,tc->dc", a_all[u], piece, preferred_element_type=F32)
        return total.astype(BF16)

    def finish_inputs(u, hold):
        nonlocal gain_one_sum
        grad_a, low = reduce_rows(
            after(g_list[u], hold),
            lambda rows: jnp.einsum("tc,dc->td", rows, qkv_cols, preferred_element_type=F32),
            my_dp,
        )
        dga = grad_a[:, width : width + 2]
        grad_a = grad_a[:, :width]
        gates_home = lax.dynamic_slice_in_dim(gates_all[u], my_dp * local_len, local_len, axis=0)
        dla = gate_backward(gates_home, dga, route_onehot(attn_routes[u], experts))
        dla_list.append(dla)
        grad_a = grad_a + jnp.einsum("re,de->rd", dla, router_one, precision=PRECISION_TOP)
        grad_inputs, gain_one_term = norm_backward(inputs[u], inverse_one[u], gain_one, grad_a)
        gain_one_sum = gain_one_sum + gain_one_term
        input_parts.append(grad_states[u] + grad_inputs)
        return low

    output_grad, arrivals = reduce_planes(
        [output_part[c * head_cols : (c + 1) * head_cols] for c in range(planes)]
    )
    done = after(g_list[-1], *arrivals[0])
    query_parts = []
    for e in range(planes):
        done = cols_grad((e - plane) % planes, done)
        query_parts.append(done.reshape(dp, query_rows, head_cols))
    kv_part = []
    for i in range(2):
        done = cols_grad(experts + i, done)
        kv_part.append(done.reshape(dp, planes, kv_rows, head_cols))
    packed_grad = jnp.concatenate(
        [jnp.stack(query_parts, axis=0)] + [part.transpose(1, 0, 2, 3) for part in kv_part], axis=2
    )
    packed_grad = after(packed_grad, out_rows, output_grad)
    packed_grad = lax.psum_scatter(packed_grad, "expert", scatter_dimension=0, tiled=False)

    for u in each:
        out_slots = to_home(out_rows[:, u * width : (u + 1) * width])
        gated_table = jnp.sum(hits_list[u] * gates_mlp[u][None], axis=2).T
        gated_high = gated_table.astype(BF16)
        gated_low = (gated_table - gated_high.astype(F32)).astype(BF16)
        mlp_sum = dot_f32(gated_high, out_slots) + dot_f32(gated_low, out_slots)
        mixed_parts.append((states[u] + mlp_sum).astype(BF16))

    for u in each:
        done = after(done, *mixed_parts[: u])
        done = finish_inputs(u, done)
    both_grad = after(both_grad, done)
    gate_up_grad = weave_rows(both_grad, hidden_units)
    down_grad = after(down_grad, done)[:hidden_units]

    packed_grad = lax.all_to_all(packed_grad, "dp", split_axis=0, concat_axis=0, tiled=True)
    packed_grad = packed_grad.transpose(1, 0, 2).reshape(-1, width).astype(F32)
    query_grad = packed_grad[:query_rows]
    kv_grad = packed_grad[query_rows:].reshape(2, kv_rows, width).transpose(1, 0, 2)

    router_one_grad = jnp.einsum(
        "re,rd->ed",
        jnp.concatenate(dla_list, axis=0),
        jnp.concatenate(a_home, axis=0).astype(F32),
        precision=PRECISION_TOP,
    )
    router_two_grad = jnp.einsum(
        "re,rd->ed",
        jnp.concatenate(dlm_list, axis=0),
        jnp.concatenate(b_home, axis=0).astype(F32),
        precision=PRECISION_TOP,
    )
    small_grad = jnp.concatenate(
        [gain_one_sum[None], gain_two_sum[None], router_one_grad, router_two_grad], axis=0
    )
    small_grad = all_sum(all_sum(small_grad, "dp"), "expert")
    small_grad = lax.dynamic_index_in_dim(
        small_grad.reshape(-1, dp * planes, kv_rows), my_dp * planes + plane, axis=1, keepdims=False
    )

    shape = (micro_count, seq_count, local_len, width)
    return (
        jnp.stack(mixed_parts, axis=0).reshape(shape),
        jnp.stack(input_parts, axis=0).reshape(shape),
        small_grad[0],
        kv_grad,
        small_grad[2 : 2 + experts].T,
        query_grad[None],
        output_grad[None],
        small_grad[1],
        small_grad[2 + experts :].T,
        gate_up_grad,
        down_grad[None],
    )


def solution(mesh):
    in_specs = (
        P(None, "expert", "dp", None),
        P(None, "expert", None),
        P(None, "expert", "dp", None),
        P(None, "expert", "dp", None),
        P(None, "expert", "dp", None),
        P(("dp", "expert")),
        P(("dp", "expert"), None, None),
        P(("dp", "expert"), None),
        P("expert", "dp", None),
        P("expert", "dp", None),
        P(("dp", "expert")),
        P(("dp", "expert"), None),
        P("expert", "dp", None, None),
        P("expert", "dp", None),
    )
    out_specs = (
        P(None, "expert", "dp", None),
        P(None, "expert", "dp", None),
        P(("dp", "expert")),
        P(("dp", "expert"), None, None),
        P(("dp", "expert"), None),
        P("expert", "dp", None),
        P("expert", "dp", None),
        P(("dp", "expert")),
        P(("dp", "expert"), None),
        P("expert", "dp", None, None),
        P("expert", "dp", None),
    )
    return jax.shard_map(
        per_device, mesh=mesh, in_specs=in_specs, out_specs=out_specs, check_vma=False
    )
```
